32 devices in a mesh: freq: 2 (over x), azim: 16 (over z, y, core).
Axes of the slice: x: 2, y: 2, z: 4, core: 2. Of those that a mesh axis runs over, the one named last changes fastest.
Arguments:
- coupling: bfloat16 [16, 10, 2, 384, 384], P('azim', 'freq'), parts along dimension 1
- band: int32 [10], P('freq'), parts along dimension 0, may hold values from 1 to 8, as said below
- precond: float32 [16, 4, 384, 384], P('azim', 'freq'), parts along dimension 1
- basis: float32 [8, 16, 32, 2, 384], P('freq', 'azim'), parts along dimension 0
- mask: int32 [16, 32], P('azim'), may hold values 0 or 1
Outputs:
- new_vector: float32 [16, 64, 2, 384], P('azim', 'freq'), parts along dimension 1
- hessenberg_column: float32 [4, 5], P('freq'), parts along dimension 0
The draws below stay inside these ranges and needn't reach their ends.
There are 2 independent parts, one for each index of `freq`. The reference program is written for one: setup_inputs(seed, part) draws one part's arguments, and reference() takes and returns one part's arrays. A program takes and returns all parts, laid end to end along the dimension named above; an argument that names none is the same for every part. Nothing has to cross between parts.
Inputs may be any that keep to these rules, and one draw needn't show every extreme that they name: `band`: the entry for cycle offset zero (index 2) equals 8, so that offset couples all columns.
All inputs are finite; a program needn't handle non-finite values. No bound on the sum of `mask` on one device may be relied on, other than what follows from the above.
Results may differ from the reference program's by a relative error of at most 0.00045.
Values may be sent and summed in bfloat16 or wider, within the bound.
A program may use at most 128 MiB of HBM per device.

```python
import jax
import jax.numpy as jnp
from jax import lax

B = 384
CYCLES = 32
RW = 2
ARNOLDI = 4
NDR = 5
NAZ = 16


def draw_coupling(key, part):
    shape = (NAZ, NDR, 2, B, B)
    sigma = 0.7 / (NAZ * NDR * 2 * B) ** 0.5
    values = jax.random.normal(jax.random.fold_in(key, 11), shape, jnp.float32)
    gains = jnp.exp(jax.random.uniform(jax.random.fold_in(key, 12), (NAZ, NDR, 1, 1, 1), jnp.float32, -0.7, 0.7))
    basis_steps = jnp.arange(B)
    identity = (basis_steps[:, None] == basis_steps[None, :]).astype(jnp.float32)
    anchor = ((jnp.arange(NAZ) == 0)[:, None] & (jnp.arange(NDR) == RW)[None, :]).astype(jnp.float32)
    real_mark = (jnp.arange(2) == 0).astype(jnp.float32)
    self_part = anchor[:, :, None, None, None] * real_mark[None, None, :, None, None] * identity[None, None, None]
    return (values * gains * sigma + self_part).astype(jnp.bfloat16)


def draw_band(key, part):
    raw_band = jax.random.randint(jax.random.fold_in(key, 21), (NDR,), 1, NAZ // 2 + 1)
    return jnp.where(jnp.arange(NDR) == RW, NAZ // 2, raw_band).astype(jnp.int32)


def draw_precond(key, part):
    shape = (NAZ, 2, B, B)
    values = jax.random.normal(jax.random.fold_in(key, 31), shape, jnp.float32)
    basis_steps = jnp.arange(B)
    identity = (basis_steps[:, None] == basis_steps[None, :]).astype(jnp.float32)
    real_mark = (jnp.arange(2) == 0).astype(jnp.float32)
    return values * (0.4 / (2 * B) ** 0.5) + real_mark[None, :, None, None] * identity[None, None]


def draw_basis(key, part):
    shape = (ARNOLDI, NAZ, CYCLES, 2, B)
    position = jnp.arange(NAZ).astype(jnp.float32) / (NAZ - 1)
    common = jax.random.normal(jax.random.fold_in(key, 41), shape[1:], jnp.float32)
    own = jax.random.normal(jax.random.fold_in(key, 42), shape, jnp.float32)
    rise = 3.0 ** (0.5 * position)
    mixed = 0.8 * common[None] + 0.6 * own
    spread = jnp.exp(jax.random.uniform(jax.random.fold_in(key, 43), (1, NAZ, CYCLES, 1, 1), jnp.float32, 0.0, 1.1631508))
    return mixed * spread * rise[None, :, None, None, None]


def touch_ends(entries, stream_key, least, top_value):
    longest = entries.shape.index(max(entries.shape))
    spots = []
    for shift in (0, 1):
        where = [jax.random.randint(jax.random.fold_in(stream_key, axis), (), 0, length) for axis, length in enumerate(entries.shape)]
        where[longest] = (where[longest] + shift) % entries.shape[longest]
        spots.append(tuple(where))
    return entries.at[spots[0]].set(least).at[spots[1]].set(top_value)


def setup_inputs(seed: int = 0, part: int = 0) -> dict:
    key_of = jax.random.split(jax.random.key(seed), 6)
    part_splits = jax.random.split(jax.random.fold_in(key_of[5], part), 6)
    coupling = draw_coupling(jax.random.fold_in(jax.random.fold_in(key_of[5], part), 71), part)
    band = draw_band(jax.random.fold_in(jax.random.fold_in(key_of[5], part), 71), part)
    precond = draw_precond(jax.random.fold_in(jax.random.fold_in(key_of[5], part), 71), part)
    basis = draw_basis(jax.random.fold_in(jax.random.fold_in(key_of[5], part), 71), part)
    mask = touch_ends((jax.random.randint(key_of[4], (NAZ, CYCLES), 0, 8) < 7).astype(jnp.int32), jax.random.fold_in(key_of[4], 1), 0, 1)
    return {"coupling": coupling, "band": band, "precond": precond, "basis": basis, "mask": mask}


def fourier_tables(azimuths):
    azimuth_steps = jnp.arange(azimuths, dtype=jnp.int32)
    phase_index = azimuth_steps[:, None] * azimuth_steps[None, :] % azimuths
    angles = phase_index.astype(jnp.float32) * (2.0 * jnp.pi / azimuths)
    return (jnp.cos(angles), jnp.sin(angles))

def transform(real_part, imag_part, cosine_table, sine_table, inverse):
    highest_accuracy = lax.Precision.HIGHEST
    cos_real = jnp.tensordot(cosine_table, real_part, axes=1, precision=highest_accuracy)
    cos_imag = jnp.tensordot(cosine_table, imag_part, axes=1, precision=highest_accuracy)
    sin_real = jnp.tensordot(sine_table, real_part, axes=1, precision=highest_accuracy)
    sin_imag = jnp.tensordot(sine_table, imag_part, axes=1, precision=highest_accuracy)
    if inverse:
        scaling = 1.0 / cosine_table.shape[0]
        return ((cos_real - sin_imag) * scaling, (cos_imag + sin_real) * scaling)
    return (cos_real + sin_imag, cos_imag - sin_real)

def block_matrix(matrix):
    real_part = matrix[..., 0, :, :]
    imag_part = matrix[..., 1, :, :]
    upper = jnp.concatenate([real_part, imag_part], axis=-1)
    lower = jnp.concatenate([-imag_part, real_part], axis=-1)
    return jnp.concatenate([upper, lower], axis=-2)

def cycle_coupling(column_rows, blocks, matmul_accuracy):
    row_total, cycle_count, parts, basis_width = column_rows.shape
    cycle_reach = blocks.shape[0] // 2
    flattened = column_rows.reshape(row_total, cycle_count, parts * basis_width)
    padded = jnp.pad(flattened, ((0, 0), (cycle_reach, cycle_reach), (0, 0)))
    summed = jnp.zeros((row_total * cycle_count, parts * basis_width), jnp.float32)
    for offset in range(blocks.shape[0]):
        shifted = padded[:, 2 * cycle_reach - offset:2 * cycle_reach - offset + cycle_count]
        summed = summed + jnp.dot(shifted.reshape(row_total * cycle_count, parts * basis_width), blocks[offset], preferred_element_type=jnp.float32, precision=matmul_accuracy)
    return summed.reshape(row_total, cycle_count, parts, basis_width)

def reference(coupling, band, precond, basis, mask):
    highest_accuracy = lax.Precision.HIGHEST
    azimuths = NAZ
    cosine_table, sine_table = fourier_tables(azimuths)
    current = basis[ARNOLDI - 1]
    active = mask.astype(jnp.float32)[:, :, None, None]
    driving = (active * current).astype(jnp.bfloat16)
    azimuth_steps = jnp.arange(azimuths, dtype=jnp.int32)
    distance = jnp.minimum(azimuth_steps, azimuths - azimuth_steps)
    inside = (distance[:, None] <= band[None, :]).astype(jnp.bfloat16)
    kernel = (coupling * inside[:, :, None, None, None]).astype(jnp.float32)
    kernel_real, kernel_imag = transform(kernel[:, :, 0], kernel[:, :, 1], cosine_table, sine_table, False)
    spectrum_kernel = jnp.stack([kernel_real, kernel_imag], axis=2)
    driving_wide = driving.astype(jnp.float32)
    drive_real, drive_imag = transform(driving_wide[:, :, 0], driving_wide[:, :, 1], cosine_table, sine_table, False)
    drive_modes = jnp.stack([drive_real, drive_imag], axis=2)

    def per_mode(mode_pair):
        return cycle_coupling(mode_pair[1][None], block_matrix(mode_pair[0]), highest_accuracy)[0]
    response = lax.map(per_mode, (spectrum_kernel, drive_modes))
    applied_real, applied_imag = transform(response[:, :, 0], response[:, :, 1], cosine_table, sine_table, True)
    applied = jnp.stack([applied_real, applied_imag], axis=2)
    driven = active * applied + (1.0 - active) * current
    fourier_spectrum_real, fourier_spectrum_imaginary = transform(driven[:, :, 0], driven[:, :, 1], cosine_table, sine_table, False)
    conditioner_real = precond[:, 0]
    conditioner_imaginary = precond[:, 1]
    solution_real = jnp.einsum('qhn,qnw->qhw', fourier_spectrum_real, conditioner_real, precision=highest_accuracy) - jnp.einsum('qhn,qnw->qhw', fourier_spectrum_imaginary, conditioner_imaginary, precision=highest_accuracy)
    solution_imaginary = jnp.einsum('qhn,qnw->qhw', fourier_spectrum_real, conditioner_imaginary, precision=highest_accuracy) + jnp.einsum('qhn,qnw->qhw', fourier_spectrum_imaginary, conditioner_real, precision=highest_accuracy)
    result_real, result_imag = transform(solution_real, solution_imaginary, cosine_table, sine_table, True)
    elements = float(NAZ * CYCLES * B)
    basis_real = basis[:, :, :, 0]
    basis_imag = basis[:, :, :, 1]
    project_real = lax.optimization_barrier(jnp.sum(basis_real * result_real[None] + basis_imag * result_imag[None], axis=(1, 2, 3))) / elements
    project_imag = lax.optimization_barrier(jnp.sum(basis_real * result_imag[None] - basis_imag * result_real[None], axis=(1, 2, 3))) / elements
    coef_real = project_real[:, None, None, None]
    coef_imag = project_imag[:, None, None, None]
    remainder_real = result_real - lax.optimization_barrier(jnp.sum(coef_real * basis_real - coef_imag * basis_imag, axis=0))
    remainder_imag = result_imag - lax.optimization_barrier(jnp.sum(coef_real * basis_imag + coef_imag * basis_real, axis=0))
    norm_square = jnp.sum(remainder_real * remainder_real + remainder_imag * remainder_imag) / elements
    scale_norm = jnp.sqrt(norm_square + 1e-06)
    new_vector = jnp.stack([remainder_real, remainder_imag], axis=2) / scale_norm
    hessenberg_column = jnp.stack([jnp.concatenate([project_real, scale_norm[None]]), jnp.concatenate([project_imag, jnp.zeros((1,), jnp.float32)])])
    return (new_vector, hessenberg_column)
```

```python
import functools

import jax
import jax.numpy as jnp
import numpy as np
from jax import lax
from jax.experimental import pallas as pl
from jax.experimental.pallas import tpu as pltpu
from jax.sharding import PartitionSpec as P


def fourier_tables(azimuths):
    azimuth_steps = jnp.arange(azimuths, dtype=jnp.int32)
    phase_index = azimuth_steps[:, None] * azimuth_steps[None, :] % azimuths
    angles = phase_index.astype(jnp.float32) * (2.0 * jnp.pi / azimuths)
    return (jnp.cos(angles), jnp.sin(angles))


def transform(real_part, imag_part, cosine_table, sine_table, inverse):
    highest_accuracy = lax.Precision.HIGHEST
    cos_real = jnp.tensordot(cosine_table, real_part, axes=1, precision=highest_accuracy)
    cos_imag = jnp.tensordot(cosine_table, imag_part, axes=1, precision=highest_accuracy)
    sin_real = jnp.tensordot(sine_table, real_part, axes=1, precision=highest_accuracy)
    sin_imag = jnp.tensordot(sine_table, imag_part, axes=1, precision=highest_accuracy)
    if inverse:
        scaling = 1.0 / cosine_table.shape[0]
        return ((cos_real - sin_imag) * scaling, (cos_imag + sin_real) * scaling)
    return (cos_real + sin_imag, cos_imag - sin_real)


def block_matrix(matrix):
    real_part = matrix[..., 0, :, :]
    imag_part = matrix[..., 1, :, :]
    upper = jnp.concatenate([real_part, imag_part], axis=-1)
    lower = jnp.concatenate([-imag_part, real_part], axis=-1)
    return jnp.concatenate([upper, lower], axis=-2)


def cycle_coupling(column_rows, blocks):
    row_total, cycle_count, parts, basis_width = column_rows.shape
    cycle_reach = blocks.shape[0] // 2
    flattened = column_rows.reshape(row_total, cycle_count, parts * basis_width)
    padded = jnp.pad(flattened, ((0, 0), (cycle_reach, cycle_reach), (0, 0)))
    summed = jnp.zeros((row_total * cycle_count, parts * basis_width), jnp.float32)
    for offset in range(blocks.shape[0]):
        shifted = padded[:, 2 * cycle_reach - offset : 2 * cycle_reach - offset + cycle_count]
        summed = summed + jnp.dot(
            shifted.reshape(row_total * cycle_count, parts * basis_width),
            blocks[offset],
            preferred_element_type=jnp.float32,
            precision=None,
        )
    return summed.reshape(row_total, cycle_count, parts, basis_width)


def relayout(field, cosine_table, sine_table, send_out, send_back, inverse):
    azimuths = cosine_table.shape[0]
    cycle_count = field.shape[1]
    basis_width = field.shape[3]
    piece_width = cycle_count * basis_width // azimuths
    split_parts = jnp.transpose(field[0], (1, 0, 2)).reshape(2, azimuths, piece_width)
    pieces = jnp.transpose(split_parts, (1, 0, 2)).reshape(azimuths, 2 * piece_width)
    spread = send_out(pieces).reshape(azimuths, 2, piece_width)
    real_part, imag_part = transform(spread[:, 0], spread[:, 1], cosine_table, sine_table, inverse)
    joined = jnp.stack([real_part, imag_part], axis=1).reshape(azimuths, 2 * piece_width)
    returned = send_back(joined).reshape(azimuths, 2, piece_width)
    whole = jnp.transpose(returned, (1, 0, 2)).reshape(2, cycle_count, basis_width)
    return jnp.transpose(whole, (1, 0, 2))[None]


def plain_body(coupling, band, precond, basis, mask):
    highest_accuracy = lax.Precision.HIGHEST
    azimuths = lax.axis_size("azim")
    position = lax.axis_index("azim")
    cosine_table, sine_table = fourier_tables(azimuths)
    vectors = basis[:, 0]
    arnoldi_count = vectors.shape[0]
    cycle_count = vectors.shape[1]
    basis_width = vectors.shape[3]
    current = vectors[arnoldi_count - 1][None]
    active = mask.astype(jnp.float32)[:, :, None, None]
    driving = (active * current).astype(jnp.bfloat16)
    distance = jnp.minimum(position, azimuths - position)
    inside = (distance <= band).astype(coupling.dtype)
    kernel = coupling[0] * inside[:, None, None, None]
    blocks = block_matrix(kernel)
    gathered = lax.all_gather(driving, "azim", axis=0, tiled=True)
    aligned = jnp.roll(gathered, position, axis=0)
    applied = lax.psum_scatter(
        cycle_coupling(aligned, blocks), "azim", scatter_dimension=0, tiled=True
    )
    driven = active * applied + (1.0 - active) * current
    spectrum = relayout(
        driven,
        cosine_table,
        sine_table,
        lambda tensor: lax.all_to_all(
            tensor.astype(jnp.bfloat16), "azim", split_axis=0, concat_axis=0, tiled=True
        ).astype(tensor.dtype),
        lambda tensor: lax.all_to_all(
            tensor.astype(jnp.bfloat16), "azim", split_axis=0, concat_axis=0, tiled=True
        ).astype(tensor.dtype),
        False,
    )
    precond_blocks = block_matrix(precond[0])
    solved = jnp.dot(
        spectrum.reshape(cycle_count, 2 * basis_width),
        precond_blocks,
        preferred_element_type=jnp.float32,
        precision=highest_accuracy,
    )
    solved = solved.reshape(1, cycle_count, 2, basis_width)
    result = relayout(
        solved,
        cosine_table,
        sine_table,
        lambda tensor: lax.all_to_all(
            tensor.astype(jnp.bfloat16), "azim", split_axis=0, concat_axis=0, tiled=True
        ).astype(tensor.dtype),
        lambda tensor: lax.all_to_all(
            tensor.astype(jnp.bfloat16), "azim", split_axis=0, concat_axis=0, tiled=True
        ).astype(tensor.dtype),
        True,
    )
    elements = float(azimuths * cycle_count * basis_width)
    basis_real = vectors[:, :, 0]
    basis_imag = vectors[:, :, 1]
    result_real = result[0, :, 0]
    result_imag = result[0, :, 1]
    local_real = jnp.sum(
        basis_real * result_real[None] + basis_imag * result_imag[None], axis=(1, 2)
    )
    local_imag = jnp.sum(
        basis_real * result_imag[None] - basis_imag * result_real[None], axis=(1, 2)
    )
    sum_real, sum_imag = lax.psum((local_real, local_imag), "azim")
    project_real = sum_real / elements
    project_imag = sum_imag / elements
    coef_real = project_real[:, None, None]
    coef_imag = project_imag[:, None, None]
    remainder_real = result_real - jnp.sum(coef_real * basis_real - coef_imag * basis_imag, axis=0)
    remainder_imag = result_imag - jnp.sum(coef_real * basis_imag + coef_imag * basis_real, axis=0)
    norm_square = (
        lax.psum(jnp.sum(remainder_real * remainder_real + remainder_imag * remainder_imag), "azim")
        / elements
    )
    scale_norm = jnp.sqrt(norm_square + 1e-06)
    new_vector = (jnp.stack([remainder_real, remainder_imag], axis=1) / scale_norm)[None]
    hessenberg_column = jnp.stack(
        [
            jnp.concatenate([project_real, scale_norm[None]]),
            jnp.concatenate([project_imag, jnp.zeros((1,), jnp.float32)]),
        ]
    )
    return (new_vector, hessenberg_column)


def fourier_constants(azimuths):
    steps = np.arange(azimuths)
    angles = (steps[:, None] * steps[None, :] % azimuths) * (2.0 * np.pi / azimuths)
    return np.concatenate([np.cos(angles), np.sin(angles)], axis=0).astype(np.float32)


GROUP = 2


def shift_of(value):
    return int(value).bit_length() - 1


def step_kernel(
    n,
    cycles,
    reach,
    band_ref,
    mask_any,
    basis_any,
    table_any,
    coupling_ref,
    precond_ref,
    out_ref,
    hess_ref,
    mask_ref,
    raw_basis,
    basis_ref,
    table_ref,
    raw_coupling,
    raw_precond,
    blocks,
    solver,
    columns,
    drive,
    partial,
    core_in,
    side_kept,
    side_out,
    side_in,
    line_out,
    line_in,
    mode_out,
    mode_in,
    back_out,
    back_in,
    field_out,
    field_in,
    basis_out,
    basis_in,
    load_sem,
    send_sem,
    recv_sem,
):
    arnoldi = basis_ref.shape[0]
    width2 = basis_ref.shape[2]
    width = width2 // 2
    offsets = 2 * reach + 1
    per = cycles // n
    piece = per * n
    elements = float(n * cycles * width)
    me = lax.axis_index("azim")

    load_coupling = pltpu.make_async_copy(coupling_ref, raw_coupling, load_sem.at[0])
    load_precond = pltpu.make_async_copy(precond_ref, raw_precond, load_sem.at[1])
    load_mask = pltpu.make_async_copy(mask_any, mask_ref, load_sem.at[2])
    load_basis = pltpu.make_async_copy(basis_any, raw_basis, load_sem.at[3])
    load_table = pltpu.make_async_copy(table_any, table_ref, load_sem.at[4])

    def peer(step):
        return lax.rem(me + step, n)

    barrier = pltpu.get_barrier_semaphore()

    for step in range(1, n):
        pl.semaphore_signal(
            barrier, inc=1, device_id={"azim": peer(step)}, device_id_type=pl.DeviceIdType.MESH
        )

    load_mask.start()
    load_basis.start()
    load_coupling.start()
    load_table.start()
    load_precond.start()

    def remote(phase, source, target, other, slot):
        return pltpu.make_async_remote_copy(
            src_ref=source,
            dst_ref=target,
            send_sem=send_sem.at[phase, other],
            recv_sem=recv_sem.at[phase, slot],
            device_id={"azim": other},
            device_id_type=pl.DeviceIdType.MESH,
        )

    def send_all(phase, sources, targets):
        for step in range(1, n):
            other = peer(step)
            remote(phase, sources(other), targets.at[me], other, me).start()

    def wait_arrivals(phase, targets):
        for step in range(1, n):
            other = peer(step)
            remote(phase, targets.at[other], targets.at[other], other, other).wait_recv()

    def wait_sends(phase, sources, targets):
        for step in range(1, n):
            other = peer(step)
            remote(phase, sources(other), targets.at[me], other, me).wait_send()

    def to_lanes(value):
        return jnp.concatenate([value[i * n : (i + 1) * n] for i in range(per)], axis=1)

    core = me & 1
    side = (me >> 1) & 1
    line = me >> 2
    lines = n // 4
    core_peer = me ^ 1
    side_peer = me ^ 2

    def line_peer(step):
        return lax.rem(line + step, lines)

    def order_basis(j):
        for i in range(per):
            for part in range(2):
                basis_ref[j, i * n : (i + 1) * n, part * width : (part + 1) * width] = raw_basis[
                    j, :, i, part, :
                ]

    load_mask.wait()
    load_basis.wait()
    order_basis(arnoldi - 1)

    row = lax.broadcasted_iota(jnp.int32, (cycles, cycles), 0)
    lane = lax.broadcasted_iota(jnp.int32, (cycles, cycles), 1)
    cycle_of_row = (row & (n - 1)) * per + (row >> shift_of(n))
    mask_row = mask_ref[...].astype(jnp.float32)
    mask_column = jnp.sum(jnp.where(lane == cycle_of_row, mask_row, 0.0), axis=1, keepdims=True)
    columns[me, :, :width2] = basis_ref[arnoldi - 1].astype(jnp.bfloat16)
    columns[me, :, width2:] = jnp.broadcast_to(mask_column, (cycles, 128)).astype(jnp.bfloat16)

    edge = reach * n
    drive[:edge] = jnp.zeros((edge, width2), jnp.bfloat16)
    drive[edge + cycles * n :] = jnp.zeros((edge, width2), jnp.bfloat16)
    total_rows = cycles * n
    order = lax.broadcasted_iota(jnp.int32, (total_rows, 1), 0)
    azimuth = order & (n - 1)
    cycle = order >> shift_of(n)
    block_row = (cycle & (per - 1)) * n + (cycle >> shift_of(per))
    wanted = ((azimuth - me) & (n - 1)) * cycles + block_row
    lanes = lax.broadcasted_iota(jnp.int32, (total_rows, total_rows), 1)
    pick = jnp.where(lanes == wanted, 1.0, 0.0).astype(jnp.bfloat16)
    own_order = lax.broadcasted_iota(jnp.int32, (piece, 1), 0)
    own_wanted = (own_order & (n - 1)) * cycles + (own_order >> shift_of(n)) * n + me
    own_lanes = lax.broadcasted_iota(jnp.int32, (piece, total_rows), 1)
    own_pick = jnp.where(own_lanes == own_wanted, 1.0, 0.0).astype(jnp.bfloat16)

    pl.semaphore_wait(barrier, n - 1)
    gather_sends = []

    def pass_on(slot, other):
        index = len(gather_sends)
        copy = pltpu.make_async_remote_copy(
            src_ref=columns.at[slot],
            dst_ref=columns.at[slot],
            send_sem=send_sem.at[0, index],
            recv_sem=recv_sem.at[0, slot],
            device_id={"azim": other},
            device_id_type=pl.DeviceIdType.MESH,
        )
        copy.start()
        gather_sends.append(copy)

    def arrived(slot):
        remote(0, columns.at[slot], columns.at[slot], core_peer, slot).wait_recv()

    for step in range(1, lines):
        pass_on(me, line_peer(step) * 4 + (me & 3))
    pass_on(me, side_peer)
    pass_on(me, core_peer)

    distance = jnp.minimum(me, n - me)

    def build(first, last):
        for offset in range(first, last):
            inside = jnp.where(distance <= band_ref[offset], 1.0, 0.0).astype(jnp.float32)
            keep = jnp.full((width, width), inside, jnp.float32).astype(jnp.bfloat16)
            real_part = raw_coupling[offset, 0] * keep
            imag_part = raw_coupling[offset, 1] * keep
            blocks[offset, :width, :width] = real_part
            blocks[offset, :width, width:] = imag_part
            blocks[offset, width:, :width] = -imag_part
            blocks[offset, width:, width:] = real_part

    for j in range(arnoldi - 1):
        order_basis(j)
    used = per * width2 // 128
    stored = basis_out.shape[1] // arnoldi
    for j in range(arnoldi):
        basis_out[:, j * stored : j * stored + used, :] = (
            to_lanes(basis_ref[j]).reshape(n, used, 128).astype(jnp.bfloat16)
        )

    arrived(side_peer)
    pass_on(side_peer, core_peer)
    load_coupling.wait()
    build(0, 1)
    built = 1
    for step in range(1, lines):
        far = lax.rem(line + lines - step, lines) * 4
        arrived(far + (me & 3))
        pass_on(far + (me & 3), side_peer)
        pass_on(far + (me & 3), core_peer)
        ready = 1 + (offsets - 1) * step // (lines - 1)
        build(built, ready)
        built = ready
    for step in range(1, lines):
        far = lax.rem(line + lines - step, lines) * 4
        arrived(far + (side_peer & 3))
        pass_on(far + (side_peer & 3), core_peer)
    for step in range(lines):
        far = lax.rem(line + lines - step, lines) * 4
        arrived(far + (core_peer & 3))
        arrived(far + ((me ^ 3) & 3))
    send_all(5, lambda other: basis_out.at[other], basis_in)
    basis_in[me] = basis_out[me]
    gathered = columns[...].reshape(total_rows, width2 + 128)
    picked = jnp.dot(pick, gathered, preferred_element_type=jnp.float32)
    drive[edge : edge + total_rows] = (picked[:, :width2] * picked[:, width2 : width2 + 1]).astype(
        jnp.bfloat16
    )
    own = jnp.dot(own_pick, gathered, preferred_element_type=jnp.float32)
    own_current = own[:, :width2]
    own_active = own[:, width2 : width2 + 1]

    def to_core(target):
        return pltpu.make_async_remote_copy(
            src_ref=partial.at[1 - core, target],
            dst_ref=core_in.at[target],
            send_sem=send_sem.at[1, target],
            recv_sem=recv_sem.at[1, target],
            device_id={"azim": core_peer},
            device_id_type=pl.DeviceIdType.MESH,
        )

    def to_side(target):
        return pltpu.make_async_remote_copy(
            src_ref=side_out.at[target],
            dst_ref=side_in.at[target],
            send_sem=send_sem.at[6, target],
            recv_sem=recv_sem.at[6, target],
            device_id={"azim": side_peer},
            device_id_type=pl.DeviceIdType.MESH,
        )

    def to_line(target):
        return pltpu.make_async_remote_copy(
            src_ref=line_out.at[target],
            dst_ref=line_in.at[line],
            send_sem=send_sem.at[7, target],
            recv_sem=recv_sem.at[7, line],
            device_id={"azim": target * 4 + (me & 3)},
            device_id_type=pl.DeviceIdType.MESH,
        )

    def from_line(source):
        return pltpu.make_async_remote_copy(
            src_ref=line_out.at[source],
            dst_ref=line_in.at[source],
            send_sem=send_sem.at[7, source],
            recv_sem=recv_sem.at[7, source],
            device_id={"azim": source * 4 + (me & 3)},
            device_id_type=pl.DeviceIdType.MESH,
        )

    group_rows = GROUP * 4 * piece
    groups = lines // GROUP
    own_group = line // GROUP
    targets = []
    for step in range(groups):
        group = lax.rem(own_group + 1 + step, groups)
        applied = jnp.zeros((group_rows, width2), jnp.float32)
        for offset in range(offsets):
            start = pl.multiple_of(group * group_rows + (2 * reach - offset) * n, 16)
            applied = applied + jnp.dot(
                drive[pl.ds(start, group_rows)],
                blocks[offset],
                preferred_element_type=jnp.float32,
            )
        applied = applied.astype(jnp.bfloat16)
        for i in range(GROUP):
            target = group * GROUP + i
            for part in range(4):
                first_row = (i * 4 + part) * piece
                partial[part & 1, target, part >> 1] = applied[first_row : first_row + piece]
            to_core(target).start()
            targets.append(target)

    load_precond.wait()
    load_table.wait()
    real_part = raw_precond[0].astype(jnp.bfloat16)
    imag_part = raw_precond[1].astype(jnp.bfloat16)
    solver[:width, :width] = real_part
    solver[:width, width:] = imag_part
    solver[width:, :width] = -imag_part
    solver[width:, width:] = real_part

    for target in targets:
        to_core(target).wait_recv()
        side_kept[target] = partial[core, target, side].astype(jnp.float32) + core_in[
            target, side
        ].astype(jnp.float32)
        side_out[target] = (
            partial[core, target, 1 - side].astype(jnp.float32)
            + core_in[target, 1 - side].astype(jnp.float32)
        ).astype(jnp.bfloat16)
        to_side(target).start()
    small_lane = lax.broadcasted_iota(jnp.int32, (1, 128), 1)

    def place(total, index, value):
        return total + jnp.where(small_lane == index, value, 0.0)

    def full_sum(value):
        return jnp.sum(jnp.sum(value, axis=0, keepdims=True), axis=1, keepdims=True)

    packed = jnp.zeros((1, 128), jnp.float32)
    gram_slots = []
    slot = 2 * arnoldi + 1
    for i in range(arnoldi):
        for j in range(i, arnoldi):
            left_real = basis_ref[i, :, :width]
            left_imag = basis_ref[i, :, width:]
            right_real = basis_ref[j, :, :width]
            right_imag = basis_ref[j, :, width:]
            packed = place(packed, slot, full_sum(left_real * right_real + left_imag * right_imag))
            if i == j:
                gram_slots.append((i, j, slot, None))
                slot += 1
            else:
                packed = place(
                    packed, slot + 1, full_sum(left_real * right_imag - left_imag * right_real)
                )
                gram_slots.append((i, j, slot, slot + 1))
                slot += 2

    for target in targets:
        to_side(target).wait_recv()
        both_sides = side_kept[target] + side_in[target].astype(jnp.float32)
        side_kept[target] = both_sides
        line_out[target] = both_sides.astype(jnp.bfloat16)

        @pl.when(target != line)
        def _():
            to_line(target).start()

    applied = side_kept[line]
    for step in range(1, lines):
        source = line_peer(step)
        from_line(source).wait_recv()
        applied = applied + line_in[source].astype(jnp.float32)
    driven = own_active * applied + (1.0 - own_active) * own_current

    def to_rows(value):
        return jnp.concatenate(
            [value[:, i * width2 : (i + 1) * width2] for i in range(per)], axis=0
        )

    def azimuth_transform(value, inverse):
        both = jnp.dot(
            table_ref[...],
            value,
            preferred_element_type=jnp.float32,
            precision=lax.Precision.HIGHEST,
        )
        cosine = both[:n]
        sine = both[n:]
        outs = []
        for i in range(per):
            real = slice(i * width2, i * width2 + width)
            imag = slice(i * width2 + width, (i + 1) * width2)
            if inverse:
                outs.append((cosine[:, real] - sine[:, imag]) * (1.0 / n))
                outs.append((cosine[:, imag] + sine[:, real]) * (1.0 / n))
            else:
                outs.append(cosine[:, real] + sine[:, imag])
                outs.append(cosine[:, imag] - sine[:, real])
        return jnp.concatenate(outs, axis=1)

    def exchange(phase, value, out_buffer, in_buffer):
        used = value.shape[1] // 128
        out_buffer[:, :used, :] = value.reshape(n, used, 128).astype(jnp.bfloat16)
        send_all(phase, lambda other: out_buffer.at[other], in_buffer)
        in_buffer[me] = out_buffer[me]
        wait_arrivals(phase, in_buffer)
        return in_buffer[:, :used, :].astype(jnp.float32).reshape(n, used * 128)

    spectrum = exchange(2, azimuth_transform(to_lanes(driven), False), mode_out, mode_in)
    solved = jnp.dot(
        to_rows(spectrum).astype(jnp.bfloat16), solver[...], preferred_element_type=jnp.float32
    )
    pieces = exchange(3, to_lanes(solved), back_out, back_in)
    field = azimuth_transform(pieces, True)
    wait_arrivals(5, basis_in)
    packed = place(packed, 2 * arnoldi, full_sum(field * field))
    turned = jnp.concatenate(
        [
            part
            for i in range(per)
            for part in (
                field[:, i * width2 + width : (i + 1) * width2],
                -field[:, i * width2 : i * width2 + width],
            )
        ],
        axis=1,
    )
    for j in range(arnoldi):
        vector = (
            basis_in[:, j * stored : j * stored + used, :].astype(jnp.float32).reshape(n, used * 128)
        )
        packed = place(packed, j, full_sum(vector * field))
        packed = place(packed, arnoldi + j, full_sum(vector * turned))
    head = packed.astype(jnp.bfloat16)
    rest = packed - head.astype(jnp.float32)
    middle = rest.astype(jnp.bfloat16)
    last = (rest - middle.astype(jnp.float32)).astype(jnp.bfloat16)
    field_out[:, :used, :] = field.reshape(n, used, 128).astype(jnp.bfloat16)
    for part, value in enumerate((head, middle, last)):
        field_out[:, used + part : used + part + 1, :] = jnp.broadcast_to(
            value.reshape(1, 1, 128), (n, 1, 128)
        )
    send_all(4, lambda other: field_out.at[other], field_in)
    field_in[me] = field_out[me]
    wait_arrivals(4, field_in)
    result = to_rows(field_in[:, :used, :].astype(jnp.float32).reshape(n, used * 128))
    result_real = result[:, :width]
    result_imag = result[:, width:]
    parts = jnp.sum(field_in[:, used : used + 3, :].astype(jnp.float32), axis=0)
    total = parts[0:1] + parts[1:2] + parts[2:3]
    total = total * (1.0 / elements)

    def entry(index):
        return total[:, index : index + 1]

    project_real = [entry(j) for j in range(arnoldi)]
    project_imag = [entry(arnoldi + j) for j in range(arnoldi)]
    norm_square = entry(2 * arnoldi)
    for j in range(arnoldi):
        norm_square = norm_square - 2.0 * (
            project_real[j] * project_real[j] + project_imag[j] * project_imag[j]
        )
    for i, j, real_slot, imag_slot in gram_slots:
        cross_real = project_real[i] * project_real[j] + project_imag[i] * project_imag[j]
        if i == j:
            norm_square = norm_square + cross_real * entry(real_slot)
        else:
            cross_imag = project_real[i] * project_imag[j] - project_imag[i] * project_real[j]
            norm_square = norm_square + 2.0 * (
                cross_real * entry(real_slot) - cross_imag * entry(imag_slot)
            )
    scale_norm = jnp.sqrt(jnp.maximum(norm_square, 0.0) + 1e-06)
    remainder_real = result_real
    remainder_imag = result_imag
    for j in range(arnoldi):
        basis_real = basis_ref[j, :, :width]
        basis_imag = basis_ref[j, :, width:]
        remainder_real = remainder_real - (
            project_real[j] * basis_real - project_imag[j] * basis_imag
        )
        remainder_imag = remainder_imag - (
            project_real[j] * basis_imag + project_imag[j] * basis_real
        )
    for i in range(per):
        out_ref[:, i, 0, :] = remainder_real[i * n : (i + 1) * n] / scale_norm
        out_ref[:, i, 1, :] = remainder_imag[i * n : (i + 1) * n] / scale_norm
    first = jnp.zeros((1, 128), jnp.float32)
    second = jnp.zeros((1, 128), jnp.float32)
    for j in range(arnoldi):
        first = place(first, j, project_real[j])
        second = place(second, j, project_imag[j])
    first = place(first, arnoldi, scale_norm)
    hess_ref[0:1] = first[:, : arnoldi + 1]
    hess_ref[1:2] = second[:, : arnoldi + 1]

    for copy in gather_sends:
        copy.wait_send()
    for target in range(lines):
        to_core(target).wait_send()
        to_side(target).wait_send()
    for step in range(1, lines):
        from_line(line_peer(step)).wait_send()
    wait_sends(2, lambda other: mode_out.at[other], mode_in)
    wait_sends(3, lambda other: back_out.at[other], back_in)
    wait_sends(4, lambda other: field_out.at[other], field_in)
    wait_sends(5, lambda other: basis_out.at[other], basis_in)


def fused_body(coupling, band, precond, basis, mask):
    n = lax.axis_size("azim")
    arnoldi, _, cycles, _, width = basis.shape
    offsets = coupling.shape[1]
    reach = offsets // 2
    per = cycles // n
    width2 = 2 * width
    rows = basis.reshape(arnoldi, n, per, 2, width)
    vmem = pl.BlockSpec(memory_space=pltpu.VMEM)
    anywhere = pl.BlockSpec(memory_space=pl.ANY)
    lines = n // 4
    message_rows = -(-(per * width2 // 128 + 3) // 16) * 16
    message = pltpu.VMEM((n, message_rows, 128), jnp.bfloat16)
    vector, column = pl.pallas_call(
        functools.partial(step_kernel, n, cycles, reach),
        out_shape=(
            jax.ShapeDtypeStruct((n, per, 2, width), jnp.float32),
            jax.ShapeDtypeStruct((2, arnoldi + 1), jnp.float32),
        ),
        in_specs=[
            pl.BlockSpec(memory_space=pltpu.SMEM),
            anywhere,
            anywhere,
            anywhere,
            anywhere,
            anywhere,
        ],
        out_specs=(vmem, vmem),
        scratch_shapes=[
            pltpu.VMEM(mask.shape, mask.dtype),
            pltpu.VMEM(rows.shape, rows.dtype),
            pltpu.VMEM((arnoldi, cycles, width2), rows.dtype),
            pltpu.VMEM((2 * n, n), jnp.float32),
            pltpu.VMEM(coupling.shape[1:], coupling.dtype),
            pltpu.VMEM(precond.shape[1:], precond.dtype),
            pltpu.VMEM((offsets, width2, width2), jnp.bfloat16),
            pltpu.VMEM((width2, width2), jnp.bfloat16),
            pltpu.VMEM((n, cycles, width2 + 128), jnp.bfloat16),
            pltpu.VMEM(((cycles + 2 * reach) * n, width2), jnp.bfloat16),
            pltpu.VMEM((2, lines, 2, per * n, width2), jnp.bfloat16),
            pltpu.VMEM((lines, 2, per * n, width2), jnp.bfloat16),
            pltpu.VMEM((lines, per * n, width2), jnp.float32),
            pltpu.VMEM((lines, per * n, width2), jnp.bfloat16),
            pltpu.VMEM((lines, per * n, width2), jnp.bfloat16),
            pltpu.VMEM((lines, per * n, width2), jnp.bfloat16),
            pltpu.VMEM((lines, per * n, width2), jnp.bfloat16),
            message,
            message,
            message,
            message,
            message,
            message,
            pltpu.VMEM((n, arnoldi * message_rows, 128), jnp.bfloat16),
            pltpu.VMEM((n, arnoldi * message_rows, 128), jnp.bfloat16),
            pltpu.SemaphoreType.DMA((5,)),
            pltpu.SemaphoreType.DMA((8, n)),
            pltpu.SemaphoreType.DMA((8, n)),
        ],
        compiler_params=pltpu.CompilerParams(
            collective_id=0, has_side_effects=True, vmem_limit_bytes=60 * 1024 * 1024
        ),
    )(band, mask, rows, jnp.asarray(fourier_constants(n)), coupling[0], precond[0])
    return vector.reshape(1, cycles, 2, width), column


def body(coupling, band, precond, basis, mask):
    n = lax.axis_size("azim")
    cycles = basis.shape[2]
    width = basis.shape[4]
    whole_pieces = cycles % n == 0 and n % 16 == 0 and width % 128 == 0
    if whole_pieces and n & (n - 1) == 0 and cycles & (cycles - 1) == 0:
        return fused_body(coupling, band, precond, basis, mask)
    return plain_body(coupling, band, precond, basis, mask)


def solution(mesh):
    return jax.shard_map(
        body,
        mesh=mesh,
        in_specs=(
            P("azim", "freq", None, None, None),
            P("freq"),
            P("azim", "freq", None, None),
            P("freq", "azim", None, None, None),
            P("azim", None),
        ),
        out_specs=(P("azim", "freq", None, None), P("freq", None)),
        check_vma=False,
    )
```

```python
import functools

import jax
import jax.numpy as jnp
import numpy as np
from jax import lax
from jax.experimental import pallas as pl
from jax.experimental.pallas import tpu as pltpu
from jax.sharding import PartitionSpec as P


def fourier_tables(azimuths):
    azimuth_steps = jnp.arange(azimuths, dtype=jnp.int32)
    phase_index = azimuth_steps[:, None] * azimuth_steps[None, :] % azimuths
    angles = phase_index.astype(jnp.float32) * (2.0 * jnp.pi / azimuths)
    return (jnp.cos(angles), jnp.sin(angles))


def transform(real_part, imag_part, cosine_table, sine_table, inverse):
    highest_accuracy = lax.Precision.HIGHEST
    cos_real = jnp.tensordot(cosine_table, real_part, axes=1, precision=highest_accuracy)
    cos_imag = jnp.tensordot(cosine_table, imag_part, axes=1, precision=highest_accuracy)
    sin_real = jnp.tensordot(sine_table, real_part, axes=1, precision=highest_accuracy)
    sin_imag = jnp.tensordot(sine_table, imag_part, axes=1, precision=highest_accuracy)
    if inverse:
        scaling = 1.0 / cosine_table.shape[0]
        return ((cos_real - sin_imag) * scaling, (cos_imag + sin_real) * scaling)
    return (cos_real + sin_imag, cos_imag - sin_real)


def block_matrix(matrix):
    real_part = matrix[..., 0, :, :]
    imag_part = matrix[..., 1, :, :]
    upper = jnp.concatenate([real_part, imag_part], axis=-1)
    lower = jnp.concatenate([-imag_part, real_part], axis=-1)
    return jnp.concatenate([upper, lower], axis=-2)


def cycle_coupling(column_rows, blocks):
    row_total, cycle_count, parts, basis_width = column_rows.shape
    cycle_reach = blocks.shape[0] // 2
    flattened = column_rows.reshape(row_total, cycle_count, parts * basis_width)
    padded = jnp.pad(flattened, ((0, 0), (cycle_reach, cycle_reach), (0, 0)))
    summed = jnp.zeros((row_total * cycle_count, parts * basis_width), jnp.float32)
    for offset in range(blocks.shape[0]):
        shifted = padded[:, 2 * cycle_reach - offset : 2 * cycle_reach - offset + cycle_count]
        summed = summed + jnp.dot(
            shifted.reshape(row_total * cycle_count, parts * basis_width),
            blocks[offset],
            preferred_element_type=jnp.float32,
            precision=None,
        )
    return summed.reshape(row_total, cycle_count, parts, basis_width)


def relayout(field, cosine_table, sine_table, send_out, send_back, inverse):
    azimuths = cosine_table.shape[0]
    cycle_count = field.shape[1]
    basis_width = field.shape[3]
    piece_width = cycle_count * basis_width // azimuths
    split_parts = jnp.transpose(field[0], (1, 0, 2)).reshape(2, azimuths, piece_width)
    pieces = jnp.transpose(split_parts, (1, 0, 2)).reshape(azimuths, 2 * piece_width)
    spread = send_out(pieces).reshape(azimuths, 2, piece_width)
    real_part, imag_part = transform(spread[:, 0], spread[:, 1], cosine_table, sine_table, inverse)
    joined = jnp.stack([real_part, imag_part], axis=1).reshape(azimuths, 2 * piece_width)
    returned = send_back(joined).reshape(azimuths, 2, piece_width)
    whole = jnp.transpose(returned, (1, 0, 2)).reshape(2, cycle_count, basis_width)
    return jnp.transpose(whole, (1, 0, 2))[None]


def plain_body(coupling, band, precond, basis, mask):
    highest_accuracy = lax.Precision.HIGHEST
    azimuths = lax.axis_size("azim")
    position = lax.axis_index("azim")
    cosine_table, sine_table = fourier_tables(azimuths)
    vectors = basis[:, 0]
    arnoldi_count = vectors.shape[0]
    cycle_count = vectors.shape[1]
    basis_width = vectors.shape[3]
    current = vectors[arnoldi_count - 1][None]
    active = mask.astype(jnp.float32)[:, :, None, None]
    driving = (active * current).astype(jnp.bfloat16)
    distance = jnp.minimum(position, azimuths - position)
    inside = (distance <= band).astype(coupling.dtype)
    kernel = coupling[0] * inside[:, None, None, None]
    blocks = block_matrix(kernel)
    gathered = lax.all_gather(driving, "azim", axis=0, tiled=True)
    aligned = jnp.roll(gathered, position, axis=0)
    applied = lax.psum_scatter(
        cycle_coupling(aligned, blocks), "azim", scatter_dimension=0, tiled=True
    )
    driven = active * applied + (1.0 - active) * current
    spectrum = relayout(
        driven,
        cosine_table,
        sine_table,
        lambda tensor: lax.all_to_all(
            tensor.astype(jnp.bfloat16), "azim", split_axis=0, concat_axis=0, tiled=True
        ).astype(tensor.dtype),
        lambda tensor: lax.all_to_all(
            tensor.astype(jnp.bfloat16), "azim", split_axis=0, concat_axis=0, tiled=True
        ).astype(tensor.dtype),
        False,
    )
    precond_blocks = block_matrix(precond[0])
    solved = jnp.dot(
        spectrum.reshape(cycle_count, 2 * basis_width),
        precond_blocks,
        preferred_element_type=jnp.float32,
        precision=highest_accuracy,
    )
    solved = solved.reshape(1, cycle_count, 2, basis_width)
    result = relayout(
        solved,
        cosine_table,
        sine_table,
        lambda tensor: lax.all_to_all(
            tensor.astype(jnp.bfloat16), "azim", split_axis=0, concat_axis=0, tiled=True
        ).astype(tensor.dtype),
        lambda tensor: lax.all_to_all(
            tensor.astype(jnp.bfloat16), "azim", split_axis=0, concat_axis=0, tiled=True
        ).astype(tensor.dtype),
        True,
    )
    elements = float(azimuths * cycle_count * basis_width)
    basis_real = vectors[:, :, 0]
    basis_imag = vectors[:, :, 1]
    result_real = result[0, :, 0]
    result_imag = result[0, :, 1]
    local_real = jnp.sum(
        basis_real * result_real[None] + basis_imag * result_imag[None], axis=(1, 2)
    )
    local_imag = jnp.sum(
        basis_real * result_imag[None] - basis_imag * result_real[None], axis=(1, 2)
    )
    sum_real, sum_imag = lax.psum((local_real, local_imag), "azim")
    project_real = sum_real / elements
    project_imag = sum_imag / elements
    coef_real = project_real[:, None, None]
    coef_imag = project_imag[:, None, None]
    remainder_real = result_real - jnp.sum(coef_real * basis_real - coef_imag * basis_imag, axis=0)
    remainder_imag = result_imag - jnp.sum(coef_real * basis_imag + coef_imag * basis_real, axis=0)
    norm_square = (
        lax.psum(jnp.sum(remainder_real * remainder_real + remainder_imag * remainder_imag), "azim")
        / elements
    )
    scale_norm = jnp.sqrt(norm_square + 1e-06)
    new_vector = (jnp.stack([remainder_real, remainder_imag], axis=1) / scale_norm)[None]
    hessenberg_column = jnp.stack(
        [
            jnp.concatenate([project_real, scale_norm[None]]),
            jnp.concatenate([project_imag, jnp.zeros((1,), jnp.float32)]),
        ]
    )
    return (new_vector, hessenberg_column)


def fourier_constants(azimuths):
    steps = np.arange(azimuths)
    angles = (steps[:, None] * steps[None, :] % azimuths) * (2.0 * np.pi / azimuths)
    table = np.concatenate([np.cos(angles), np.sin(angles)], axis=0)
    return (table / TABLE_SCALE).astype(np.float32)


TABLE_SCALE = 1.1328025


def wave_constants(azimuths, chunk):
    half = azimuths // 2
    start = np.arange(azimuths)[:, None, None, None, None, None]
    mode = np.arange(azimuths)[None, :, None, None, None, None]
    out_cycle = np.arange(chunk)[None, None, :, None, None, None]
    part = np.arange(2)[None, None, None, :, None, None]
    in_cycle = np.arange(chunk)[None, None, None, None, :, None]
    step = np.arange(half)[None, None, None, None, None, :]
    angle = (mode * (start + step) % azimuths) * (2.0 * np.pi / azimuths)
    value = np.where(part == 0, np.cos(angle), np.sin(angle)) * (out_cycle == in_cycle)
    value = value * TABLE_SCALE
    return value.reshape(azimuths, azimuths * chunk, 2 * chunk * half).astype(jnp.bfloat16)


def idle_constants(azimuths, cycles):
    half = azimuths // 2
    mode = np.arange(azimuths)[:, None, None, None, None, None]
    part = np.arange(2)[None, :, None, None, None, None]
    out_cycle = np.arange(cycles)[None, None, :, None, None, None]
    group = np.arange(2)[None, None, None, :, None, None]
    step = np.arange(half)[None, None, None, None, :, None]
    in_cycle = np.arange(cycles)[None, None, None, None, None, :]
    column = ((mode // half) ^ group) * half + step
    angle = (mode * column % azimuths) * (2.0 * np.pi / azimuths)
    value = np.where(part == 0, np.cos(angle), np.sin(angle)) * (out_cycle == in_cycle)
    value = value * TABLE_SCALE
    return value.reshape(azimuths, 2 * cycles, azimuths * cycles).astype(jnp.bfloat16)


CHUNK = 16


def step_kernel(
    n,
    cycles,
    reach,
    band_ref,
    mask_any,
    basis_any,
    table_any,
    wave_any,
    idle_any,
    coupling_ref,
    precond_ref,
    out_ref,
    hess_ref,
    mask_ref,
    raw_basis,
    basis_ref,
    table_ref,
    wave_ref,
    idle_ref,
    raw_coupling,
    raw_precond,
    blocks,
    solver,
    columns,
    masks,
    even_drive,
    odd_drive,
    early,
    partial,
    core_in,
    side_kept,
    side_out,
    side_in,
    line_out,
    line_in,
    back_out,
    back_in,
    field_out,
    field_in,
    basis_out,
    basis_in,
    load_sem,
    send_sem,
    recv_sem,
):
    arnoldi = basis_ref.shape[0]
    width2 = basis_ref.shape[2]
    width = width2 // 2
    lane_tiles = width2 // 128
    offsets = 2 * reach + 1
    per = cycles // n
    half = n // 2
    chunks = cycles // CHUNK
    elements = float(n * cycles * width)
    me = lax.axis_index("azim")
    core = me & 1
    side = (me >> 1) & 1
    line = me >> 2
    lines = n // 4
    core_peer = me ^ 1
    side_peer = me ^ 2
    own_half = me >> 3

    def peer(step):
        return lax.rem(me + step, n)

    barrier = pltpu.get_barrier_semaphore()
    for step in range(1, n):
        pl.semaphore_signal(
            barrier, inc=1, device_id={"azim": peer(step)}, device_id_type=pl.DeviceIdType.MESH
        )

    load_mask = pltpu.make_async_copy(mask_any, mask_ref, load_sem.at[0])
    load_last = pltpu.make_async_copy(
        basis_any.at[pl.ds(arnoldi - 1, 1)], raw_basis.at[pl.ds(arnoldi - 1, 1)], load_sem.at[1]
    )
    load_basis = pltpu.make_async_copy(
        basis_any.at[pl.ds(0, arnoldi - 1)], raw_basis.at[pl.ds(0, arnoldi - 1)], load_sem.at[2]
    )
    load_coupling = pltpu.make_async_copy(coupling_ref, raw_coupling, load_sem.at[3])
    load_table = pltpu.make_async_copy(table_any, table_ref, load_sem.at[4])
    start = (own_half * half + me) & (n - 1)
    load_wave = pltpu.make_async_copy(wave_any.at[start], wave_ref, load_sem.at[5])
    load_idle = pltpu.make_async_copy(idle_any.at[me], idle_ref, load_sem.at[6])
    load_precond = pltpu.make_async_copy(precond_ref, raw_precond, load_sem.at[7])
    for load in (
        load_mask,
        load_last,
        load_coupling,
        load_basis,
        load_table,
        load_wave,
        load_idle,
        load_precond,
    ):
        load.start()

    def remote(phase, source, target, other, slot):
        return pltpu.make_async_remote_copy(
            src_ref=source,
            dst_ref=target,
            send_sem=send_sem.at[phase, other],
            recv_sem=recv_sem.at[phase, slot],
            device_id={"azim": other},
            device_id_type=pl.DeviceIdType.MESH,
        )

    def send_all(phase, sources, targets):
        for step in range(1, n):
            other = peer(step)
            remote(phase, sources(other), targets.at[me], other, me).start()

    def wait_arrivals(phase, targets):
        for step in range(1, n):
            other = peer(step)
            remote(phase, targets.at[other], targets.at[other], other, other).wait_recv()

    def wait_sends(phase, sources, targets):
        for step in range(1, n):
            other = peer(step)
            remote(phase, sources(other), targets.at[me], other, me).wait_send()

    def to_lanes(value):
        return jnp.concatenate([value[i * n : (i + 1) * n] for i in range(per)], axis=1)

    def to_rows(value):
        return jnp.concatenate(
            [value[:, i * width2 : (i + 1) * width2] for i in range(per)], axis=0
        )

    def order_basis(j):
        for part in range(2):
            basis_ref[j, :, part * width : (part + 1) * width] = raw_basis[j, :, part, :]

    load_mask.wait()
    masks[me] = jnp.zeros((1, 128), jnp.float32)
    masks[me, :, :cycles] = mask_ref[...].astype(jnp.float32)
    load_last.wait()
    order_basis(arnoldi - 1)
    current = basis_ref[arnoldi - 1].astype(jnp.bfloat16)
    for tile in range(lane_tiles):
        columns[me, tile * cycles : (tile + 1) * cycles, :] = current[
            :, tile * 128 : (tile + 1) * 128
        ]

    pl.semaphore_wait(barrier, n - 1)
    gather_sends = []

    def pass_on(slot, other):
        index = len(gather_sends)
        copy = pltpu.make_async_remote_copy(
            src_ref=columns.at[slot],
            dst_ref=columns.at[slot],
            send_sem=send_sem.at[0, index],
            recv_sem=recv_sem.at[0, slot],
            device_id={"azim": other},
            device_id_type=pl.DeviceIdType.MESH,
        )
        copy.start()
        gather_sends.append(copy)

    def arrived(slot):
        remote(0, columns.at[slot], columns.at[slot], core_peer, slot).wait_recv()

    def slot_of(far, plane):
        return (line ^ far) * 4 + plane

    plane = me & 3
    for far in (1, 3, 2):
        pass_on(me, slot_of(far, plane))
    pass_on(me, side_peer)
    pass_on(me, core_peer)
    send_all(2, lambda other: masks.at[me], masks)

    rows = half * cycles
    padded = (cycles + 2 * reach) * half
    pick_row = lax.broadcasted_iota(jnp.int32, (padded, rows), 0)
    pick_lane = lax.broadcasted_iota(jnp.int32, (padded, rows), 1)
    pick_match = ((pick_row & (half - 1)) * cycles + (pick_row // half) - reach == pick_lane) & (
        (pick_row // half >= reach) & (pick_row // half < cycles + reach)
    )
    pick = jnp.where(pick_match, 1.0, 0.0).astype(jnp.bfloat16)

    load_basis.wait()
    for j in range(arnoldi - 1):
        order_basis(j)
    used = per * width2 // 128
    stored = basis_out.shape[1] // arnoldi
    for j in range(arnoldi):
        basis_out[:, j * stored : j * stored + used, :] = (
            to_lanes(basis_ref[j]).reshape(n, used, 128).astype(jnp.bfloat16)
        )

    distance = jnp.minimum(me, n - me)

    def build(offset):
        inside = jnp.where(distance <= band_ref[offset], 1.0, 0.0).astype(jnp.float32)
        keep = jnp.full((width, width), inside, jnp.float32).astype(jnp.bfloat16)
        real_part = raw_coupling[offset, 0] * keep
        imag_part = raw_coupling[offset, 1] * keep
        blocks[offset, :width, :width] = real_part
        blocks[offset, :width, width:] = imag_part
        blocks[offset, width:, :width] = -imag_part
        blocks[offset, width:, width:] = real_part

    load_coupling.wait()
    build(0)
    arrived(side_peer)
    pass_on(side_peer, core_peer)
    build(1)
    arrived(slot_of(1, plane))
    pass_on(slot_of(1, plane), side_peer)
    pass_on(slot_of(1, plane), core_peer)
    build(2)
    for far in (3, 2):
        arrived(slot_of(far, plane))
        pass_on(slot_of(far, plane), side_peer)
        pass_on(slot_of(far, plane), core_peer)
        build(6 - far)
    arrived(slot_of(1, plane ^ 2))
    pass_on(slot_of(1, plane ^ 2), core_peer)

    wait_arrivals(2, masks)
    every_mask = masks[...].reshape(n, 128)
    turn_row = lax.broadcasted_iota(jnp.int32, (n, n), 0)
    turn_lane = lax.broadcasted_iota(jnp.int32, (n, n), 1)
    turn = jnp.where(((start + turn_row) & (n - 1)) == turn_lane, 1.0, 0.0).astype(jnp.bfloat16)
    turned_mask = jnp.dot(
        turn, every_mask.astype(jnp.bfloat16), preferred_element_type=jnp.float32
    )
    mask_lane = lax.broadcasted_iota(jnp.int32, (rows, 128), 1)
    mask_row = lax.broadcasted_iota(jnp.int32, (rows, 128), 0)
    load_wave.wait()
    load_idle.wait()

    def group_start(group):
        base = pl.multiple_of((own_half ^ group) * half, half)
        tiles = [
            columns[pl.ds(base, half), tile * cycles : (tile + 1) * cycles, :].reshape(rows, 128)
            for tile in range(lane_tiles)
        ]
        gathered = jnp.concatenate(tiles, axis=1)
        group_mask = masks[pl.ds(base, half)]
        spread = jnp.broadcast_to(group_mask, (half, cycles, 128)).reshape(rows, 128)
        active = jnp.sum(
            jnp.where(mask_lane == (mask_row & (cycles - 1)), spread, 0.0), axis=1, keepdims=True
        )
        driving = (gathered.astype(jnp.float32) * active).astype(jnp.bfloat16)
        picked = jnp.dot(pick, driving, preferred_element_type=jnp.float32)
        even_drive[group] = picked.astype(jnp.bfloat16)
        odd_drive[group] = picked[half : padded - half].astype(jnp.bfloat16)
        return (gathered - driving).astype(jnp.bfloat16)

    def group_offset(group, offset):
        first = (2 * reach - offset) * half
        if offset % 2 == 0:
            source = even_drive[group, first : first + rows]
        else:
            source = odd_drive[group, first - half : first - half + rows]
        return jnp.dot(source, blocks[offset], preferred_element_type=jnp.float32)

    def group_finish(group, applied):
        spread = jnp.broadcast_to(
            turned_mask[group * half : (group + 1) * half].reshape(1, half, 128),
            (cycles, half, 128),
        ).reshape(rows, 128)
        active = jnp.sum(
            jnp.where(mask_lane == (mask_row // half), spread, 0.0), axis=1, keepdims=True
        )
        return (applied * active).astype(jnp.bfloat16)

    def wave(masked, chunk):
        block = masked[chunk * CHUNK * half : (chunk + 1) * CHUNK * half]
        swapped = jnp.concatenate([block[:, width:], -block[:, :width]], axis=1)
        return jnp.dot(
            wave_ref[...],
            jnp.concatenate([block, swapped], axis=0),
            preferred_element_type=jnp.float32,
        )

    for far in (0, 1):
        arrived(slot_of(far, plane ^ 1))
        arrived(slot_of(far, plane ^ 3))
    idle_rows = group_start(0)
    applied = group_offset(0, 0)
    for offset in range(1, offsets):
        applied = applied + group_offset(0, offset)
    masked = group_finish(0, applied)
    for chunk in range(chunks):
        early[chunk] = wave(masked, chunk)
    idle_modes = jnp.dot(
        idle_ref[:, :rows], idle_rows, preferred_element_type=jnp.float32
    )

    for far in (3, 2):
        arrived(slot_of(far, plane ^ 2))
        pass_on(slot_of(far, plane ^ 2), core_peer)
    for far in (3, 2):
        arrived(slot_of(far, plane ^ 1))
        arrived(slot_of(far, plane ^ 3))
    idle_rows = group_start(1)
    applied = group_offset(1, 0)
    for offset in range(1, offsets):
        applied = applied + group_offset(1, offset)
    masked = group_finish(1, applied)

    def to_core(chunk):
        return pltpu.make_async_remote_copy(
            src_ref=partial.at[1 - core, chunk],
            dst_ref=core_in.at[chunk],
            send_sem=send_sem.at[1, chunk],
            recv_sem=recv_sem.at[1, chunk],
            device_id={"azim": core_peer},
            device_id_type=pl.DeviceIdType.MESH,
        )

    def to_side(chunk, target):
        return pltpu.make_async_remote_copy(
            src_ref=side_out.at[chunk, target],
            dst_ref=side_in.at[chunk, target],
            send_sem=send_sem.at[6, chunk * lines + target],
            recv_sem=recv_sem.at[6, chunk * lines + target],
            device_id={"azim": side_peer},
            device_id_type=pl.DeviceIdType.MESH,
        )

    def to_line(chunk, target):
        return pltpu.make_async_remote_copy(
            src_ref=line_out.at[chunk, target],
            dst_ref=line_in.at[chunk, line],
            send_sem=send_sem.at[7, chunk * lines + target],
            recv_sem=recv_sem.at[7, chunk * lines + line],
            device_id={"azim": target * 4 + plane},
            device_id_type=pl.DeviceIdType.MESH,
        )

    def from_line(chunk, source):
        return pltpu.make_async_remote_copy(
            src_ref=line_out.at[chunk, source],
            dst_ref=line_in.at[chunk, source],
            send_sem=send_sem.at[7, chunk * lines + source],
            recv_sem=recv_sem.at[7, chunk * lines + source],
            device_id={"azim": source * 4 + plane},
            device_id_type=pl.DeviceIdType.MESH,
        )

    mode_of_row = lax.broadcasted_iota(jnp.int32, (n * CHUNK, 1), 0) // CHUNK
    sign = jnp.where((mode_of_row & 1) == 0, 1.0, -1.0)
    for chunk in range(chunks):
        modes = (early[chunk] + sign * wave(masked, chunk)).astype(jnp.bfloat16)
        for mode in range(n):
            partial[mode & 1, chunk, mode >> 2, (mode >> 1) & 1] = modes[
                mode * CHUNK : (mode + 1) * CHUNK
            ]
        to_core(chunk).start()

    def fold_core(chunk, target):
        side_out[chunk, target] = (
            partial[core, chunk, target, 1 - side].astype(jnp.float32)
            + core_in[chunk, target, 1 - side].astype(jnp.float32)
        ).astype(jnp.bfloat16)
        to_side(chunk, target).start()
        side_kept[chunk, target] = partial[core, chunk, target, side].astype(
            jnp.float32
        ) + core_in[chunk, target, side].astype(jnp.float32)

    for chunk in range(chunks):
        to_core(chunk).wait_recv()
        for far in (3, 2):
            fold_core(chunk, line ^ far)
    for far in (1, 0):
        for chunk in range(chunks):
            fold_core(chunk, line ^ far)

    send_all(5, lambda other: basis_out.at[other], basis_in)
    basis_in[me] = basis_out[me]
    idle_modes = idle_modes + jnp.dot(
        idle_ref[:, rows:], idle_rows, preferred_element_type=jnp.float32
    )
    idle_cos = idle_modes[:cycles]
    idle_sin = idle_modes[cycles:]
    idle_field = jnp.concatenate(
        [
            idle_cos[:, :width] + idle_sin[:, width:],
            idle_cos[:, width:] - idle_sin[:, :width],
        ],
        axis=1,
    )
    load_precond.wait()
    load_table.wait()
    real_part = raw_precond[0].astype(jnp.bfloat16)
    imag_part = raw_precond[1].astype(jnp.bfloat16)
    solver[:width, :width] = real_part
    solver[:width, width:] = imag_part
    solver[width:, :width] = -imag_part
    solver[width:, width:] = real_part

    for chunk, far in [(c, f) for fars in ((3, 2), (1,)) for c in range(chunks) for f in fars]:
        target = line ^ far
        to_side(chunk, target).wait_recv()
        line_out[chunk, target] = (
            side_kept[chunk, target] + side_in[chunk, target].astype(jnp.float32)
        ).astype(jnp.bfloat16)
        to_line(chunk, target).start()

    small_lane = lax.broadcasted_iota(jnp.int32, (1, 128), 1)

    def place(total, index, value):
        return total + jnp.where(small_lane == index, value, 0.0)

    def full_sum(value):
        return jnp.sum(jnp.sum(value, axis=0, keepdims=True), axis=1, keepdims=True)

    packed = jnp.zeros((1, 128), jnp.float32)
    gram_slots = []
    slot = 2 * arnoldi + 1
    for i in range(arnoldi):
        for j in range(i, arnoldi):
            left_real = basis_ref[i, :, :width]
            left_imag = basis_ref[i, :, width:]
            right_real = basis_ref[j, :, :width]
            right_imag = basis_ref[j, :, width:]
            packed = place(packed, slot, full_sum(left_real * right_real + left_imag * right_imag))
            if i == j:
                gram_slots.append((i, j, slot, None))
                slot += 1
            else:
                packed = place(
                    packed, slot + 1, full_sum(left_real * right_imag - left_imag * right_real)
                )
                gram_slots.append((i, j, slot, slot + 1))
                slot += 2

    spectrum_chunks = []
    for chunk in range(chunks):
        to_side(chunk, line).wait_recv()
        spectrum = side_kept[chunk, line] + side_in[chunk, line].astype(jnp.float32)
        for far in (1, 3, 2):
            from_line(chunk, line ^ far).wait_recv()
            spectrum = spectrum + line_in[chunk, line ^ far].astype(jnp.float32)
        spectrum_chunks.append(spectrum)
    spectrum = jnp.concatenate(spectrum_chunks, axis=0) + idle_field

    def azimuth_transform(value):
        both = jnp.dot(
            table_ref[...],
            value,
            preferred_element_type=jnp.float32,
            precision=lax.Precision.HIGHEST,
        )
        cosine = both[:n]
        sine = both[n:]
        outs = []
        for i in range(per):
            real = slice(i * width2, i * width2 + width)
            imag = slice(i * width2 + width, (i + 1) * width2)
            outs.append((cosine[:, real] - sine[:, imag]) * (1.0 / n))
            outs.append((cosine[:, imag] + sine[:, real]) * (1.0 / n))
        return jnp.concatenate(outs, axis=1)

    def exchange(phase, value, out_buffer, in_buffer):
        out_buffer[:, :used, :] = value.reshape(n, used, 128).astype(jnp.bfloat16)
        send_all(phase, lambda other: out_buffer.at[other], in_buffer)
        in_buffer[me] = out_buffer[me]
        wait_arrivals(phase, in_buffer)
        return in_buffer[:, :used, :].astype(jnp.float32).reshape(n, used * 128)

    solved = jnp.dot(
        spectrum.astype(jnp.bfloat16), solver[...], preferred_element_type=jnp.float32
    )
    pieces = exchange(3, to_lanes(solved), back_out, back_in)
    field = azimuth_transform(pieces)
    wait_arrivals(5, basis_in)
    packed = place(packed, 2 * arnoldi, full_sum(field * field))
    turned = jnp.concatenate(
        [
            part
            for i in range(per)
            for part in (
                field[:, i * width2 + width : (i + 1) * width2],
                -field[:, i * width2 : i * width2 + width],
            )
        ],
        axis=1,
    )
    for j in range(arnoldi):
        vector = (
            basis_in[:, j * stored : j * stored + used, :].astype(jnp.float32).reshape(n, used * 128)
        )
        packed = place(packed, j, full_sum(vector * field))
        packed = place(packed, arnoldi + j, full_sum(vector * turned))
    head = packed.astype(jnp.bfloat16)
    rest = packed - head.astype(jnp.float32)
    middle = rest.astype(jnp.bfloat16)
    last = (rest - middle.astype(jnp.float32)).astype(jnp.bfloat16)
    field_out[:, :used, :] = field.reshape(n, used, 128).astype(jnp.bfloat16)
    for part, value in enumerate((head, middle, last)):
        field_out[:, used + part : used + part + 1, :] = jnp.broadcast_to(
            value.reshape(1, 1, 128), (n, 1, 128)
        )
    send_all(4, lambda other: field_out.at[other], field_in)
    field_in[me] = field_out[me]
    wait_arrivals(4, field_in)
    result = to_rows(field_in[:, :used, :].astype(jnp.float32).reshape(n, used * 128))
    result_real = result[:, :width]
    result_imag = result[:, width:]
    parts = jnp.sum(field_in[:, used : used + 3, :].astype(jnp.float32), axis=0)
    total = parts[0:1] + parts[1:2] + parts[2:3]
    total = total * (1.0 / elements)

    def entry(index):
        return total[:, index : index + 1]

    project_real = [entry(j) for j in range(arnoldi)]
    project_imag = [entry(arnoldi + j) for j in range(arnoldi)]
    norm_square = entry(2 * arnoldi)
    for j in range(arnoldi):
        norm_square = norm_square - 2.0 * (
            project_real[j] * project_real[j] + project_imag[j] * project_imag[j]
        )
    for i, j, real_slot, imag_slot in gram_slots:
        cross_real = project_real[i] * project_real[j] + project_imag[i] * project_imag[j]
        if i == j:
            norm_square = norm_square + cross_real * entry(real_slot)
        else:
            cross_imag = project_real[i] * project_imag[j] - project_imag[i] * project_real[j]
            norm_square = norm_square + 2.0 * (
                cross_real * entry(real_slot) - cross_imag * entry(imag_slot)
            )
    scale_norm = jnp.sqrt(jnp.maximum(norm_square, 0.0) + 1e-06)
    remainder_real = result_real
    remainder_imag = result_imag
    for j in range(arnoldi):
        basis_real = basis_ref[j, :, :width]
        basis_imag = basis_ref[j, :, width:]
        remainder_real = remainder_real - (
            project_real[j] * basis_real - project_imag[j] * basis_imag
        )
        remainder_imag = remainder_imag - (
            project_real[j] * basis_imag + project_imag[j] * basis_real
        )
    out_ref[:, 0, :] = remainder_real / scale_norm
    out_ref[:, 1, :] = remainder_imag / scale_norm
    first = jnp.zeros((1, 128), jnp.float32)
    second = jnp.zeros((1, 128), jnp.float32)
    for j in range(arnoldi):
        first = place(first, j, project_real[j])
        second = place(second, j, project_imag[j])
    first = place(first, arnoldi, scale_norm)
    hess_ref[0:1] = first[:, : arnoldi + 1]
    hess_ref[1:2] = second[:, : arnoldi + 1]

    for copy in gather_sends:
        copy.wait_send()
    for chunk in range(chunks):
        to_core(chunk).wait_send()
        for target in range(lines):
            to_side(chunk, target).wait_send()
        for far in (1, 2, 3):
            to_line(chunk, line ^ far).wait_send()
    wait_sends(2, lambda other: masks.at[me], masks)
    wait_sends(3, lambda other: back_out.at[other], back_in)
    wait_sends(4, lambda other: field_out.at[other], field_in)
    wait_sends(5, lambda other: basis_out.at[other], basis_in)


def fused_body(coupling, band, precond, basis, mask):
    n = lax.axis_size("azim")
    arnoldi, _, cycles, _, width = basis.shape
    offsets = coupling.shape[1]
    reach = offsets // 2
    per = cycles // n
    half = n // 2
    chunks = cycles // CHUNK
    width2 = 2 * width
    vmem = pl.BlockSpec(memory_space=pltpu.VMEM)
    anywhere = pl.BlockSpec(memory_space=pl.ANY)
    lines = n // 4
    message_rows = -(-(per * width2 // 128 + 3) // 16) * 16
    message = pltpu.VMEM((n, message_rows, 128), jnp.bfloat16)
    waves = jnp.asarray(wave_constants(n, CHUNK))
    idles = jnp.asarray(idle_constants(n, cycles))
    vector, column = pl.pallas_call(
        functools.partial(step_kernel, n, cycles, reach),
        out_shape=(
            jax.ShapeDtypeStruct((cycles, 2, width), jnp.float32),
            jax.ShapeDtypeStruct((2, arnoldi + 1), jnp.float32),
        ),
        in_specs=[pl.BlockSpec(memory_space=pltpu.SMEM)] + [anywhere] * 7,
        out_specs=(vmem, vmem),
        scratch_shapes=[
            pltpu.VMEM(mask.shape, mask.dtype),
            pltpu.VMEM((arnoldi, cycles, 2, width), basis.dtype),
            pltpu.VMEM((arnoldi, cycles, width2), basis.dtype),
            pltpu.VMEM((2 * n, n), jnp.float32),
            pltpu.VMEM(waves.shape[1:], waves.dtype),
            pltpu.VMEM(idles.shape[1:], idles.dtype),
            pltpu.VMEM(coupling.shape[1:], coupling.dtype),
            pltpu.VMEM(precond.shape[1:], precond.dtype),
            pltpu.VMEM((offsets, width2, width2), jnp.bfloat16),
            pltpu.VMEM((width2, width2), jnp.bfloat16),
            pltpu.VMEM((n, width2 // 128 * cycles, 128), jnp.bfloat16),
            pltpu.VMEM((n, 1, 128), jnp.float32),
            pltpu.VMEM((2, (cycles + 2 * reach) * half, width2), jnp.bfloat16),
            pltpu.VMEM((2, (cycles + 2 * reach - 2) * half, width2), jnp.bfloat16),
            pltpu.VMEM((chunks, n * CHUNK, width2), jnp.float32),
            pltpu.VMEM((2, chunks, lines, 2, CHUNK, width2), jnp.bfloat16),
            pltpu.VMEM((chunks, lines, 2, CHUNK, width2), jnp.bfloat16),
            pltpu.VMEM((chunks, lines, CHUNK, width2), jnp.float32),
            pltpu.VMEM((chunks, lines, CHUNK, width2), jnp.bfloat16),
            pltpu.VMEM((chunks, lines, CHUNK, width2), jnp.bfloat16),
            pltpu.VMEM((chunks, lines, CHUNK, width2), jnp.bfloat16),
            pltpu.VMEM((chunks, lines, CHUNK, width2), jnp.bfloat16),
            message,
            message,
            message,
            message,
            pltpu.VMEM((n, arnoldi * message_rows, 128), jnp.bfloat16),
            pltpu.VMEM((n, arnoldi * message_rows, 128), jnp.bfloat16),
            pltpu.SemaphoreType.DMA((8,)),
            pltpu.SemaphoreType.DMA((8, n)),
            pltpu.SemaphoreType.DMA((8, n)),
        ],
        compiler_params=pltpu.CompilerParams(
            collective_id=0, has_side_effects=True, vmem_limit_bytes=60 * 1024 * 1024
        ),
    )(
        band,
        mask,
        basis[:, 0],
        jnp.asarray(fourier_constants(n)),
        waves,
        idles,
        coupling[0],
        precond[0],
    )
    return vector[None], column


def body(coupling, band, precond, basis, mask):
    n = lax.axis_size("azim")
    cycles = basis.shape[2]
    width = basis.shape[4]
    if n == 16 and cycles == 32 and width % 128 == 0:
        return fused_body(coupling, band, precond, basis, mask)
    return plain_body(coupling, band, precond, basis, mask)


def solution(mesh):
    return jax.shard_map(
        body,
        mesh=mesh,
        in_specs=(
            P("azim", "freq", None, None, None),
            P("freq"),
            P("azim", "freq", None, None),
            P("freq", "azim", None, None, None),
            P("azim", None),
        ),
        out_specs=(P("azim", "freq", None, None), P("freq", None)),
        check_vma=False,
    )
```

```python
import functools

import jax
import jax.numpy as jnp
import numpy as np
from jax import lax
from jax.experimental import pallas as pl
from jax.experimental.pallas import tpu as pltpu
from jax.sharding import PartitionSpec as P


def fourier_tables(azimuths):
    azimuth_steps = jnp.arange(azimuths, dtype=jnp.int32)
    phase_index = azimuth_steps[:, None] * azimuth_steps[None, :] % azimuths
    angles = phase_index.astype(jnp.float32) * (2.0 * jnp.pi / azimuths)
    return (jnp.cos(angles), jnp.sin(angles))


def transform(real_part, imag_part, cosine_table, sine_table, inverse):
    highest_accuracy = lax.Precision.HIGHEST
    cos_real = jnp.tensordot(cosine_table, real_part, axes=1, precision=highest_accuracy)
    cos_imag = jnp.tensordot(cosine_table, imag_part, axes=1, precision=highest_accuracy)
    sin_real = jnp.tensordot(sine_table, real_part, axes=1, precision=highest_accuracy)
    sin_imag = jnp.tensordot(sine_table, imag_part, axes=1, precision=highest_accuracy)
    if inverse:
        scaling = 1.0 / cosine_table.shape[0]
        return ((cos_real - sin_imag) * scaling, (cos_imag + sin_real) * scaling)
    return (cos_real + sin_imag, cos_imag - sin_real)


def block_matrix(matrix):
    real_part = matrix[..., 0, :, :]
    imag_part = matrix[..., 1, :, :]
    upper = jnp.concatenate([real_part, imag_part], axis=-1)
    lower = jnp.concatenate([-imag_part, real_part], axis=-1)
    return jnp.concatenate([upper, lower], axis=-2)


def cycle_coupling(column_rows, blocks):
    row_total, cycle_count, parts, basis_width = column_rows.shape
    cycle_reach = blocks.shape[0] // 2
    flattened = column_rows.reshape(row_total, cycle_count, parts * basis_width)
    padded = jnp.pad(flattened, ((0, 0), (cycle_reach, cycle_reach), (0, 0)))
    summed = jnp.zeros((row_total * cycle_count, parts * basis_width), jnp.float32)
    for offset in range(blocks.shape[0]):
        shifted = padded[:, 2 * cycle_reach - offset : 2 * cycle_reach - offset + cycle_count]
        summed = summed + jnp.dot(
            shifted.reshape(row_total * cycle_count, parts * basis_width),
            blocks[offset],
            preferred_element_type=jnp.float32,
            precision=None,
        )
    return summed.reshape(row_total, cycle_count, parts, basis_width)


def relayout(field, cosine_table, sine_table, send_out, send_back, inverse):
    azimuths = cosine_table.shape[0]
    cycle_count = field.shape[1]
    basis_width = field.shape[3]
    piece_width = cycle_count * basis_width // azimuths
    split_parts = jnp.transpose(field[0], (1, 0, 2)).reshape(2, azimuths, piece_width)
    pieces = jnp.transpose(split_parts, (1, 0, 2)).reshape(azimuths, 2 * piece_width)
    spread = send_out(pieces).reshape(azimuths, 2, piece_width)
    real_part, imag_part = transform(spread[:, 0], spread[:, 1], cosine_table, sine_table, inverse)
    joined = jnp.stack([real_part, imag_part], axis=1).reshape(azimuths, 2 * piece_width)
    returned = send_back(joined).reshape(azimuths, 2, piece_width)
    whole = jnp.transpose(returned, (1, 0, 2)).reshape(2, cycle_count, basis_width)
    return jnp.transpose(whole, (1, 0, 2))[None]


def plain_body(coupling, band, precond, basis, mask):
    highest_accuracy = lax.Precision.HIGHEST
    azimuths = lax.axis_size("azim")
    position = lax.axis_index("azim")
    cosine_table, sine_table = fourier_tables(azimuths)
    vectors = basis[:, 0]
    arnoldi_count = vectors.shape[0]
    cycle_count = vectors.shape[1]
    basis_width = vectors.shape[3]
    current = vectors[arnoldi_count - 1][None]
    active = mask.astype(jnp.float32)[:, :, None, None]
    driving = (active * current).astype(jnp.bfloat16)
    distance = jnp.minimum(position, azimuths - position)
    inside = (distance <= band).astype(coupling.dtype)
    kernel = coupling[0] * inside[:, None, None, None]
    blocks = block_matrix(kernel)
    gathered = lax.all_gather(driving, "azim", axis=0, tiled=True)
    aligned = jnp.roll(gathered, position, axis=0)
    applied = lax.psum_scatter(
        cycle_coupling(aligned, blocks), "azim", scatter_dimension=0, tiled=True
    )
    driven = active * applied + (1.0 - active) * current
    spectrum = relayout(
        driven,
        cosine_table,
        sine_table,
        lambda tensor: lax.all_to_all(
            tensor.astype(jnp.bfloat16), "azim", split_axis=0, concat_axis=0, tiled=True
        ).astype(tensor.dtype),
        lambda tensor: lax.all_to_all(
            tensor.astype(jnp.bfloat16), "azim", split_axis=0, concat_axis=0, tiled=True
        ).astype(tensor.dtype),
        False,
    )
    precond_blocks = block_matrix(precond[0])
    solved = jnp.dot(
        spectrum.reshape(cycle_count, 2 * basis_width),
        precond_blocks,
        preferred_element_type=jnp.float32,
        precision=highest_accuracy,
    )
    solved = solved.reshape(1, cycle_count, 2, basis_width)
    result = relayout(
        solved,
        cosine_table,
        sine_table,
        lambda tensor: lax.all_to_all(
            tensor.astype(jnp.bfloat16), "azim", split_axis=0, concat_axis=0, tiled=True
        ).astype(tensor.dtype),
        lambda tensor: lax.all_to_all(
            tensor.astype(jnp.bfloat16), "azim", split_axis=0, concat_axis=0, tiled=True
        ).astype(tensor.dtype),
        True,
    )
    elements = float(azimuths * cycle_count * basis_width)
    basis_real = vectors[:, :, 0]
    basis_imag = vectors[:, :, 1]
    result_real = result[0, :, 0]
    result_imag = result[0, :, 1]
    local_real = jnp.sum(
        basis_real * result_real[None] + basis_imag * result_imag[None], axis=(1, 2)
    )
    local_imag = jnp.sum(
        basis_real * result_imag[None] - basis_imag * result_real[None], axis=(1, 2)
    )
    sum_real, sum_imag = lax.psum((local_real, local_imag), "azim")
    project_real = sum_real / elements
    project_imag = sum_imag / elements
    coef_real = project_real[:, None, None]
    coef_imag = project_imag[:, None, None]
    remainder_real = result_real - jnp.sum(coef_real * basis_real - coef_imag * basis_imag, axis=0)
    remainder_imag = result_imag - jnp.sum(coef_real * basis_imag + coef_imag * basis_real, axis=0)
    norm_square = (
        lax.psum(jnp.sum(remainder_real * remainder_real + remainder_imag * remainder_imag), "azim")
        / elements
    )
    scale_norm = jnp.sqrt(norm_square + 1e-06)
    new_vector = (jnp.stack([remainder_real, remainder_imag], axis=1) / scale_norm)[None]
    hessenberg_column = jnp.stack(
        [
            jnp.concatenate([project_real, scale_norm[None]]),
            jnp.concatenate([project_imag, jnp.zeros((1,), jnp.float32)]),
        ]
    )
    return (new_vector, hessenberg_column)


def fourier_constants(azimuths):
    steps = np.arange(azimuths)
    angles = (steps[:, None] * steps[None, :] % azimuths) * (2.0 * np.pi / azimuths)
    table = np.concatenate([np.cos(angles), np.sin(angles)], axis=0)
    return (table / TABLE_SCALE).astype(np.float32)


TABLE_SCALE = 1.1328025


def wave_constants(azimuths, chunk):
    half = azimuths // 2
    start = np.arange(azimuths)[:, None, None, None, None, None]
    mode = np.arange(azimuths)[None, :, None, None, None, None]
    out_cycle = np.arange(chunk)[None, None, :, None, None, None]
    part = np.arange(2)[None, None, None, :, None, None]
    in_cycle = np.arange(chunk)[None, None, None, None, :, None]
    step = np.arange(half)[None, None, None, None, None, :]
    angle = (mode * (start + step) % azimuths) * (2.0 * np.pi / azimuths)
    value = np.where(part == 0, np.cos(angle), np.sin(angle)) * (out_cycle == in_cycle)
    value = value * TABLE_SCALE
    return value.reshape(azimuths, azimuths * chunk, 2 * chunk * half).astype(jnp.bfloat16)


def idle_constants(azimuths, cycles):
    half = azimuths // 2
    mode = np.arange(azimuths)[:, None, None, None, None, None]
    part = np.arange(2)[None, :, None, None, None, None]
    out_cycle = np.arange(cycles)[None, None, :, None, None, None]
    group = np.arange(2)[None, None, None, :, None, None]
    step = np.arange(half)[None, None, None, None, :, None]
    in_cycle = np.arange(cycles)[None, None, None, None, None, :]
    column = ((mode // half) ^ group) * half + step
    angle = (mode * column % azimuths) * (2.0 * np.pi / azimuths)
    value = np.where(part == 0, np.cos(angle), np.sin(angle)) * (out_cycle == in_cycle)
    value = value * TABLE_SCALE
    return value.reshape(azimuths, 2 * cycles, azimuths * cycles).astype(jnp.bfloat16)


CHUNK = 16
MASKS, BACK, FIELD, BASIS, GATHER, CORE, SIDE, LINE = range(8)


def step_kernel(
    n,
    cycles,
    reach,
    band_ref,
    mask_any,
    basis_any,
    table_any,
    wave_any,
    idle_any,
    coupling_ref,
    precond_ref,
    out_ref,
    hess_ref,
    mask_ref,
    raw_basis,
    basis_ref,
    table_ref,
    wave_ref,
    idle_ref,
    raw_coupling,
    raw_precond,
    blocks,
    solver,
    columns,
    masks,
    even_drive,
    odd_drive,
    early,
    partial,
    core_in,
    side_kept,
    side_out,
    side_in,
    line_out,
    line_in,
    back_out,
    back_in,
    field_out,
    field_in,
    basis_out,
    basis_in,
    load_sem,
    send_sem,
    recv_sem,
):
    arnoldi = basis_ref.shape[0]
    width2 = basis_ref.shape[2]
    width = width2 // 2
    lane_tiles = width2 // 128
    offsets = 2 * reach + 1
    per = cycles // n
    half = n // 2
    chunks = cycles // CHUNK
    elements = float(n * cycles * width)
    me = lax.axis_index("azim")
    core = me & 1
    side = (me >> 1) & 1
    line = me >> 2
    lines = n // 4
    core_peer = me ^ 1
    side_peer = me ^ 2
    own_half = me >> 3

    def peer(step):
        return lax.rem(me + step, n)

    barrier = pltpu.get_barrier_semaphore()
    for step in range(1, n):
        pl.semaphore_signal(
            barrier, inc=1, device_id={"azim": peer(step)}, device_id_type=pl.DeviceIdType.MESH
        )

    load_mask = pltpu.make_async_copy(mask_any, mask_ref, load_sem.at[0])
    load_last = pltpu.make_async_copy(
        basis_any.at[pl.ds(arnoldi - 1, 1)], raw_basis.at[pl.ds(arnoldi - 1, 1)], load_sem.at[1]
    )
    load_basis = pltpu.make_async_copy(
        basis_any.at[pl.ds(0, arnoldi - 1)], raw_basis.at[pl.ds(0, arnoldi - 1)], load_sem.at[2]
    )
    load_coupling = pltpu.make_async_copy(coupling_ref, raw_coupling, load_sem.at[3])
    load_table = pltpu.make_async_copy(table_any, table_ref, load_sem.at[4])
    start = (own_half * half + me) & (n - 1)
    load_wave = pltpu.make_async_copy(wave_any.at[start], wave_ref, load_sem.at[5])
    load_idle = pltpu.make_async_copy(idle_any.at[me], idle_ref, load_sem.at[6])
    load_precond = pltpu.make_async_copy(precond_ref, raw_precond, load_sem.at[7])
    for load in (
        load_mask,
        load_last,
        load_coupling,
        load_basis,
        load_table,
        load_wave,
        load_idle,
        load_precond,
    ):
        load.start()

    def message(source, target, send, recv, other):
        return pltpu.make_async_remote_copy(
            src_ref=source,
            dst_ref=target,
            send_sem=send_sem.at[send],
            recv_sem=recv_sem.at[recv],
            device_id={"azim": other},
            device_id_type=pl.DeviceIdType.MESH,
        )

    def send_all(phase, sources, targets):
        for step in range(1, n):
            other = peer(step)
            message(sources(other), targets.at[me], phase, phase, other).start()

    def all_of(phase, buffers):
        return message(
            buffers.at[pl.ds(0, n - 1)], buffers.at[pl.ds(0, n - 1)], phase, phase, core_peer
        )

    def wait_arrivals(phase, targets):
        all_of(phase, targets).wait_recv()

    def wait_sends(phase, sources):
        all_of(phase, sources).wait_send()

    def to_lanes(value):
        return jnp.concatenate([value[i * n : (i + 1) * n] for i in range(per)], axis=1)

    def to_rows(value):
        return jnp.concatenate(
            [value[:, i * width2 : (i + 1) * width2] for i in range(per)], axis=0
        )

    def order_basis(j):
        for part in range(2):
            basis_ref[j, :, part * width : (part + 1) * width] = raw_basis[j, :, part, :]

    load_mask.wait()
    masks[me] = jnp.zeros((1, 128), jnp.float32)
    masks[me, :, :cycles] = mask_ref[...].astype(jnp.float32)
    load_last.wait()
    order_basis(arnoldi - 1)
    current = basis_ref[arnoldi - 1].astype(jnp.bfloat16)
    for tile in range(lane_tiles):
        columns[me, tile * cycles : (tile + 1) * cycles, :] = current[
            :, tile * 128 : (tile + 1) * 128
        ]

    pl.semaphore_wait(barrier, n - 1)

    def pass_on(slot, other):
        message(columns.at[slot], columns.at[slot], GATHER, GATHER + slot, other).start()

    def arrived(slot):
        message(
            columns.at[slot], columns.at[slot], GATHER, GATHER + slot, core_peer
        ).wait_recv()

    def slot_of(far, plane):
        return (line ^ far) * 4 + plane

    plane = me & 3
    for far in (1, 3, 2):
        pass_on(me, slot_of(far, plane))
    pass_on(me, side_peer)
    pass_on(me, core_peer)
    send_all(MASKS, lambda other: masks.at[me], masks)

    rows = half * cycles
    padded = (cycles + 2 * reach) * half
    pick_row = lax.broadcasted_iota(jnp.int32, (padded, rows), 0)
    pick_lane = lax.broadcasted_iota(jnp.int32, (padded, rows), 1)
    pick_match = ((pick_row & (half - 1)) * cycles + (pick_row // half) - reach == pick_lane) & (
        (pick_row // half >= reach) & (pick_row // half < cycles + reach)
    )
    pick = jnp.where(pick_match, 1.0, 0.0).astype(jnp.bfloat16)

    load_basis.wait()
    for j in range(arnoldi - 1):
        order_basis(j)
    used = per * width2 // 128
    stored = basis_out.shape[1] // arnoldi
    for j in range(arnoldi):
        basis_out[:, j * stored : j * stored + used, :] = (
            to_lanes(basis_ref[j]).reshape(n, used, 128).astype(jnp.bfloat16)
        )

    distance = jnp.minimum(me, n - me)

    def build(offset):
        inside = jnp.where(distance <= band_ref[offset], 1.0, 0.0).astype(jnp.float32)
        keep = jnp.full((width, width), inside, jnp.float32).astype(jnp.bfloat16)
        real_part = raw_coupling[offset, 0] * keep
        imag_part = raw_coupling[offset, 1] * keep
        blocks[offset, :width, :width] = real_part
        blocks[offset, :width, width:] = imag_part
        blocks[offset, width:, :width] = -imag_part
        blocks[offset, width:, width:] = real_part

    load_coupling.wait()
    build(0)
    arrived(side_peer)
    pass_on(side_peer, core_peer)
    build(1)
    arrived(slot_of(1, plane))
    pass_on(slot_of(1, plane), side_peer)
    pass_on(slot_of(1, plane), core_peer)
    build(2)
    for far in (3, 2):
        arrived(slot_of(far, plane))
        pass_on(slot_of(far, plane), side_peer)
        pass_on(slot_of(far, plane), core_peer)
        build(6 - far)
    arrived(slot_of(1, plane ^ 2))
    pass_on(slot_of(1, plane ^ 2), core_peer)

    wait_arrivals(MASKS, masks)
    every_mask = masks[...].reshape(n, 128)
    turn_row = lax.broadcasted_iota(jnp.int32, (n, n), 0)
    turn_lane = lax.broadcasted_iota(jnp.int32, (n, n), 1)
    turn = jnp.where(((start + turn_row) & (n - 1)) == turn_lane, 1.0, 0.0).astype(jnp.bfloat16)
    turned_mask = jnp.dot(
        turn, every_mask.astype(jnp.bfloat16), preferred_element_type=jnp.float32
    )
    mask_lane = lax.broadcasted_iota(jnp.int32, (rows, 128), 1)
    mask_row = lax.broadcasted_iota(jnp.int32, (rows, 128), 0)
    load_wave.wait()
    load_idle.wait()

    def group_start(group):
        base = pl.multiple_of((own_half ^ group) * half, half)
        tiles = [
            columns[pl.ds(base, half), tile * cycles : (tile + 1) * cycles, :].reshape(rows, 128)
            for tile in range(lane_tiles)
        ]
        gathered = jnp.concatenate(tiles, axis=1)
        group_mask = masks[pl.ds(base, half)]
        spread = jnp.broadcast_to(group_mask, (half, cycles, 128)).reshape(rows, 128)
        active = jnp.sum(
            jnp.where(mask_lane == (mask_row & (cycles - 1)), spread, 0.0), axis=1, keepdims=True
        )
        driving = (gathered.astype(jnp.float32) * active).astype(jnp.bfloat16)
        picked = jnp.dot(pick, driving, preferred_element_type=jnp.float32)
        even_drive[group] = picked.astype(jnp.bfloat16)
        odd_drive[group] = picked[half : padded - half].astype(jnp.bfloat16)
        return (gathered - driving).astype(jnp.bfloat16)

    def group_offset(group, offset):
        first = (2 * reach - offset) * half
        if offset % 2 == 0:
            source = even_drive[group, first : first + rows]
        else:
            source = odd_drive[group, first - half : first - half + rows]
        return jnp.dot(source, blocks[offset], preferred_element_type=jnp.float32)

    def group_finish(group, applied):
        spread = jnp.broadcast_to(
            turned_mask[group * half : (group + 1) * half].reshape(1, half, 128),
            (cycles, half, 128),
        ).reshape(rows, 128)
        active = jnp.sum(
            jnp.where(mask_lane == (mask_row // half), spread, 0.0), axis=1, keepdims=True
        )
        return (applied * active).astype(jnp.bfloat16)

    def wave(masked, chunk):
        block = masked[chunk * CHUNK * half : (chunk + 1) * CHUNK * half]
        swapped = jnp.concatenate([block[:, width:], -block[:, :width]], axis=1)
        return jnp.dot(
            wave_ref[...],
            jnp.concatenate([block, swapped], axis=0),
            preferred_element_type=jnp.float32,
        )

    for far in (0, 1):
        arrived(slot_of(far, plane ^ 1))
        arrived(slot_of(far, plane ^ 3))
    idle_rows = group_start(0)
    applied = group_offset(0, 0)
    for offset in range(1, offsets):
        applied = applied + group_offset(0, offset)
    masked = group_finish(0, applied)
    for chunk in range(chunks):
        early[chunk] = wave(masked, chunk)
    idle_modes = jnp.dot(
        idle_ref[:, :rows], idle_rows, preferred_element_type=jnp.float32
    )

    for far in (3, 2):
        arrived(slot_of(far, plane ^ 2))
        pass_on(slot_of(far, plane ^ 2), core_peer)
    for far in (3, 2):
        arrived(slot_of(far, plane ^ 1))
        arrived(slot_of(far, plane ^ 3))
    idle_rows = group_start(1)
    applied = group_offset(1, 0)
    for offset in range(1, offsets):
        applied = applied + group_offset(1, offset)
    masked = group_finish(1, applied)

    core_recv = GATHER + n
    side_recv = core_recv + chunks
    line_recv = side_recv + chunks * lines

    def to_core(chunk):
        return message(
            partial.at[1 - core, chunk], core_in.at[chunk], CORE, core_recv + chunk, core_peer
        )

    def to_side(chunk, target):
        return message(
            side_out.at[chunk, target],
            side_in.at[chunk, target],
            SIDE,
            side_recv + chunk * lines + target,
            side_peer,
        )

    def to_line(chunk, target):
        return message(
            line_out.at[chunk, target],
            line_in.at[chunk, line],
            LINE,
            line_recv + chunk,
            target * 4 + plane,
        )

    def from_lines(chunk):
        inner = line_in.at[chunk, pl.ds(0, lines - 1)]
        return message(inner, inner, LINE, line_recv + chunk, core_peer)

    mode_of_row = lax.broadcasted_iota(jnp.int32, (n * CHUNK, 1), 0) // CHUNK
    sign = jnp.where((mode_of_row & 1) == 0, 1.0, -1.0)
    for chunk in range(chunks):
        modes = (early[chunk] + sign * wave(masked, chunk)).astype(jnp.bfloat16)
        for mode in range(n):
            partial[mode & 1, chunk, mode >> 2, (mode >> 1) & 1] = modes[
                mode * CHUNK : (mode + 1) * CHUNK
            ]
        to_core(chunk).start()

    def fold_core(chunk, target):
        side_out[chunk, target] = (
            partial[core, chunk, target, 1 - side].astype(jnp.float32)
            + core_in[chunk, target, 1 - side].astype(jnp.float32)
        ).astype(jnp.bfloat16)
        to_side(chunk, target).start()
        side_kept[chunk, target] = partial[core, chunk, target, side].astype(
            jnp.float32
        ) + core_in[chunk, target, side].astype(jnp.float32)

    for chunk in range(chunks):
        to_core(chunk).wait_recv()
        for far in (3, 2):
            fold_core(chunk, line ^ far)
    for far in (1, 0):
        for chunk in range(chunks):
            fold_core(chunk, line ^ far)

    send_all(BASIS, lambda other: basis_out.at[other], basis_in)
    basis_in[me] = basis_out[me]
    idle_modes = idle_modes + jnp.dot(
        idle_ref[:, rows:], idle_rows, preferred_element_type=jnp.float32
    )
    idle_cos = idle_modes[:cycles]
    idle_sin = idle_modes[cycles:]
    idle_field = jnp.concatenate(
        [
            idle_cos[:, :width] + idle_sin[:, width:],
            idle_cos[:, width:] - idle_sin[:, :width],
        ],
        axis=1,
    )
    load_precond.wait()
    load_table.wait()
    real_part = raw_precond[0].astype(jnp.bfloat16)
    imag_part = raw_precond[1].astype(jnp.bfloat16)
    solver[:width, :width] = real_part
    solver[:width, width:] = imag_part
    solver[width:, :width] = -imag_part
    solver[width:, width:] = real_part

    for chunk, far in [(c, f) for fars in ((3, 2), (1,)) for c in range(chunks) for f in fars]:
        target = line ^ far
        to_side(chunk, target).wait_recv()
        line_out[chunk, target] = (
            side_kept[chunk, target] + side_in[chunk, target].astype(jnp.float32)
        ).astype(jnp.bfloat16)
        to_line(chunk, target).start()

    small_lane = lax.broadcasted_iota(jnp.int32, (1, 128), 1)

    def place(total, index, value):
        return total + jnp.where(small_lane == index, value, 0.0)

    def full_sum(value):
        return jnp.sum(jnp.sum(value, axis=0, keepdims=True), axis=1, keepdims=True)

    packed = jnp.zeros((1, 128), jnp.float32)
    gram_slots = []
    slot = 2 * arnoldi + 1
    for i in range(arnoldi):
        for j in range(i, arnoldi):
            left_real = basis_ref[i, :, :width]
            left_imag = basis_ref[i, :, width:]
            right_real = basis_ref[j, :, :width]
            right_imag = basis_ref[j, :, width:]
            packed = place(packed, slot, full_sum(left_real * right_real + left_imag * right_imag))
            if i == j:
                gram_slots.append((i, j, slot, None))
                slot += 1
            else:
                packed = place(
                    packed, slot + 1, full_sum(left_real * right_imag - left_imag * right_real)
                )
                gram_slots.append((i, j, slot, slot + 1))
                slot += 2

    spectrum_chunks = []
    for chunk in range(chunks):
        to_side(chunk, line).wait_recv()
        spectrum = side_kept[chunk, line] + side_in[chunk, line].astype(jnp.float32)
        from_lines(chunk).wait_recv()
        for far in (1, 3, 2):
            spectrum = spectrum + line_in[chunk, line ^ far].astype(jnp.float32)
        spectrum_chunks.append(spectrum)
    spectrum = jnp.concatenate(spectrum_chunks, axis=0) + idle_field

    def azimuth_transform(value):
        both = jnp.dot(
            table_ref[...],
            value,
            preferred_element_type=jnp.float32,
            precision=lax.Precision.HIGHEST,
        )
        cosine = both[:n]
        sine = both[n:]
        outs = []
        for i in range(per):
            real = slice(i * width2, i * width2 + width)
            imag = slice(i * width2 + width, (i + 1) * width2)
            outs.append((cosine[:, real] - sine[:, imag]) * (1.0 / n))
            outs.append((cosine[:, imag] + sine[:, real]) * (1.0 / n))
        return jnp.concatenate(outs, axis=1)

    def exchange(phase, value, out_buffer, in_buffer):
        out_buffer[:, :used, :] = value.reshape(n, used, 128).astype(jnp.bfloat16)
        send_all(phase, lambda other: out_buffer.at[other], in_buffer)
        in_buffer[me] = out_buffer[me]
        wait_arrivals(phase, in_buffer)
        return in_buffer[:, :used, :].astype(jnp.float32).reshape(n, used * 128)

    solved = jnp.dot(
        spectrum.astype(jnp.bfloat16), solver[...], preferred_element_type=jnp.float32
    )
    pieces = exchange(BACK, to_lanes(solved), back_out, back_in)
    field = azimuth_transform(pieces)
    wait_arrivals(BASIS, basis_in)
    packed = place(packed, 2 * arnoldi, full_sum(field * field))
    turned = jnp.concatenate(
        [
            part
            for i in range(per)
            for part in (
                field[:, i * width2 + width : (i + 1) * width2],
                -field[:, i * width2 : i * width2 + width],
            )
        ],
        axis=1,
    )
    for j in range(arnoldi):
        vector = (
            basis_in[:, j * stored : j * stored + used, :].astype(jnp.float32).reshape(n, used * 128)
        )
        packed = place(packed, j, full_sum(vector * field))
        packed = place(packed, arnoldi + j, full_sum(vector * turned))
    head = packed.astype(jnp.bfloat16)
    rest = packed - head.astype(jnp.float32)
    middle = rest.astype(jnp.bfloat16)
    last = (rest - middle.astype(jnp.float32)).astype(jnp.bfloat16)
    field_out[:, :used, :] = field.reshape(n, used, 128).astype(jnp.bfloat16)
    for part, value in enumerate((head, middle, last)):
        field_out[:, used + part : used + part + 1, :] = jnp.broadcast_to(
            value.reshape(1, 1, 128), (n, 1, 128)
        )
    send_all(FIELD, lambda other: field_out.at[other], field_in)
    field_in[me] = field_out[me]
    wait_arrivals(FIELD, field_in)
    result = to_rows(field_in[:, :used, :].astype(jnp.float32).reshape(n, used * 128))
    result_real = result[:, :width]
    result_imag = result[:, width:]
    parts = jnp.sum(field_in[:, used : used + 3, :].astype(jnp.float32), axis=0)
    total = parts[0:1] + parts[1:2] + parts[2:3]
    total = total * (1.0 / elements)

    def entry(index):
        return total[:, index : index + 1]

    project_real = [entry(j) for j in range(arnoldi)]
    project_imag = [entry(arnoldi + j) for j in range(arnoldi)]
    norm_square = entry(2 * arnoldi)
    for j in range(arnoldi):
        norm_square = norm_square - 2.0 * (
            project_real[j] * project_real[j] + project_imag[j] * project_imag[j]
        )
    for i, j, real_slot, imag_slot in gram_slots:
        cross_real = project_real[i] * project_real[j] + project_imag[i] * project_imag[j]
        if i == j:
            norm_square = norm_square + cross_real * entry(real_slot)
        else:
            cross_imag = project_real[i] * project_imag[j] - project_imag[i] * project_real[j]
            norm_square = norm_square + 2.0 * (
                cross_real * entry(real_slot) - cross_imag * entry(imag_slot)
            )
    scale_norm = jnp.sqrt(jnp.maximum(norm_square, 0.0) + 1e-06)
    remainder_real = result_real
    remainder_imag = result_imag
    for j in range(arnoldi):
        basis_real = basis_ref[j, :, :width]
        basis_imag = basis_ref[j, :, width:]
        remainder_real = remainder_real - (
            project_real[j] * basis_real - project_imag[j] * basis_imag
        )
        remainder_imag = remainder_imag - (
            project_real[j] * basis_imag + project_imag[j] * basis_real
        )
    out_ref[:, 0, :] = remainder_real / scale_norm
    out_ref[:, 1, :] = remainder_imag / scale_norm
    first = jnp.zeros((1, 128), jnp.float32)
    second = jnp.zeros((1, 128), jnp.float32)
    for j in range(arnoldi):
        first = place(first, j, project_real[j])
        second = place(second, j, project_imag[j])
    first = place(first, arnoldi, scale_norm)
    hess_ref[0:1] = first[:, : arnoldi + 1]
    hess_ref[1:2] = second[:, : arnoldi + 1]

    wait_sends(GATHER, columns)
    message(partial.at[0], partial.at[0], CORE, core_recv, core_peer).wait_send()
    message(side_out, side_out, SIDE, side_recv, side_peer).wait_send()
    sent = line_out.at[:, pl.ds(0, lines - 1)]
    message(sent, sent, LINE, line_recv, core_peer).wait_send()
    wait_sends(MASKS, masks)
    wait_sends(BACK, back_out)
    wait_sends(FIELD, field_out)
    wait_sends(BASIS, basis_out)


def hand_over(vector_ref, column_ref, out_ref, hess_ref):
    out_ref[0] = vector_ref[...]
    hess_ref[...] = column_ref[...]


def fused_body(coupling, band, precond, basis, mask):
    n = lax.axis_size("azim")
    arnoldi, _, cycles, _, width = basis.shape
    offsets = coupling.shape[1]
    reach = offsets // 2
    per = cycles // n
    half = n // 2
    chunks = cycles // CHUNK
    width2 = 2 * width
    vmem = pl.BlockSpec(memory_space=pltpu.VMEM)
    anywhere = pl.BlockSpec(memory_space=pl.ANY)
    lines = n // 4
    message_rows = -(-(per * width2 // 128 + 3) // 16) * 16
    message = pltpu.VMEM((n, message_rows, 128), jnp.bfloat16)
    waves = jnp.asarray(wave_constants(n, CHUNK))
    idles = jnp.asarray(idle_constants(n, cycles))
    vector, column = pl.pallas_call(
        functools.partial(step_kernel, n, cycles, reach),
        out_shape=(
            jax.ShapeDtypeStruct((cycles, 2, width), jnp.float32),
            jax.ShapeDtypeStruct((2, arnoldi + 1), jnp.float32),
        ),
        in_specs=[pl.BlockSpec(memory_space=pltpu.SMEM)] + [anywhere] * 7,
        out_specs=(vmem, vmem),
        scratch_shapes=[
            pltpu.VMEM(mask.shape, mask.dtype),
            pltpu.VMEM((arnoldi, cycles, 2, width), basis.dtype),
            pltpu.VMEM((arnoldi, cycles, width2), basis.dtype),
            pltpu.VMEM((2 * n, n), jnp.float32),
            pltpu.VMEM(waves.shape[1:], waves.dtype),
            pltpu.VMEM(idles.shape[1:], idles.dtype),
            pltpu.VMEM(coupling.shape[1:], coupling.dtype),
            pltpu.VMEM(precond.shape[1:], precond.dtype),
            pltpu.VMEM((offsets, width2, width2), jnp.bfloat16),
            pltpu.VMEM((width2, width2), jnp.bfloat16),
            pltpu.VMEM((n, width2 // 128 * cycles, 128), jnp.bfloat16),
            pltpu.VMEM((n, 1, 128), jnp.float32),
            pltpu.VMEM((2, (cycles + 2 * reach) * half, width2), jnp.bfloat16),
            pltpu.VMEM((2, (cycles + 2 * reach - 2) * half, width2), jnp.bfloat16),
            pltpu.VMEM((chunks, n * CHUNK, width2), jnp.float32),
            pltpu.VMEM((2, chunks, lines, 2, CHUNK, width2), jnp.bfloat16),
            pltpu.VMEM((chunks, lines, 2, CHUNK, width2), jnp.bfloat16),
            pltpu.VMEM((chunks, lines, CHUNK, width2), jnp.float32),
            pltpu.VMEM((chunks, lines, CHUNK, width2), jnp.bfloat16),
            pltpu.VMEM((chunks, lines, CHUNK, width2), jnp.bfloat16),
            pltpu.VMEM((chunks, lines, CHUNK, width2), jnp.bfloat16),
            pltpu.VMEM((chunks, lines, CHUNK, width2), jnp.bfloat16),
            message,
            message,
            message,
            message,
            pltpu.VMEM((n, arnoldi * message_rows, 128), jnp.bfloat16),
            pltpu.VMEM((n, arnoldi * message_rows, 128), jnp.bfloat16),
            pltpu.SemaphoreType.DMA((8,)),
            pltpu.SemaphoreType.DMA((8,)),
            pltpu.SemaphoreType.DMA((GATHER + n + chunks * (lines + 2),)),
        ],
        compiler_params=pltpu.CompilerParams(
            collective_id=0, has_side_effects=True, vmem_limit_bytes=60 * 1024 * 1024
        ),
    )(
        band,
        mask,
        basis[:, 0],
        jnp.asarray(fourier_constants(n)),
        waves,
        idles,
        coupling[0],
        precond[0],
    )
    return pl.pallas_call(
        hand_over,
        out_shape=(
            jax.ShapeDtypeStruct((1,) + vector.shape, vector.dtype),
            jax.ShapeDtypeStruct(column.shape, column.dtype),
        ),
        in_specs=[vmem, vmem],
        out_specs=(vmem, vmem),
    )(vector, column)


def body(coupling, band, precond, basis, mask):
    n = lax.axis_size("azim")
    cycles = basis.shape[2]
    width = basis.shape[4]
    if n == 16 and cycles == 32 and width % 128 == 0:
        return fused_body(coupling, band, precond, basis, mask)
    return plain_body(coupling, band, precond, basis, mask)


def solution(mesh):
    return jax.shard_map(
        body,
        mesh=mesh,
        in_specs=(
            P("azim", "freq", None, None, None),
            P("freq"),
            P("azim", "freq", None, None),
            P("freq", "azim", None, None, None),
            P("azim", None),
        ),
        out_specs=(P("azim", "freq", None, None), P("freq", None)),
        check_vma=False,
    )
```

```python
import functools

import jax
import jax.numpy as jnp
import numpy as np
from jax import lax
from jax.experimental import pallas as pl
from jax.experimental.pallas import tpu as pltpu
from jax.sharding import PartitionSpec as P


def fourier_tables(azimuths):
    azimuth_steps = jnp.arange(azimuths, dtype=jnp.int32)
    phase_index = azimuth_steps[:, None] * azimuth_steps[None, :] % azimuths
    angles = phase_index.astype(jnp.float32) * (2.0 * jnp.pi / azimuths)
    return (jnp.cos(angles), jnp.sin(angles))


def transform(real_part, imag_part, cosine_table, sine_table, inverse):
    highest_accuracy = lax.Precision.HIGHEST
    cos_real = jnp.tensordot(cosine_table, real_part, axes=1, precision=highest_accuracy)
    cos_imag = jnp.tensordot(cosine_table, imag_part, axes=1, precision=highest_accuracy)
    sin_real = jnp.tensordot(sine_table, real_part, axes=1, precision=highest_accuracy)
    sin_imag = jnp.tensordot(sine_table, imag_part, axes=1, precision=highest_accuracy)
    if inverse:
        scaling = 1.0 / cosine_table.shape[0]
        return ((cos_real - sin_imag) * scaling, (cos_imag + sin_real) * scaling)
    return (cos_real + sin_imag, cos_imag - sin_real)


def block_matrix(matrix):
    real_part = matrix[..., 0, :, :]
    imag_part = matrix[..., 1, :, :]
    upper = jnp.concatenate([real_part, imag_part], axis=-1)
    lower = jnp.concatenate([-imag_part, real_part], axis=-1)
    return jnp.concatenate([upper, lower], axis=-2)


def cycle_coupling(column_rows, blocks):
    row_total, cycle_count, parts, basis_width = column_rows.shape
    cycle_reach = blocks.shape[0] // 2
    flattened = column_rows.reshape(row_total, cycle_count, parts * basis_width)
    padded = jnp.pad(flattened, ((0, 0), (cycle_reach, cycle_reach), (0, 0)))
    summed = jnp.zeros((row_total * cycle_count, parts * basis_width), jnp.float32)
    for offset in range(blocks.shape[0]):
        shifted = padded[:, 2 * cycle_reach - offset : 2 * cycle_reach - offset + cycle_count]
        summed = summed + jnp.dot(
            shifted.reshape(row_total * cycle_count, parts * basis_width),
            blocks[offset],
            preferred_element_type=jnp.float32,
            precision=None,
        )
    return summed.reshape(row_total, cycle_count, parts, basis_width)


def relayout(field, cosine_table, sine_table, send_out, send_back, inverse):
    azimuths = cosine_table.shape[0]
    cycle_count = field.shape[1]
    basis_width = field.shape[3]
    piece_width = cycle_count * basis_width // azimuths
    split_parts = jnp.transpose(field[0], (1, 0, 2)).reshape(2, azimuths, piece_width)
    pieces = jnp.transpose(split_parts, (1, 0, 2)).reshape(azimuths, 2 * piece_width)
    spread = send_out(pieces).reshape(azimuths, 2, piece_width)
    real_part, imag_part = transform(spread[:, 0], spread[:, 1], cosine_table, sine_table, inverse)
    joined = jnp.stack([real_part, imag_part], axis=1).reshape(azimuths, 2 * piece_width)
    returned = send_back(joined).reshape(azimuths, 2, piece_width)
    whole = jnp.transpose(returned, (1, 0, 2)).reshape(2, cycle_count, basis_width)
    return jnp.transpose(whole, (1, 0, 2))[None]


def plain_body(coupling, band, precond, basis, mask):
    highest_accuracy = lax.Precision.HIGHEST
    azimuths = lax.axis_size("azim")
    position = lax.axis_index("azim")
    cosine_table, sine_table = fourier_tables(azimuths)
    vectors = basis[:, 0]
    arnoldi_count = vectors.shape[0]
    cycle_count = vectors.shape[1]
    basis_width = vectors.shape[3]
    current = vectors[arnoldi_count - 1][None]
    active = mask.astype(jnp.float32)[:, :, None, None]
    driving = (active * current).astype(jnp.bfloat16)
    distance = jnp.minimum(position, azimuths - position)
    inside = (distance <= band).astype(coupling.dtype)
    kernel = coupling[0] * inside[:, None, None, None]
    blocks = block_matrix(kernel)
    gathered = lax.all_gather(driving, "azim", axis=0, tiled=True)
    aligned = jnp.roll(gathered, position, axis=0)
    applied = lax.psum_scatter(
        cycle_coupling(aligned, blocks), "azim", scatter_dimension=0, tiled=True
    )
    driven = active * applied + (1.0 - active) * current
    spectrum = relayout(
        driven,
        cosine_table,
        sine_table,
        lambda tensor: lax.all_to_all(
            tensor.astype(jnp.bfloat16), "azim", split_axis=0, concat_axis=0, tiled=True
        ).astype(tensor.dtype),
        lambda tensor: lax.all_to_all(
            tensor.astype(jnp.bfloat16), "azim", split_axis=0, concat_axis=0, tiled=True
        ).astype(tensor.dtype),
        False,
    )
    precond_blocks = block_matrix(precond[0])
    solved = jnp.dot(
        spectrum.reshape(cycle_count, 2 * basis_width),
        precond_blocks,
        preferred_element_type=jnp.float32,
        precision=highest_accuracy,
    )
    solved = solved.reshape(1, cycle_count, 2, basis_width)
    result = relayout(
        solved,
        cosine_table,
        sine_table,
        lambda tensor: lax.all_to_all(
            tensor.astype(jnp.bfloat16), "azim", split_axis=0, concat_axis=0, tiled=True
        ).astype(tensor.dtype),
        lambda tensor: lax.all_to_all(
            tensor.astype(jnp.bfloat16), "azim", split_axis=0, concat_axis=0, tiled=True
        ).astype(tensor.dtype),
        True,
    )
    elements = float(azimuths * cycle_count * basis_width)
    basis_real = vectors[:, :, 0]
    basis_imag = vectors[:, :, 1]
    result_real = result[0, :, 0]
    result_imag = result[0, :, 1]
    local_real = jnp.sum(
        basis_real * result_real[None] + basis_imag * result_imag[None], axis=(1, 2)
    )
    local_imag = jnp.sum(
        basis_real * result_imag[None] - basis_imag * result_real[None], axis=(1, 2)
    )
    sum_real, sum_imag = lax.psum((local_real, local_imag), "azim")
    project_real = sum_real / elements
    project_imag = sum_imag / elements
    coef_real = project_real[:, None, None]
    coef_imag = project_imag[:, None, None]
    remainder_real = result_real - jnp.sum(coef_real * basis_real - coef_imag * basis_imag, axis=0)
    remainder_imag = result_imag - jnp.sum(coef_real * basis_imag + coef_imag * basis_real, axis=0)
    norm_square = (
        lax.psum(jnp.sum(remainder_real * remainder_real + remainder_imag * remainder_imag), "azim")
        / elements
    )
    scale_norm = jnp.sqrt(norm_square + 1e-06)
    new_vector = (jnp.stack([remainder_real, remainder_imag], axis=1) / scale_norm)[None]
    hessenberg_column = jnp.stack(
        [
            jnp.concatenate([project_real, scale_norm[None]]),
            jnp.concatenate([project_imag, jnp.zeros((1,), jnp.float32)]),
        ]
    )
    return (new_vector, hessenberg_column)


def fourier_constants(azimuths):
    steps = np.arange(azimuths)
    angles = (steps[:, None] * steps[None, :] % azimuths) * (2.0 * np.pi / azimuths)
    table = np.concatenate([np.cos(angles), np.sin(angles)], axis=0)
    return (table / TABLE_SCALE).astype(np.float32)


TABLE_SCALE = 1.1328025


def wave_constants(azimuths, chunk):
    half = azimuths // 2
    start = np.arange(azimuths)[:, None, None, None, None, None]
    mode = np.arange(azimuths)[None, :, None, None, None, None]
    out_cycle = np.arange(chunk)[None, None, :, None, None, None]
    part = np.arange(2)[None, None, None, :, None, None]
    in_cycle = np.arange(chunk)[None, None, None, None, :, None]
    step = np.arange(half)[None, None, None, None, None, :]
    angle = (mode * (start + step) % azimuths) * (2.0 * np.pi / azimuths)
    value = np.where(part == 0, np.cos(angle), np.sin(angle)) * (out_cycle == in_cycle)
    value = value * TABLE_SCALE
    return value.reshape(azimuths, azimuths * chunk, 2 * chunk * half).astype(jnp.bfloat16)


def idle_constants(azimuths, cycles):
    half = azimuths // 2
    mode = np.arange(azimuths)[:, None, None, None, None, None]
    part = np.arange(2)[None, :, None, None, None, None]
    out_cycle = np.arange(cycles)[None, None, :, None, None, None]
    group = np.arange(2)[None, None, None, :, None, None]
    step = np.arange(half)[None, None, None, None, :, None]
    in_cycle = np.arange(cycles)[None, None, None, None, None, :]
    column = ((mode // half) ^ group) * half + step
    angle = (mode * column % azimuths) * (2.0 * np.pi / azimuths)
    value = np.where(part == 0, np.cos(angle), np.sin(angle)) * (out_cycle == in_cycle)
    value = value * TABLE_SCALE
    return value.reshape(azimuths, 2 * cycles, azimuths * cycles).astype(jnp.bfloat16)


CHUNK = 16
MASKS, BACK, FIELD, BASIS, GATHER, CORE, SIDE, LINE = range(8)


def step_kernel(
    n,
    cycles,
    reach,
    band_ref,
    mask_any,
    basis_any,
    table_any,
    wave_any,
    idle_any,
    coupling_ref,
    precond_ref,
    out_ref,
    hess_ref,
    mask_ref,
    raw_basis,
    basis_ref,
    table_ref,
    wave_ref,
    idle_ref,
    raw_coupling,
    raw_precond,
    blocks,
    solver,
    columns,
    masks,
    even_drive,
    odd_drive,
    early,
    partial,
    core_in,
    side_out,
    side_in,
    line_out,
    line_in,
    back_out,
    back_in,
    field_out,
    field_in,
    basis_out,
    basis_in,
    spread_ref,
    load_sem,
    send_sem,
    recv_sem,
):
    arnoldi = basis_ref.shape[0]
    width2 = basis_ref.shape[2]
    width = width2 // 2
    lane_tiles = width2 // 128
    offsets = 2 * reach + 1
    per = cycles // n
    half = n // 2
    chunks = cycles // CHUNK
    elements = float(n * cycles * width)
    me = lax.axis_index("azim")
    core = me & 1
    side = (me >> 1) & 1
    line = me >> 2
    lines = n // 4
    core_peer = me ^ 1
    side_peer = me ^ 2
    own_half = me >> 3

    def peer(step):
        return me ^ (n - step)

    barrier = pltpu.get_barrier_semaphore()
    for step in range(1, n):
        pl.semaphore_signal(
            barrier, inc=1, device_id={"azim": peer(step)}, device_id_type=pl.DeviceIdType.MESH
        )

    load_mask = pltpu.make_async_copy(mask_any, mask_ref, load_sem.at[0])
    load_last = pltpu.make_async_copy(
        basis_any.at[pl.ds(arnoldi - 1, 1)], raw_basis.at[pl.ds(arnoldi - 1, 1)], load_sem.at[1]
    )
    load_basis = pltpu.make_async_copy(
        basis_any.at[pl.ds(0, arnoldi - 1)], raw_basis.at[pl.ds(0, arnoldi - 1)], load_sem.at[2]
    )
    load_coupling = pltpu.make_async_copy(coupling_ref, raw_coupling, load_sem.at[3])
    load_table = pltpu.make_async_copy(table_any, table_ref, load_sem.at[4])
    start = (own_half * half + me) & (n - 1)
    load_wave = pltpu.make_async_copy(wave_any.at[start], wave_ref, load_sem.at[5])
    load_idle = pltpu.make_async_copy(idle_any.at[me], idle_ref, load_sem.at[6])
    load_precond = pltpu.make_async_copy(precond_ref, raw_precond, load_sem.at[7])
    for load in (
        load_mask,
        load_last,
        load_coupling,
        load_basis,
        load_table,
        load_wave,
        load_idle,
        load_precond,
    ):
        load.start()

    def message(source, target, send, recv, other):
        return pltpu.make_async_remote_copy(
            src_ref=source,
            dst_ref=target,
            send_sem=send_sem.at[send],
            recv_sem=recv_sem.at[recv],
            device_id={"azim": other},
            device_id_type=pl.DeviceIdType.MESH,
        )

    def send_all(phase, sources, targets):
        for step in range(1, n):
            other = peer(step)
            message(sources(other), targets.at[me], phase, phase, other).start()

    def all_of(phase, buffers):
        return message(
            buffers.at[pl.ds(0, n - 1)], buffers.at[pl.ds(0, n - 1)], phase, phase, core_peer
        )

    def wait_arrivals(phase, targets):
        all_of(phase, targets).wait_recv()

    def wait_sends(phase, sources):
        all_of(phase, sources).wait_send()

    def to_lanes(value):
        return jnp.concatenate([value[i * n : (i + 1) * n] for i in range(per)], axis=1)

    def to_rows(value):
        return jnp.concatenate(
            [value[:, i * width2 : (i + 1) * width2] for i in range(per)], axis=0
        )

    def order_basis(j):
        for part in range(2):
            basis_ref[j, :, part * width : (part + 1) * width] = raw_basis[j, :, part, :]

    load_mask.wait()
    masks[me] = jnp.zeros((1, 128), jnp.float32)
    masks[me, :, :cycles] = mask_ref[...].astype(jnp.float32)
    load_last.wait()
    order_basis(arnoldi - 1)
    current = basis_ref[arnoldi - 1].astype(jnp.bfloat16)
    for tile in range(lane_tiles):
        columns[me, tile * cycles : (tile + 1) * cycles, :] = current[
            :, tile * 128 : (tile + 1) * 128
        ]

    pl.semaphore_wait(barrier, n - 1)

    def pass_on(slot, other):
        message(columns.at[slot], columns.at[slot], GATHER, GATHER + slot, other).start()

    def arrived(slot):
        message(
            columns.at[slot], columns.at[slot], GATHER, GATHER + slot, core_peer
        ).wait_recv()

    def slot_of(far, plane):
        return (line ^ far) * 4 + plane

    plane = me & 3
    for far in (1, 3, 2):
        pass_on(me, slot_of(far, plane))
    pass_on(me, side_peer)
    pass_on(me, core_peer)
    send_all(MASKS, lambda other: masks.at[me], masks)

    rows = half * cycles
    padded = (cycles + 2 * reach) * half
    pick_row = lax.broadcasted_iota(jnp.int32, (padded, rows), 0)
    pick_lane = lax.broadcasted_iota(jnp.int32, (padded, rows), 1)
    pick_match = ((pick_row & (half - 1)) * cycles + (pick_row // half) - reach == pick_lane) & (
        (pick_row // half >= reach) & (pick_row // half < cycles + reach)
    )
    pick = jnp.where(pick_match, 1.0, 0.0).astype(jnp.bfloat16)

    load_basis.wait()
    for j in range(arnoldi - 1):
        order_basis(j)
    used = per * width2 // 128
    stored = basis_out.shape[1] // arnoldi
    for j in range(arnoldi):
        basis_out[:, j * stored : j * stored + used, :] = (
            to_lanes(basis_ref[j]).reshape(n, used, 128).astype(jnp.bfloat16)
        )

    distance = jnp.minimum(me, n - me)

    def build(offset):
        inside = jnp.where(distance <= band_ref[offset], 1.0, 0.0).astype(jnp.float32)
        keep = jnp.full((width, width), inside, jnp.float32).astype(jnp.bfloat16)
        real_part = raw_coupling[offset, 0] * keep
        imag_part = raw_coupling[offset, 1] * keep
        blocks[offset, :width, :width] = real_part
        blocks[offset, :width, width:] = imag_part
        blocks[offset, width:, :width] = -imag_part
        blocks[offset, width:, width:] = real_part

    load_coupling.wait()
    build(0)
    arrived(side_peer)
    pass_on(side_peer, core_peer)
    build(1)
    arrived(slot_of(1, plane))
    pass_on(slot_of(1, plane), side_peer)
    pass_on(slot_of(1, plane), core_peer)
    build(2)
    for far in (3, 2):
        arrived(slot_of(far, plane))
        pass_on(slot_of(far, plane), side_peer)
        pass_on(slot_of(far, plane), core_peer)
        build(6 - far)
    arrived(slot_of(1, plane ^ 2))
    pass_on(slot_of(1, plane ^ 2), core_peer)

    wait_arrivals(MASKS, masks)
    every_mask = masks[...].reshape(n, 128)
    turn_row = lax.broadcasted_iota(jnp.int32, (n, n), 0)
    turn_lane = lax.broadcasted_iota(jnp.int32, (n, n), 1)
    turn = jnp.where(((start + turn_row) & (n - 1)) == turn_lane, 1.0, 0.0).astype(jnp.bfloat16)
    turned_mask = jnp.dot(
        turn, every_mask.astype(jnp.bfloat16), preferred_element_type=jnp.float32
    )
    mask_lane = lax.broadcasted_iota(jnp.int32, (rows, 128), 1)
    mask_row = lax.broadcasted_iota(jnp.int32, (rows, 128), 0)
    load_wave.wait()
    load_idle.wait()

    def group_start(group):
        base = pl.multiple_of((own_half ^ group) * half, half)
        tiles = [
            columns[pl.ds(base, half), tile * cycles : (tile + 1) * cycles, :].reshape(rows, 128)
            for tile in range(lane_tiles)
        ]
        gathered = jnp.concatenate(tiles, axis=1)
        group_mask = masks[pl.ds(base, half)]
        spread = jnp.broadcast_to(group_mask, (half, cycles, 128)).reshape(rows, 128)
        active = jnp.sum(
            jnp.where(mask_lane == (mask_row & (cycles - 1)), spread, 0.0), axis=1, keepdims=True
        )
        driving = (gathered.astype(jnp.float32) * active).astype(jnp.bfloat16)
        picked = jnp.dot(pick, driving, preferred_element_type=jnp.float32)
        even_drive[group] = picked.astype(jnp.bfloat16)
        odd_drive[group] = picked[half : padded - half].astype(jnp.bfloat16)
        return (gathered - driving).astype(jnp.bfloat16)

    def group_source(group, offset):
        first = (2 * reach - offset) * half
        if offset % 2 == 0:
            return even_drive[group, first : first + rows]
        return odd_drive[group, first - half : first - half + rows]

    def group_product(group):
        return jnp.dot(
            jnp.concatenate([group_source(group, offset) for offset in range(offsets)], axis=1),
            blocks[...].reshape(offsets * width2, width2),
            preferred_element_type=jnp.float32,
        )

    def group_finish(group, applied):
        spread = jnp.broadcast_to(
            turned_mask[group * half : (group + 1) * half].reshape(1, half, 128),
            (cycles, half, 128),
        ).reshape(rows, 128)
        active = jnp.sum(
            jnp.where(mask_lane == (mask_row // half), spread, 0.0), axis=1, keepdims=True
        )
        return (applied * active).astype(jnp.bfloat16)

    def wave(masked, chunk):
        block = masked[chunk * CHUNK * half : (chunk + 1) * CHUNK * half]
        swapped = jnp.concatenate([block[:, width:], -block[:, :width]], axis=1)
        return jnp.dot(
            wave_ref[...],
            jnp.concatenate([block, swapped], axis=0),
            preferred_element_type=jnp.float32,
        )

    for far in (0, 1):
        arrived(slot_of(far, plane ^ 1))
        arrived(slot_of(far, plane ^ 3))
    idle_rows = group_start(0)
    applied = group_product(0)
    for far in (3, 2):
        arrived(slot_of(far, plane ^ 2))
        pass_on(slot_of(far, plane ^ 2), core_peer)
    masked = group_finish(0, applied)
    for chunk in range(chunks):
        early[chunk] = wave(masked, chunk)
    idle_modes = jnp.dot(
        idle_ref[:, :rows], idle_rows, preferred_element_type=jnp.float32
    )

    for far in (3, 2):
        arrived(slot_of(far, plane ^ 1))
        arrived(slot_of(far, plane ^ 3))
    send_all(BASIS, lambda other: basis_out.at[other], basis_in)
    basis_in[me] = basis_out[me]
    idle_rows = group_start(1)
    applied = group_product(1)
    masked = group_finish(1, applied)

    core_recv = GATHER + n
    side_recv = core_recv + chunks
    line_recv = side_recv + chunks * lines

    def to_core(chunk):
        return message(
            partial.at[1 - core, chunk], core_in.at[chunk], CORE, core_recv + chunk, core_peer
        )

    def to_side(chunk, target):
        return message(
            side_out.at[chunk, target],
            side_in.at[chunk, target],
            SIDE,
            side_recv + chunk * lines + target,
            side_peer,
        )

    def to_line(chunk, target):
        return message(
            line_out.at[chunk, target],
            line_in.at[chunk, line],
            LINE,
            line_recv + chunk,
            target * 4 + plane,
        )

    def from_lines(chunk):
        inner = line_in.at[chunk, pl.ds(0, lines - 1)]
        return message(inner, inner, LINE, line_recv + chunk, core_peer)

    mode_of_row = lax.broadcasted_iota(jnp.int32, (n * CHUNK, 1), 0) // CHUNK
    sign = jnp.where((mode_of_row & 1) == 0, 1.0, -1.0)
    for chunk in range(chunks):
        modes = (early[chunk] + sign * wave(masked, chunk)).astype(jnp.bfloat16)
        for mode in range(n):
            partial[mode & 1, chunk, mode >> 2, (mode >> 1) & 1] = modes[
                mode * CHUNK : (mode + 1) * CHUNK
            ]
        to_core(chunk).start()

    def core_sum(chunk, target, half_side):
        return partial[core, chunk, target, half_side].astype(jnp.float32) + core_in[
            chunk, target, half_side
        ].astype(jnp.float32)

    def fold_core(chunk, target):
        side_out[chunk, target] = core_sum(chunk, target, 1 - side).astype(jnp.bfloat16)
        to_side(chunk, target).start()

    def side_sum(chunk, target):
        return core_sum(chunk, target, side) + side_in[chunk, target].astype(jnp.float32)

    for chunk in range(chunks):
        to_core(chunk).wait_recv()
        for far in (3, 2):
            fold_core(chunk, line ^ far)
    for far in (1, 0):
        for chunk in range(chunks):
            fold_core(chunk, line ^ far)

    idle_modes = idle_modes + jnp.dot(
        idle_ref[:, rows:], idle_rows, preferred_element_type=jnp.float32
    )
    idle_cos = idle_modes[:cycles]
    idle_sin = idle_modes[cycles:]
    idle_field = jnp.concatenate(
        [
            idle_cos[:, :width] + idle_sin[:, width:],
            idle_cos[:, width:] - idle_sin[:, :width],
        ],
        axis=1,
    )
    load_precond.wait()
    load_table.wait()
    real_part = raw_precond[0].astype(jnp.bfloat16)
    imag_part = raw_precond[1].astype(jnp.bfloat16)
    solver[:width, :width] = real_part
    solver[:width, width:] = imag_part
    solver[width:, :width] = -imag_part
    solver[width:, width:] = real_part

    for chunk, far in [(c, f) for fars in ((3, 2), (1,)) for c in range(chunks) for f in fars]:
        target = line ^ far
        to_side(chunk, target).wait_recv()
        line_out[chunk, target] = side_sum(chunk, target).astype(jnp.bfloat16)
        to_line(chunk, target).start()

    small_lane = lax.broadcasted_iota(jnp.int32, (1, 128), 1)

    def place(total, index, value):
        return total + jnp.where(small_lane == index, value, 0.0)

    def full_sum(value):
        return jnp.sum(jnp.sum(value, axis=0, keepdims=True), axis=1, keepdims=True)

    packed = jnp.zeros((1, 128), jnp.float32)
    gram_slots = []
    slot = 2 * arnoldi + 1
    for i in range(arnoldi):
        for j in range(i, arnoldi):
            left_real = basis_ref[i, :, :width]
            left_imag = basis_ref[i, :, width:]
            right_real = basis_ref[j, :, :width]
            right_imag = basis_ref[j, :, width:]
            packed = place(packed, slot, full_sum(left_real * right_real + left_imag * right_imag))
            if i == j:
                gram_slots.append((i, j, slot, None))
                slot += 1
            else:
                packed = place(
                    packed, slot + 1, full_sum(left_real * right_imag - left_imag * right_real)
                )
                gram_slots.append((i, j, slot, slot + 1))
                slot += 2

    spectrum_chunks = []
    for chunk in range(chunks):
        to_side(chunk, line).wait_recv()
        spectrum = side_sum(chunk, line)
        from_lines(chunk).wait_recv()
        for far in (1, 3, 2):
            spectrum = spectrum + line_in[chunk, line ^ far].astype(jnp.float32)
        spectrum_chunks.append(spectrum)
    spectrum = jnp.concatenate(spectrum_chunks, axis=0) + idle_field

    def azimuth_transform(value):
        both = jnp.dot(
            table_ref[...],
            value,
            preferred_element_type=jnp.float32,
            precision=lax.Precision.HIGHEST,
        )
        cosine = both[:n]
        sine = both[n:]
        outs = []
        for i in range(per):
            real = slice(i * width2, i * width2 + width)
            imag = slice(i * width2 + width, (i + 1) * width2)
            outs.append((cosine[:, real] - sine[:, imag]) * (1.0 / n))
            outs.append((cosine[:, imag] + sine[:, real]) * (1.0 / n))
        return jnp.concatenate(outs, axis=1)

    def exchange(phase, value, out_buffer, in_buffer, meanwhile):
        out_buffer[:, :used, :] = value.reshape(n, used, 128).astype(jnp.bfloat16)
        send_all(phase, lambda other: out_buffer.at[other], in_buffer)
        in_buffer[me] = out_buffer[me]
        meanwhile()
        wait_arrivals(phase, in_buffer)
        return in_buffer[:, :used, :].astype(jnp.float32).reshape(n, used * 128)

    solved = jnp.dot(
        spectrum.astype(jnp.bfloat16), solver[...], preferred_element_type=jnp.float32
    )
    def spread_basis():
        wait_arrivals(BASIS, basis_in)
        for j in range(arnoldi):
            spread_ref[j] = (
                basis_in[:, j * stored : j * stored + used, :]
                .astype(jnp.float32)
                .reshape(n, used * 128)
            )

    pieces = exchange(BACK, to_lanes(solved), back_out, back_in, spread_basis)
    field = azimuth_transform(pieces)
    packed = place(packed, 2 * arnoldi, full_sum(field * field))
    turned = jnp.concatenate(
        [
            part
            for i in range(per)
            for part in (
                field[:, i * width2 + width : (i + 1) * width2],
                -field[:, i * width2 : i * width2 + width],
            )
        ],
        axis=1,
    )
    for j in range(arnoldi):
        vector = spread_ref[j]
        packed = place(packed, j, full_sum(vector * field))
        packed = place(packed, arnoldi + j, full_sum(vector * turned))
    head = packed.astype(jnp.bfloat16)
    rest = packed - head.astype(jnp.float32)
    middle = rest.astype(jnp.bfloat16)
    last = (rest - middle.astype(jnp.float32)).astype(jnp.bfloat16)
    field_out[:, :used, :] = field.reshape(n, used, 128).astype(jnp.bfloat16)
    for part, value in enumerate((head, middle, last)):
        field_out[:, used + part : used + part + 1, :] = jnp.broadcast_to(
            value.reshape(1, 1, 128), (n, 1, 128)
        )
    send_all(FIELD, lambda other: field_out.at[other], field_in)
    field_in[me] = field_out[me]
    wait_arrivals(FIELD, field_in)
    result = to_rows(field_in[:, :used, :].astype(jnp.float32).reshape(n, used * 128))
    result_real = result[:, :width]
    result_imag = result[:, width:]
    parts = jnp.sum(field_in[:, used : used + 3, :].astype(jnp.float32), axis=0)
    total = parts[0:1] + parts[1:2] + parts[2:3]
    total = total * (1.0 / elements)

    def entry(index):
        return total[:, index : index + 1]

    project_real = [entry(j) for j in range(arnoldi)]
    project_imag = [entry(arnoldi + j) for j in range(arnoldi)]
    norm_square = entry(2 * arnoldi)
    for j in range(arnoldi):
        norm_square = norm_square - 2.0 * (
            project_real[j] * project_real[j] + project_imag[j] * project_imag[j]
        )
    for i, j, real_slot, imag_slot in gram_slots:
        cross_real = project_real[i] * project_real[j] + project_imag[i] * project_imag[j]
        if i == j:
            norm_square = norm_square + cross_real * entry(real_slot)
        else:
            cross_imag = project_real[i] * project_imag[j] - project_imag[i] * project_real[j]
            norm_square = norm_square + 2.0 * (
                cross_real * entry(real_slot) - cross_imag * entry(imag_slot)
            )
    scale_norm = jnp.sqrt(jnp.maximum(norm_square, 0.0) + 1e-06)
    remainder_real = result_real
    remainder_imag = result_imag
    for j in range(arnoldi):
        basis_real = basis_ref[j, :, :width]
        basis_imag = basis_ref[j, :, width:]
        remainder_real = remainder_real - (
            project_real[j] * basis_real - project_imag[j] * basis_imag
        )
        remainder_imag = remainder_imag - (
            project_real[j] * basis_imag + project_imag[j] * basis_real
        )
    out_ref[:, 0, :] = remainder_real / scale_norm
    out_ref[:, 1, :] = remainder_imag / scale_norm
    first = jnp.zeros((1, 128), jnp.float32)
    second = jnp.zeros((1, 128), jnp.float32)
    for j in range(arnoldi):
        first = place(first, j, project_real[j])
        second = place(second, j, project_imag[j])
    first = place(first, arnoldi, scale_norm)
    hess_ref[0:1] = first[:, : arnoldi + 1]
    hess_ref[1:2] = second[:, : arnoldi + 1]

    wait_sends(GATHER, columns)
    message(partial.at[0], partial.at[0], CORE, core_recv, core_peer).wait_send()
    message(side_out, side_out, SIDE, side_recv, side_peer).wait_send()
    sent = line_out.at[:, pl.ds(0, lines - 1)]
    message(sent, sent, LINE, line_recv, core_peer).wait_send()
    wait_sends(MASKS, masks)
    wait_sends(BACK, back_out)
    wait_sends(FIELD, field_out)
    wait_sends(BASIS, basis_out)


def hand_over(vector_ref, column_ref, out_ref, hess_ref):
    out_ref[0] = vector_ref[...]
    hess_ref[...] = column_ref[...]


def fused_body(coupling, band, precond, basis, mask):
    n = lax.axis_size("azim")
    arnoldi, _, cycles, _, width = basis.shape
    offsets = coupling.shape[1]
    reach = offsets // 2
    per = cycles // n
    half = n // 2
    chunks = cycles // CHUNK
    width2 = 2 * width
    vmem = pl.BlockSpec(memory_space=pltpu.VMEM)
    anywhere = pl.BlockSpec(memory_space=pl.ANY)
    lines = n // 4
    message_rows = -(-(per * width2 // 128 + 3) // 16) * 16
    message = pltpu.VMEM((n, message_rows, 128), jnp.bfloat16)
    waves = jnp.asarray(wave_constants(n, CHUNK))
    idles = jnp.asarray(idle_constants(n, cycles))
    vector, column = pl.pallas_call(
        functools.partial(step_kernel, n, cycles, reach),
        out_shape=(
            jax.ShapeDtypeStruct((cycles, 2, width), jnp.float32),
            jax.ShapeDtypeStruct((2, arnoldi + 1), jnp.float32),
        ),
        in_specs=[pl.BlockSpec(memory_space=pltpu.SMEM)] + [anywhere] * 7,
        out_specs=(vmem, vmem),
        scratch_shapes=[
            pltpu.VMEM(mask.shape, mask.dtype),
            pltpu.VMEM((arnoldi, cycles, 2, width), basis.dtype),
            pltpu.VMEM((arnoldi, cycles, width2), basis.dtype),
            pltpu.VMEM((2 * n, n), jnp.float32),
            pltpu.VMEM(waves.shape[1:], waves.dtype),
            pltpu.VMEM(idles.shape[1:], idles.dtype),
            pltpu.VMEM(coupling.shape[1:], coupling.dtype),
            pltpu.VMEM(precond.shape[1:], precond.dtype),
            pltpu.VMEM((offsets, width2, width2), jnp.bfloat16),
            pltpu.VMEM((width2, width2), jnp.bfloat16),
            pltpu.VMEM((n, width2 // 128 * cycles, 128), jnp.bfloat16),
            pltpu.VMEM((n, 1, 128), jnp.float32),
            pltpu.VMEM((2, (cycles + 2 * reach) * half, width2), jnp.bfloat16),
            pltpu.VMEM((2, (cycles + 2 * reach - 2) * half, width2), jnp.bfloat16),
            pltpu.VMEM((chunks, n * CHUNK, width2), jnp.float32),
            pltpu.VMEM((2, chunks, lines, 2, CHUNK, width2), jnp.bfloat16),
            pltpu.VMEM((chunks, lines, 2, CHUNK, width2), jnp.bfloat16),
            pltpu.VMEM((chunks, lines, CHUNK, width2), jnp.bfloat16),
            pltpu.VMEM((chunks, lines, CHUNK, width2), jnp.bfloat16),
            pltpu.VMEM((chunks, lines, CHUNK, width2), jnp.bfloat16),
            pltpu.VMEM((chunks, lines, CHUNK, width2), jnp.bfloat16),
            message,
            message,
            message,
            message,
            pltpu.VMEM((n, arnoldi * message_rows, 128), jnp.bfloat16),
            pltpu.VMEM((n, arnoldi * message_rows, 128), jnp.bfloat16),
            pltpu.VMEM((arnoldi, n, per * width2), jnp.float32),
            pltpu.SemaphoreType.DMA((8,)),
            pltpu.SemaphoreType.DMA((8,)),
            pltpu.SemaphoreType.DMA((GATHER + n + chunks * (lines + 2),)),
        ],
        compiler_params=pltpu.CompilerParams(
            collective_id=0, has_side_effects=True, vmem_limit_bytes=60 * 1024 * 1024
        ),
    )(
        band,
        mask,
        basis[:, 0],
        jnp.asarray(fourier_constants(n)),
        waves,
        idles,
        coupling[0],
        precond[0],
    )
    return pl.pallas_call(
        hand_over,
        out_shape=(
            jax.ShapeDtypeStruct((1,) + vector.shape, vector.dtype),
            jax.ShapeDtypeStruct(column.shape, column.dtype),
        ),
        in_specs=[vmem, vmem],
        out_specs=(vmem, vmem),
    )(vector, column)


def body(coupling, band, precond, basis, mask):
    n = lax.axis_size("azim")
    cycles = basis.shape[2]
    width = basis.shape[4]
    if n == 16 and cycles == 32 and width % 128 == 0:
        return fused_body(coupling, band, precond, basis, mask)
    return plain_body(coupling, band, precond, basis, mask)


def solution(mesh):
    return jax.shard_map(
        body,
        mesh=mesh,
        in_specs=(
            P("azim", "freq", None, None, None),
            P("freq"),
            P("azim", "freq", None, None),
            P("freq", "azim", None, None, None),
            P("azim", None),
        ),
        out_specs=(P("azim", "freq", None, None), P("freq", None)),
        check_vma=False,
    )
```

```python
import functools

import jax
import jax.numpy as jnp
import numpy as np
from jax import lax
from jax.experimental import pallas as pl
from jax.experimental.pallas import tpu as pltpu
from jax.sharding import PartitionSpec as P


def fourier_tables(azimuths):
    azimuth_steps = jnp.arange(azimuths, dtype=jnp.int32)
    phase_index = azimuth_steps[:, None] * azimuth_steps[None, :] % azimuths
    angles = phase_index.astype(jnp.float32) * (2.0 * jnp.pi / azimuths)
    return (jnp.cos(angles), jnp.sin(angles))


def transform(real_part, imag_part, cosine_table, sine_table, inverse):
    highest_accuracy = lax.Precision.HIGHEST
    cos_real = jnp.tensordot(cosine_table, real_part, axes=1, precision=highest_accuracy)
    cos_imag = jnp.tensordot(cosine_table, imag_part, axes=1, precision=highest_accuracy)
    sin_real = jnp.tensordot(sine_table, real_part, axes=1, precision=highest_accuracy)
    sin_imag = jnp.tensordot(sine_table, imag_part, axes=1, precision=highest_accuracy)
    if inverse:
        scaling = 1.0 / cosine_table.shape[0]
        return ((cos_real - sin_imag) * scaling, (cos_imag + sin_real) * scaling)
    return (cos_real + sin_imag, cos_imag - sin_real)


def block_matrix(matrix):
    real_part = matrix[..., 0, :, :]
    imag_part = matrix[..., 1, :, :]
    upper = jnp.concatenate([real_part, imag_part], axis=-1)
    lower = jnp.concatenate([-imag_part, real_part], axis=-1)
    return jnp.concatenate([upper, lower], axis=-2)


def cycle_coupling(column_rows, blocks):
    row_total, cycle_count, parts, basis_width = column_rows.shape
    cycle_reach = blocks.shape[0] // 2
    flattened = column_rows.reshape(row_total, cycle_count, parts * basis_width)
    padded = jnp.pad(flattened, ((0, 0), (cycle_reach, cycle_reach), (0, 0)))
    summed = jnp.zeros((row_total * cycle_count, parts * basis_width), jnp.float32)
    for offset in range(blocks.shape[0]):
        shifted = padded[:, 2 * cycle_reach - offset : 2 * cycle_reach - offset + cycle_count]
        summed = summed + jnp.dot(
            shifted.reshape(row_total * cycle_count, parts * basis_width),
            blocks[offset],
            preferred_element_type=jnp.float32,
            precision=None,
        )
    return summed.reshape(row_total, cycle_count, parts, basis_width)


def relayout(field, cosine_table, sine_table, send_out, send_back, inverse):
    azimuths = cosine_table.shape[0]
    cycle_count = field.shape[1]
    basis_width = field.shape[3]
    piece_width = cycle_count * basis_width // azimuths
    split_parts = jnp.transpose(field[0], (1, 0, 2)).reshape(2, azimuths, piece_width)
    pieces = jnp.transpose(split_parts, (1, 0, 2)).reshape(azimuths, 2 * piece_width)
    spread = send_out(pieces).reshape(azimuths, 2, piece_width)
    real_part, imag_part = transform(spread[:, 0], spread[:, 1], cosine_table, sine_table, inverse)
    joined = jnp.stack([real_part, imag_part], axis=1).reshape(azimuths, 2 * piece_width)
    returned = send_back(joined).reshape(azimuths, 2, piece_width)
    whole = jnp.transpose(returned, (1, 0, 2)).reshape(2, cycle_count, basis_width)
    return jnp.transpose(whole, (1, 0, 2))[None]


def plain_body(coupling, band, precond, basis, mask):
    highest_accuracy = lax.Precision.HIGHEST
    azimuths = lax.axis_size("azim")
    position = lax.axis_index("azim")
    cosine_table, sine_table = fourier_tables(azimuths)
    vectors = basis[:, 0]
    arnoldi_count = vectors.shape[0]
    cycle_count = vectors.shape[1]
    basis_width = vectors.shape[3]
    current = vectors[arnoldi_count - 1][None]
    active = mask.astype(jnp.float32)[:, :, None, None]
    driving = (active * current).astype(jnp.bfloat16)
    distance = jnp.minimum(position, azimuths - position)
    inside = (distance <= band).astype(coupling.dtype)
    kernel = coupling[0] * inside[:, None, None, None]
    blocks = block_matrix(kernel)
    gathered = lax.all_gather(driving, "azim", axis=0, tiled=True)
    aligned = jnp.roll(gathered, position, axis=0)
    applied = lax.psum_scatter(
        cycle_coupling(aligned, blocks), "azim", scatter_dimension=0, tiled=True
    )
    driven = active * applied + (1.0 - active) * current
    spectrum = relayout(
        driven,
        cosine_table,
        sine_table,
        lambda tensor: lax.all_to_all(
            tensor.astype(jnp.bfloat16), "azim", split_axis=0, concat_axis=0, tiled=True
        ).astype(tensor.dtype),
        lambda tensor: lax.all_to_all(
            tensor.astype(jnp.bfloat16), "azim", split_axis=0, concat_axis=0, tiled=True
        ).astype(tensor.dtype),
        False,
    )
    precond_blocks = block_matrix(precond[0])
    solved = jnp.dot(
        spectrum.reshape(cycle_count, 2 * basis_width),
        precond_blocks,
        preferred_element_type=jnp.float32,
        precision=highest_accuracy,
    )
    solved = solved.reshape(1, cycle_count, 2, basis_width)
    result = relayout(
        solved,
        cosine_table,
        sine_table,
        lambda tensor: lax.all_to_all(
            tensor.astype(jnp.bfloat16), "azim", split_axis=0, concat_axis=0, tiled=True
        ).astype(tensor.dtype),
        lambda tensor: lax.all_to_all(
            tensor.astype(jnp.bfloat16), "azim", split_axis=0, concat_axis=0, tiled=True
        ).astype(tensor.dtype),
        True,
    )
    elements = float(azimuths * cycle_count * basis_width)
    basis_real = vectors[:, :, 0]
    basis_imag = vectors[:, :, 1]
    result_real = result[0, :, 0]
    result_imag = result[0, :, 1]
    local_real = jnp.sum(
        basis_real * result_real[None] + basis_imag * result_imag[None], axis=(1, 2)
    )
    local_imag = jnp.sum(
        basis_real * result_imag[None] - basis_imag * result_real[None], axis=(1, 2)
    )
    sum_real, sum_imag = lax.psum((local_real, local_imag), "azim")
    project_real = sum_real / elements
    project_imag = sum_imag / elements
    coef_real = project_real[:, None, None]
    coef_imag = project_imag[:, None, None]
    remainder_real = result_real - jnp.sum(coef_real * basis_real - coef_imag * basis_imag, axis=0)
    remainder_imag = result_imag - jnp.sum(coef_real * basis_imag + coef_imag * basis_real, axis=0)
    norm_square = (
        lax.psum(jnp.sum(remainder_real * remainder_real + remainder_imag * remainder_imag), "azim")
        / elements
    )
    scale_norm = jnp.sqrt(norm_square + 1e-06)
    new_vector = (jnp.stack([remainder_real, remainder_imag], axis=1) / scale_norm)[None]
    hessenberg_column = jnp.stack(
        [
            jnp.concatenate([project_real, scale_norm[None]]),
            jnp.concatenate([project_imag, jnp.zeros((1,), jnp.float32)]),
        ]
    )
    return (new_vector, hessenberg_column)


def fourier_constants(azimuths):
    steps = np.arange(azimuths)
    angles = (steps[:, None] * steps[None, :] % azimuths) * (2.0 * np.pi / azimuths)
    table = np.concatenate([np.cos(angles), np.sin(angles)], axis=0)
    return (table / TABLE_SCALE).astype(np.float32)


TABLE_SCALE = 1.1328025


def wave_constants(azimuths, chunk):
    half = azimuths // 2
    start = np.arange(azimuths)[:, None, None, None, None, None]
    mode = np.arange(azimuths)[None, :, None, None, None, None]
    out_cycle = np.arange(chunk)[None, None, :, None, None, None]
    part = np.arange(2)[None, None, None, :, None, None]
    in_cycle = np.arange(chunk)[None, None, None, None, :, None]
    step = np.arange(half)[None, None, None, None, None, :]
    angle = (mode * (start + step) % azimuths) * (2.0 * np.pi / azimuths)
    value = np.where(part == 0, np.cos(angle), np.sin(angle)) * (out_cycle == in_cycle)
    value = value * TABLE_SCALE
    return value.reshape(azimuths, azimuths * chunk, 2 * chunk * half).astype(jnp.bfloat16)


def idle_constants(azimuths, cycles):
    half = azimuths // 2
    mode = np.arange(azimuths)[:, None, None, None, None, None]
    part = np.arange(2)[None, :, None, None, None, None]
    out_cycle = np.arange(cycles)[None, None, :, None, None, None]
    group = np.arange(2)[None, None, None, :, None, None]
    step = np.arange(half)[None, None, None, None, :, None]
    in_cycle = np.arange(cycles)[None, None, None, None, None, :]
    column = ((mode // half) ^ group) * half + step
    angle = (mode * column % azimuths) * (2.0 * np.pi / azimuths)
    value = np.where(part == 0, np.cos(angle), np.sin(angle)) * (out_cycle == in_cycle)
    value = value * TABLE_SCALE
    return value.reshape(azimuths, 2 * cycles, azimuths * cycles).astype(jnp.bfloat16)


CHUNK = 16
MASKS, BACK, FIELD, BASIS, GATHER, CORE, SIDE, LINE = range(8)


def step_kernel(
    n,
    cycles,
    reach,
    band_ref,
    mask_any,
    basis_any,
    table_any,
    wave_any,
    idle_any,
    coupling_ref,
    precond_ref,
    out_ref,
    hess_ref,
    mask_ref,
    raw_basis,
    basis_ref,
    table_ref,
    wave_ref,
    idle_ref,
    raw_coupling,
    raw_precond,
    blocks,
    solver,
    columns,
    masks,
    even_drive,
    odd_drive,
    early,
    partial,
    core_in,
    side_out,
    side_in,
    line_out,
    line_in,
    back_out,
    back_in,
    field_out,
    field_in,
    basis_out,
    basis_in,
    spread_ref,
    load_sem,
    send_sem,
    recv_sem,
):
    arnoldi = basis_ref.shape[0]
    width2 = basis_ref.shape[2]
    width = width2 // 2
    lane_tiles = width2 // 128
    offsets = 2 * reach + 1
    per = cycles // n
    half = n // 2
    chunks = cycles // CHUNK
    elements = float(n * cycles * width)
    me = lax.axis_index("azim")
    core = me & 1
    side = (me >> 1) & 1
    line = me >> 2
    lines = n // 4
    core_peer = me ^ 1
    side_peer = me ^ 2
    own_half = me >> 3

    def peer(step):
        return me ^ (n - step)

    barrier = pltpu.get_barrier_semaphore()
    for step in range(1, n):
        pl.semaphore_signal(
            barrier, inc=1, device_id={"azim": peer(step)}, device_id_type=pl.DeviceIdType.MESH
        )

    load_mask = pltpu.make_async_copy(mask_any, mask_ref, load_sem.at[0])
    load_last = pltpu.make_async_copy(
        basis_any.at[pl.ds(arnoldi - 1, 1)], raw_basis.at[pl.ds(arnoldi - 1, 1)], load_sem.at[1]
    )
    load_basis = pltpu.make_async_copy(
        basis_any.at[pl.ds(0, arnoldi - 1)], raw_basis.at[pl.ds(0, arnoldi - 1)], load_sem.at[2]
    )
    load_coupling = pltpu.make_async_copy(coupling_ref, raw_coupling, load_sem.at[3])
    load_table = pltpu.make_async_copy(table_any, table_ref, load_sem.at[4])
    start = (own_half * half + me) & (n - 1)
    load_wave = pltpu.make_async_copy(wave_any.at[start], wave_ref, load_sem.at[5])
    load_idle = pltpu.make_async_copy(idle_any.at[me], idle_ref, load_sem.at[6])
    load_precond = pltpu.make_async_copy(precond_ref, raw_precond, load_sem.at[7])
    for load in (
        load_mask,
        load_last,
        load_coupling,
        load_basis,
        load_table,
        load_wave,
        load_idle,
        load_precond,
    ):
        load.start()

    def message(source, target, send, recv, other):
        return pltpu.make_async_remote_copy(
            src_ref=source,
            dst_ref=target,
            send_sem=send_sem.at[send],
            recv_sem=recv_sem.at[recv],
            device_id={"azim": other},
            device_id_type=pl.DeviceIdType.MESH,
        )

    def send_all(phase, sources, targets):
        for step in range(1, n):
            other = peer(step)
            message(sources(other), targets.at[me], phase, phase, other).start()

    def all_of(phase, buffers):
        return message(
            buffers.at[pl.ds(0, n - 1)], buffers.at[pl.ds(0, n - 1)], phase, phase, core_peer
        )

    def wait_arrivals(phase, targets):
        all_of(phase, targets).wait_recv()

    def wait_sends(phase, sources):
        all_of(phase, sources).wait_send()

    def to_lanes(value):
        return jnp.concatenate([value[i * n : (i + 1) * n] for i in range(per)], axis=1)

    def to_rows(value):
        return jnp.concatenate(
            [value[:, i * width2 : (i + 1) * width2] for i in range(per)], axis=0
        )

    def order_basis(j):
        for part in range(2):
            basis_ref[j, :, part * width : (part + 1) * width] = raw_basis[j, :, part, :]

    load_mask.wait()
    masks[me] = jnp.zeros((1, 128), jnp.float32)
    masks[me, :, :cycles] = mask_ref[...].astype(jnp.float32)
    load_last.wait()
    order_basis(arnoldi - 1)
    current = basis_ref[arnoldi - 1].astype(jnp.bfloat16)
    for tile in range(lane_tiles):
        columns[me, tile * cycles : (tile + 1) * cycles, :] = current[
            :, tile * 128 : (tile + 1) * 128
        ]

    pl.semaphore_wait(barrier, n - 1)

    def pass_on(slot, other):
        message(columns.at[slot], columns.at[slot], GATHER, GATHER + slot, other).start()

    def arrived(slot):
        message(
            columns.at[slot], columns.at[slot], GATHER, GATHER + slot, core_peer
        ).wait_recv()

    def slot_of(far, plane):
        return (line ^ far) * 4 + plane

    plane = me & 3
    for far in (1, 3, 2):
        pass_on(me, slot_of(far, plane))
    pass_on(me, side_peer)
    pass_on(me, core_peer)
    send_all(MASKS, lambda other: masks.at[me], masks)

    rows = half * cycles
    padded = (cycles + 2 * reach) * half
    pick_row = lax.broadcasted_iota(jnp.int32, (padded, rows), 0)
    pick_lane = lax.broadcasted_iota(jnp.int32, (padded, rows), 1)
    pick_match = ((pick_row & (half - 1)) * cycles + (pick_row // half) - reach == pick_lane) & (
        (pick_row // half >= reach) & (pick_row // half < cycles + reach)
    )
    pick = jnp.where(pick_match, 1.0, 0.0).astype(jnp.bfloat16)

    load_basis.wait()
    for j in range(arnoldi - 1):
        order_basis(j)
    used = per * width2 // 128
    stored = basis_out.shape[1] // arnoldi
    for j in range(arnoldi):
        basis_out[:, j * stored : j * stored + used, :] = (
            to_lanes(basis_ref[j]).reshape(n, used, 128).astype(jnp.bfloat16)
        )

    distance = jnp.minimum(me, n - me)

    def build(offset):
        inside = jnp.where(distance <= band_ref[offset], 1.0, 0.0).astype(jnp.float32)
        keep = jnp.full((width, width), inside, jnp.float32).astype(jnp.bfloat16)
        real_part = raw_coupling[offset, 0] * keep
        imag_part = raw_coupling[offset, 1] * keep
        blocks[offset, :width, :width] = real_part
        blocks[offset, :width, width:] = imag_part
        blocks[offset, width:, :width] = -imag_part
        blocks[offset, width:, width:] = real_part

    load_coupling.wait()
    build(0)
    arrived(side_peer)
    pass_on(side_peer, core_peer)
    build(1)
    arrived(slot_of(1, plane))
    pass_on(slot_of(1, plane), side_peer)
    pass_on(slot_of(1, plane), core_peer)
    build(2)
    for far in (3, 2):
        arrived(slot_of(far, plane))
        pass_on(slot_of(far, plane), side_peer)
        pass_on(slot_of(far, plane), core_peer)
        build(6 - far)
    arrived(slot_of(1, plane ^ 2))
    pass_on(slot_of(1, plane ^ 2), core_peer)

    wait_arrivals(MASKS, masks)
    every_mask = masks[...].reshape(n, 128)
    turn_row = lax.broadcasted_iota(jnp.int32, (n, n), 0)
    turn_lane = lax.broadcasted_iota(jnp.int32, (n, n), 1)
    turn = jnp.where(((start + turn_row) & (n - 1)) == turn_lane, 1.0, 0.0).astype(jnp.bfloat16)
    turned_mask = jnp.dot(
        turn, every_mask.astype(jnp.bfloat16), preferred_element_type=jnp.float32
    )
    mask_lane = lax.broadcasted_iota(jnp.int32, (rows, 128), 1)
    mask_row = lax.broadcasted_iota(jnp.int32, (rows, 128), 0)
    load_wave.wait()
    load_idle.wait()

    def group_start(group):
        base = pl.multiple_of((own_half ^ group) * half, half)
        tiles = [
            columns[pl.ds(base, half), tile * cycles : (tile + 1) * cycles, :].reshape(rows, 128)
            for tile in range(lane_tiles)
        ]
        gathered = jnp.concatenate(tiles, axis=1)
        group_mask = masks[pl.ds(base, half)]
        spread = jnp.broadcast_to(group_mask, (half, cycles, 128)).reshape(rows, 128)
        active = jnp.sum(
            jnp.where(mask_lane == (mask_row & (cycles - 1)), spread, 0.0), axis=1, keepdims=True
        )
        driving = (gathered.astype(jnp.float32) * active).astype(jnp.bfloat16)
        picked = jnp.dot(pick, driving, preferred_element_type=jnp.float32)
        even_drive[group] = picked.astype(jnp.bfloat16)
        odd_drive[group] = picked[half : padded - half].astype(jnp.bfloat16)
        return (gathered - driving).astype(jnp.bfloat16)

    def group_source(group, offset):
        first = (2 * reach - offset) * half
        if offset % 2 == 0:
            return even_drive[group, first : first + rows]
        return odd_drive[group, first - half : first - half + rows]

    def group_product(group):
        source = jnp.concatenate(
            [group_source(group, offset) for offset in range(offsets)], axis=1
        )
        return jnp.concatenate(
            [
                jnp.dot(
                    source[at : at + 128],
                    blocks[...].reshape(offsets * width2, width2),
                    preferred_element_type=jnp.float32,
                )
                for at in range(0, rows, 128)
            ],
            axis=0,
        )

    def group_finish(group, applied):
        spread = jnp.broadcast_to(
            turned_mask[group * half : (group + 1) * half].reshape(1, half, 128),
            (cycles, half, 128),
        ).reshape(rows, 128)
        active = jnp.sum(
            jnp.where(mask_lane == (mask_row // half), spread, 0.0), axis=1, keepdims=True
        )
        return (applied * active).astype(jnp.bfloat16)

    def wave(masked, chunk):
        block = masked[chunk * CHUNK * half : (chunk + 1) * CHUNK * half]
        swapped = jnp.concatenate([block[:, width:], -block[:, :width]], axis=1)
        return jnp.dot(
            wave_ref[...],
            jnp.concatenate([block, swapped], axis=0),
            preferred_element_type=jnp.float32,
        )

    for far in (0, 1):
        arrived(slot_of(far, plane ^ 1))
        arrived(slot_of(far, plane ^ 3))
    idle_rows = group_start(0)
    applied = group_product(0)
    for far in (3, 2):
        arrived(slot_of(far, plane ^ 2))
        pass_on(slot_of(far, plane ^ 2), core_peer)
    masked = group_finish(0, applied)
    for chunk in range(chunks):
        early[chunk] = wave(masked, chunk)
    idle_modes = jnp.dot(
        idle_ref[:, :rows], idle_rows, preferred_element_type=jnp.float32
    )

    for far in (3, 2):
        arrived(slot_of(far, plane ^ 1))
        arrived(slot_of(far, plane ^ 3))
    send_all(BASIS, lambda other: basis_out.at[other], basis_in)
    basis_in[me] = basis_out[me]
    idle_rows = group_start(1)
    applied = group_product(1)
    masked = group_finish(1, applied)

    core_recv = GATHER + n
    side_recv = core_recv + chunks
    line_recv = side_recv + chunks * lines

    def to_core(chunk):
        return message(
            partial.at[1 - core, chunk], core_in.at[chunk], CORE, core_recv + chunk, core_peer
        )

    def to_side(chunk, target):
        return message(
            side_out.at[chunk, target],
            side_in.at[chunk, target],
            SIDE,
            side_recv + chunk * lines + target,
            side_peer,
        )

    def to_line(chunk, target):
        return message(
            line_out.at[chunk, target],
            line_in.at[chunk, line],
            LINE,
            line_recv + chunk,
            target * 4 + plane,
        )

    def from_lines(chunk):
        inner = line_in.at[chunk, pl.ds(0, lines - 1)]
        return message(inner, inner, LINE, line_recv + chunk, core_peer)

    mode_of_row = lax.broadcasted_iota(jnp.int32, (n * CHUNK, 1), 0) // CHUNK
    sign = jnp.where((mode_of_row & 1) == 0, 1.0, -1.0)
    for chunk in range(chunks):
        modes = (early[chunk] + sign * wave(masked, chunk)).astype(jnp.bfloat16)
        for mode in range(n):
            partial[mode & 1, chunk, mode >> 2, (mode >> 1) & 1] = modes[
                mode * CHUNK : (mode + 1) * CHUNK
            ]
        to_core(chunk).start()

    def core_sum(chunk, target, half_side):
        return partial[core, chunk, target, half_side].astype(jnp.float32) + core_in[
            chunk, target, half_side
        ].astype(jnp.float32)

    def fold_core(chunk, target):
        side_out[chunk, target] = core_sum(chunk, target, 1 - side).astype(jnp.bfloat16)
        to_side(chunk, target).start()

    def side_sum(chunk, target):
        return core_sum(chunk, target, side) + side_in[chunk, target].astype(jnp.float32)

    for chunk in range(chunks):
        to_core(chunk).wait_recv()
        for far in (3, 2):
            fold_core(chunk, line ^ far)
    for far in (1, 0):
        for chunk in range(chunks):
            fold_core(chunk, line ^ far)

    idle_modes = idle_modes + jnp.dot(
        idle_ref[:, rows:], idle_rows, preferred_element_type=jnp.float32
    )
    idle_cos = idle_modes[:cycles]
    idle_sin = idle_modes[cycles:]
    idle_field = jnp.concatenate(
        [
            idle_cos[:, :width] + idle_sin[:, width:],
            idle_cos[:, width:] - idle_sin[:, :width],
        ],
        axis=1,
    )
    load_precond.wait()
    load_table.wait()
    real_part = raw_precond[0].astype(jnp.bfloat16)
    imag_part = raw_precond[1].astype(jnp.bfloat16)
    solver[:width, :width] = real_part
    solver[:width, width:] = imag_part
    solver[width:, :width] = -imag_part
    solver[width:, width:] = real_part

    for chunk, far in [(c, f) for fars in ((3, 2), (1,)) for c in range(chunks) for f in fars]:
        target = line ^ far
        to_side(chunk, target).wait_recv()
        line_out[chunk, target] = side_sum(chunk, target).astype(jnp.bfloat16)
        to_line(chunk, target).start()

    small_lane = lax.broadcasted_iota(jnp.int32, (1, 128), 1)

    def place(total, index, value):
        return total + jnp.where(small_lane == index, value, 0.0)

    def full_sum(value):
        return jnp.sum(jnp.sum(value, axis=0, keepdims=True), axis=1, keepdims=True)

    packed = jnp.zeros((1, 128), jnp.float32)
    gram_slots = []
    slot = 2 * arnoldi + 1
    for i in range(arnoldi):
        for j in range(i, arnoldi):
            left_real = basis_ref[i, :, :width]
            left_imag = basis_ref[i, :, width:]
            right_real = basis_ref[j, :, :width]
            right_imag = basis_ref[j, :, width:]
            packed = place(packed, slot, full_sum(left_real * right_real + left_imag * right_imag))
            if i == j:
                gram_slots.append((i, j, slot, None))
                slot += 1
            else:
                packed = place(
                    packed, slot + 1, full_sum(left_real * right_imag - left_imag * right_real)
                )
                gram_slots.append((i, j, slot, slot + 1))
                slot += 2

    spectrum_chunks = []
    for chunk in range(chunks):
        to_side(chunk, line).wait_recv()
        spectrum = side_sum(chunk, line)
        from_lines(chunk).wait_recv()
        for far in (1, 3, 2):
            spectrum = spectrum + line_in[chunk, line ^ far].astype(jnp.float32)
        spectrum_chunks.append(spectrum)
    spectrum = jnp.concatenate(spectrum_chunks, axis=0) + idle_field

    def azimuth_transform(value):
        both = jnp.dot(
            table_ref[...],
            value,
            preferred_element_type=jnp.float32,
            precision=lax.Precision.HIGHEST,
        )
        cosine = both[:n]
        sine = both[n:]
        outs = []
        for i in range(per):
            real = slice(i * width2, i * width2 + width)
            imag = slice(i * width2 + width, (i + 1) * width2)
            outs.append((cosine[:, real] - sine[:, imag]) * (1.0 / n))
            outs.append((cosine[:, imag] + sine[:, real]) * (1.0 / n))
        return jnp.concatenate(outs, axis=1)

    def exchange(phase, value, out_buffer, in_buffer, meanwhile):
        out_buffer[:, :used, :] = value.reshape(n, used, 128).astype(jnp.bfloat16)
        send_all(phase, lambda other: out_buffer.at[other], in_buffer)
        in_buffer[me] = out_buffer[me]
        meanwhile()
        wait_arrivals(phase, in_buffer)
        return in_buffer[:, :used, :].astype(jnp.float32).reshape(n, used * 128)

    solved = jnp.dot(
        spectrum.astype(jnp.bfloat16), solver[...], preferred_element_type=jnp.float32
    )
    def spread_basis():
        wait_arrivals(BASIS, basis_in)
        for j in range(arnoldi):
            spread_ref[j] = (
                basis_in[:, j * stored : j * stored + used, :]
                .astype(jnp.float32)
                .reshape(n, used * 128)
            )

    pieces = exchange(BACK, to_lanes(solved), back_out, back_in, spread_basis)
    field = azimuth_transform(pieces)
    packed = place(packed, 2 * arnoldi, full_sum(field * field))
    turned = jnp.concatenate(
        [
            part
            for i in range(per)
            for part in (
                field[:, i * width2 + width : (i + 1) * width2],
                -field[:, i * width2 : i * width2 + width],
            )
        ],
        axis=1,
    )
    for j in range(arnoldi):
        vector = spread_ref[j]
        packed = place(packed, j, full_sum(vector * field))
        packed = place(packed, arnoldi + j, full_sum(vector * turned))
    head = packed.astype(jnp.bfloat16)
    rest = packed - head.astype(jnp.float32)
    middle = rest.astype(jnp.bfloat16)
    last = (rest - middle.astype(jnp.float32)).astype(jnp.bfloat16)
    field_out[:, :used, :] = field.reshape(n, used, 128).astype(jnp.bfloat16)
    for part, value in enumerate((head, middle, last)):
        field_out[:, used + part : used + part + 1, :] = jnp.broadcast_to(
            value.reshape(1, 1, 128), (n, 1, 128)
        )
    send_all(FIELD, lambda other: field_out.at[other], field_in)
    field_in[me] = field_out[me]
    wait_arrivals(FIELD, field_in)
    result = to_rows(field_in[:, :used, :].astype(jnp.float32).reshape(n, used * 128))
    result_real = result[:, :width]
    result_imag = result[:, width:]
    parts = jnp.sum(field_in[:, used : used + 3, :].astype(jnp.float32), axis=0)
    total = parts[0:1] + parts[1:2] + parts[2:3]
    total = total * (1.0 / elements)

    def entry(index):
        return total[:, index : index + 1]

    project_real = [entry(j) for j in range(arnoldi)]
    project_imag = [entry(arnoldi + j) for j in range(arnoldi)]
    norm_square = entry(2 * arnoldi)
    for j in range(arnoldi):
        norm_square = norm_square - 2.0 * (
            project_real[j] * project_real[j] + project_imag[j] * project_imag[j]
        )
    for i, j, real_slot, imag_slot in gram_slots:
        cross_real = project_real[i] * project_real[j] + project_imag[i] * project_imag[j]
        if i == j:
            norm_square = norm_square + cross_real * entry(real_slot)
        else:
            cross_imag = project_real[i] * project_imag[j] - project_imag[i] * project_real[j]
            norm_square = norm_square + 2.0 * (
                cross_real * entry(real_slot) - cross_imag * entry(imag_slot)
            )
    scale_norm = jnp.sqrt(jnp.maximum(norm_square, 0.0) + 1e-06)
    remainder_real = result_real
    remainder_imag = result_imag
    for j in range(arnoldi):
        basis_real = basis_ref[j, :, :width]
        basis_imag = basis_ref[j, :, width:]
        remainder_real = remainder_real - (
            project_real[j] * basis_real - project_imag[j] * basis_imag
        )
        remainder_imag = remainder_imag - (
            project_real[j] * basis_imag + project_imag[j] * basis_real
        )
    out_ref[:, 0, :] = remainder_real / scale_norm
    out_ref[:, 1, :] = remainder_imag / scale_norm
    first = jnp.zeros((1, 128), jnp.float32)
    second = jnp.zeros((1, 128), jnp.float32)
    for j in range(arnoldi):
        first = place(first, j, project_real[j])
        second = place(second, j, project_imag[j])
    first = place(first, arnoldi, scale_norm)
    hess_ref[0:1] = first[:, : arnoldi + 1]
    hess_ref[1:2] = second[:, : arnoldi + 1]

    wait_sends(GATHER, columns)
    message(partial.at[0], partial.at[0], CORE, core_recv, core_peer).wait_send()
    message(side_out, side_out, SIDE, side_recv, side_peer).wait_send()
    sent = line_out.at[:, pl.ds(0, lines - 1)]
    message(sent, sent, LINE, line_recv, core_peer).wait_send()
    wait_sends(MASKS, masks)
    wait_sends(BACK, back_out)
    wait_sends(FIELD, field_out)
    wait_sends(BASIS, basis_out)


def hand_over(vector_ref, column_ref, out_ref, hess_ref):
    out_ref[0] = vector_ref[...]
    hess_ref[...] = column_ref[...]


def fused_body(coupling, band, precond, basis, mask):
    n = lax.axis_size("azim")
    arnoldi, _, cycles, _, width = basis.shape
    offsets = coupling.shape[1]
    reach = offsets // 2
    per = cycles // n
    half = n // 2
    chunks = cycles // CHUNK
    width2 = 2 * width
    vmem = pl.BlockSpec(memory_space=pltpu.VMEM)
    anywhere = pl.BlockSpec(memory_space=pl.ANY)
    lines = n // 4
    message_rows = -(-(per * width2 // 128 + 3) // 16) * 16
    message = pltpu.VMEM((n, message_rows, 128), jnp.bfloat16)
    waves = jnp.asarray(wave_constants(n, CHUNK))
    idles = jnp.asarray(idle_constants(n, cycles))
    vector, column = pl.pallas_call(
        functools.partial(step_kernel, n, cycles, reach),
        out_shape=(
            jax.ShapeDtypeStruct((cycles, 2, width), jnp.float32),
            jax.ShapeDtypeStruct((2, arnoldi + 1), jnp.float32),
        ),
        in_specs=[pl.BlockSpec(memory_space=pltpu.SMEM)] + [anywhere] * 7,
        out_specs=(vmem, vmem),
        scratch_shapes=[
            pltpu.VMEM(mask.shape, mask.dtype),
            pltpu.VMEM((arnoldi, cycles, 2, width), basis.dtype),
            pltpu.VMEM((arnoldi, cycles, width2), basis.dtype),
            pltpu.VMEM((2 * n, n), jnp.float32),
            pltpu.VMEM(waves.shape[1:], waves.dtype),
            pltpu.VMEM(idles.shape[1:], idles.dtype),
            pltpu.VMEM(coupling.shape[1:], coupling.dtype),
            pltpu.VMEM(precond.shape[1:], precond.dtype),
            pltpu.VMEM((offsets, width2, width2), jnp.bfloat16),
            pltpu.VMEM((width2, width2), jnp.bfloat16),
            pltpu.VMEM((n, width2 // 128 * cycles, 128), jnp.bfloat16),
            pltpu.VMEM((n, 1, 128), jnp.float32),
            pltpu.VMEM((2, (cycles + 2 * reach) * half, width2), jnp.bfloat16),
            pltpu.VMEM((2, (cycles + 2 * reach - 2) * half, width2), jnp.bfloat16),
            pltpu.VMEM((chunks, n * CHUNK, width2), jnp.float32),
            pltpu.VMEM((2, chunks, lines, 2, CHUNK, width2), jnp.bfloat16),
            pltpu.VMEM((chunks, lines, 2, CHUNK, width2), jnp.bfloat16),
            pltpu.VMEM((chunks, lines, CHUNK, width2), jnp.bfloat16),
            pltpu.VMEM((chunks, lines, CHUNK, width2), jnp.bfloat16),
            pltpu.VMEM((chunks, lines, CHUNK, width2), jnp.bfloat16),
            pltpu.VMEM((chunks, lines, CHUNK, width2), jnp.bfloat16),
            message,
            message,
            message,
            message,
            pltpu.VMEM((n, arnoldi * message_rows, 128), jnp.bfloat16),
            pltpu.VMEM((n, arnoldi * message_rows, 128), jnp.bfloat16),
            pltpu.VMEM((arnoldi, n, per * width2), jnp.float32),
            pltpu.SemaphoreType.DMA((8,)),
            pltpu.SemaphoreType.DMA((8,)),
            pltpu.SemaphoreType.DMA((GATHER + n + chunks * (lines + 2),)),
        ],
        compiler_params=pltpu.CompilerParams(
            collective_id=0, has_side_effects=True, vmem_limit_bytes=60 * 1024 * 1024
        ),
    )(
        band,
        mask,
        basis[:, 0],
        jnp.asarray(fourier_constants(n)),
        waves,
        idles,
        coupling[0],
        precond[0],
    )
    return pl.pallas_call(
        hand_over,
        out_shape=(
            jax.ShapeDtypeStruct((1,) + vector.shape, vector.dtype),
            jax.ShapeDtypeStruct(column.shape, column.dtype),
        ),
        in_specs=[vmem, vmem],
        out_specs=(vmem, vmem),
    )(vector, column)


def body(coupling, band, precond, basis, mask):
    n = lax.axis_size("azim")
    cycles = basis.shape[2]
    width = basis.shape[4]
    if n == 16 and cycles == 32 and width % 128 == 0:
        return fused_body(coupling, band, precond, basis, mask)
    return plain_body(coupling, band, precond, basis, mask)


def solution(mesh):
    return jax.shard_map(
        body,
        mesh=mesh,
        in_specs=(
            P("azim", "freq", None, None, None),
            P("freq"),
            P("azim", "freq", None, None),
            P("freq", "azim", None, None, None),
            P("azim", None),
        ),
        out_specs=(P("azim", "freq", None, None), P("freq", None)),
        check_vma=False,
    )
```

```python
import functools

import jax
import jax.numpy as jnp
import numpy as np
from jax import lax
from jax.experimental import pallas as pl
from jax.experimental.pallas import tpu as pltpu
from jax.sharding import PartitionSpec as P


def fourier_tables(azimuths):
    azimuth_steps = jnp.arange(azimuths, dtype=jnp.int32)
    phase_index = azimuth_steps[:, None] * azimuth_steps[None, :] % azimuths
    angles = phase_index.astype(jnp.float32) * (2.0 * jnp.pi / azimuths)
    return (jnp.cos(angles), jnp.sin(angles))


def transform(real_part, imag_part, cosine_table, sine_table, inverse):
    highest_accuracy = lax.Precision.HIGHEST
    cos_real = jnp.tensordot(cosine_table, real_part, axes=1, precision=highest_accuracy)
    cos_imag = jnp.tensordot(cosine_table, imag_part, axes=1, precision=highest_accuracy)
    sin_real = jnp.tensordot(sine_table, real_part, axes=1, precision=highest_accuracy)
    sin_imag = jnp.tensordot(sine_table, imag_part, axes=1, precision=highest_accuracy)
    if inverse:
        scaling = 1.0 / cosine_table.shape[0]
        return ((cos_real - sin_imag) * scaling, (cos_imag + sin_real) * scaling)
    return (cos_real + sin_imag, cos_imag - sin_real)


def block_matrix(matrix):
    real_part = matrix[..., 0, :, :]
    imag_part = matrix[..., 1, :, :]
    upper = jnp.concatenate([real_part, imag_part], axis=-1)
    lower = jnp.concatenate([-imag_part, real_part], axis=-1)
    return jnp.concatenate([upper, lower], axis=-2)


def cycle_coupling(column_rows, blocks):
    row_total, cycle_count, parts, basis_width = column_rows.shape
    cycle_reach = blocks.shape[0] // 2
    flattened = column_rows.reshape(row_total, cycle_count, parts * basis_width)
    padded = jnp.pad(flattened, ((0, 0), (cycle_reach, cycle_reach), (0, 0)))
    summed = jnp.zeros((row_total * cycle_count, parts * basis_width), jnp.float32)
    for offset in range(blocks.shape[0]):
        shifted = padded[:, 2 * cycle_reach - offset : 2 * cycle_reach - offset + cycle_count]
        summed = summed + jnp.dot(
            shifted.reshape(row_total * cycle_count, parts * basis_width),
            blocks[offset],
            preferred_element_type=jnp.float32,
            precision=None,
        )
    return summed.reshape(row_total, cycle_count, parts, basis_width)


def relayout(field, cosine_table, sine_table, send_out, send_back, inverse):
    azimuths = cosine_table.shape[0]
    cycle_count = field.shape[1]
    basis_width = field.shape[3]
    piece_width = cycle_count * basis_width // azimuths
    split_parts = jnp.transpose(field[0], (1, 0, 2)).reshape(2, azimuths, piece_width)
    pieces = jnp.transpose(split_parts, (1, 0, 2)).reshape(azimuths, 2 * piece_width)
    spread = send_out(pieces).reshape(azimuths, 2, piece_width)
    real_part, imag_part = transform(spread[:, 0], spread[:, 1], cosine_table, sine_table, inverse)
    joined = jnp.stack([real_part, imag_part], axis=1).reshape(azimuths, 2 * piece_width)
    returned = send_back(joined).reshape(azimuths, 2, piece_width)
    whole = jnp.transpose(returned, (1, 0, 2)).reshape(2, cycle_count, basis_width)
    return jnp.transpose(whole, (1, 0, 2))[None]


def plain_body(coupling, band, precond, basis, mask):
    highest_accuracy = lax.Precision.HIGHEST
    azimuths = lax.axis_size("azim")
    position = lax.axis_index("azim")
    cosine_table, sine_table = fourier_tables(azimuths)
    vectors = basis[:, 0]
    arnoldi_count = vectors.shape[0]
    cycle_count = vectors.shape[1]
    basis_width = vectors.shape[3]
    current = vectors[arnoldi_count - 1][None]
    active = mask.astype(jnp.float32)[:, :, None, None]
    driving = (active * current).astype(jnp.bfloat16)
    distance = jnp.minimum(position, azimuths - position)
    inside = (distance <= band).astype(coupling.dtype)
    kernel = coupling[0] * inside[:, None, None, None]
    blocks = block_matrix(kernel)
    gathered = lax.all_gather(driving, "azim", axis=0, tiled=True)
    aligned = jnp.roll(gathered, position, axis=0)
    applied = lax.psum_scatter(
        cycle_coupling(aligned, blocks), "azim", scatter_dimension=0, tiled=True
    )
    driven = active * applied + (1.0 - active) * current
    spectrum = relayout(
        driven,
        cosine_table,
        sine_table,
        lambda tensor: lax.all_to_all(
            tensor.astype(jnp.bfloat16), "azim", split_axis=0, concat_axis=0, tiled=True
        ).astype(tensor.dtype),
        lambda tensor: lax.all_to_all(
            tensor.astype(jnp.bfloat16), "azim", split_axis=0, concat_axis=0, tiled=True
        ).astype(tensor.dtype),
        False,
    )
    precond_blocks = block_matrix(precond[0])
    solved = jnp.dot(
        spectrum.reshape(cycle_count, 2 * basis_width),
        precond_blocks,
        preferred_element_type=jnp.float32,
        precision=highest_accuracy,
    )
    solved = solved.reshape(1, cycle_count, 2, basis_width)
    result = relayout(
        solved,
        cosine_table,
        sine_table,
        lambda tensor: lax.all_to_all(
            tensor.astype(jnp.bfloat16), "azim", split_axis=0, concat_axis=0, tiled=True
        ).astype(tensor.dtype),
        lambda tensor: lax.all_to_all(
            tensor.astype(jnp.bfloat16), "azim", split_axis=0, concat_axis=0, tiled=True
        ).astype(tensor.dtype),
        True,
    )
    elements = float(azimuths * cycle_count * basis_width)
    basis_real = vectors[:, :, 0]
    basis_imag = vectors[:, :, 1]
    result_real = result[0, :, 0]
    result_imag = result[0, :, 1]
    local_real = jnp.sum(
        basis_real * result_real[None] + basis_imag * result_imag[None], axis=(1, 2)
    )
    local_imag = jnp.sum(
        basis_real * result_imag[None] - basis_imag * result_real[None], axis=(1, 2)
    )
    sum_real, sum_imag = lax.psum((local_real, local_imag), "azim")
    project_real = sum_real / elements
    project_imag = sum_imag / elements
    coef_real = project_real[:, None, None]
    coef_imag = project_imag[:, None, None]
    remainder_real = result_real - jnp.sum(coef_real * basis_real - coef_imag * basis_imag, axis=0)
    remainder_imag = result_imag - jnp.sum(coef_real * basis_imag + coef_imag * basis_real, axis=0)
    norm_square = (
        lax.psum(jnp.sum(remainder_real * remainder_real + remainder_imag * remainder_imag), "azim")
        / elements
    )
    scale_norm = jnp.sqrt(norm_square + 1e-06)
    new_vector = (jnp.stack([remainder_real, remainder_imag], axis=1) / scale_norm)[None]
    hessenberg_column = jnp.stack(
        [
            jnp.concatenate([project_real, scale_norm[None]]),
            jnp.concatenate([project_imag, jnp.zeros((1,), jnp.float32)]),
        ]
    )
    return (new_vector, hessenberg_column)


def fourier_constants(azimuths):
    steps = np.arange(azimuths)
    angles = (steps[:, None] * steps[None, :] % azimuths) * (2.0 * np.pi / azimuths)
    table = np.concatenate([np.cos(angles), np.sin(angles)], axis=0)
    return (table / TABLE_SCALE).astype(np.float32)


TABLE_SCALE = 1.1328025


def wave_constants(azimuths, chunk):
    half = azimuths // 2
    start = np.arange(azimuths)[:, None, None, None, None, None]
    mode = np.arange(azimuths)[None, :, None, None, None, None]
    out_cycle = np.arange(chunk)[None, None, :, None, None, None]
    part = np.arange(2)[None, None, None, :, None, None]
    in_cycle = np.arange(chunk)[None, None, None, None, :, None]
    step = np.arange(half)[None, None, None, None, None, :]
    angle = (mode * (start + step) % azimuths) * (2.0 * np.pi / azimuths)
    value = np.where(part == 0, np.cos(angle), np.sin(angle)) * (out_cycle == in_cycle)
    value = value * TABLE_SCALE
    return value.reshape(azimuths, azimuths * chunk, 2 * chunk * half).astype(jnp.bfloat16)


def idle_constants(azimuths, cycles):
    half = azimuths // 2
    mode = np.arange(azimuths)[:, None, None, None, None, None]
    part = np.arange(2)[None, :, None, None, None, None]
    out_cycle = np.arange(cycles)[None, None, :, None, None, None]
    group = np.arange(2)[None, None, None, :, None, None]
    step = np.arange(half)[None, None, None, None, :, None]
    in_cycle = np.arange(cycles)[None, None, None, None, None, :]
    column = ((mode // half) ^ group) * half + step
    angle = (mode * column % azimuths) * (2.0 * np.pi / azimuths)
    value = np.where(part == 0, np.cos(angle), np.sin(angle)) * (out_cycle == in_cycle)
    value = value * TABLE_SCALE
    return value.reshape(azimuths, 2 * cycles, azimuths * cycles).astype(jnp.bfloat16)


CHUNK = 16
MASKS, BACK, FIELD, BASIS, GATHER, CORE, SIDE, LINE = range(8)


def step_kernel(
    n,
    cycles,
    reach,
    band_ref,
    mask_any,
    basis_any,
    table_any,
    wave_any,
    idle_any,
    coupling_ref,
    precond_ref,
    out_ref,
    hess_ref,
    mask_ref,
    raw_basis,
    basis_ref,
    table_ref,
    wave_ref,
    idle_ref,
    raw_coupling,
    raw_precond,
    blocks,
    solver,
    columns,
    masks,
    even_drive,
    odd_drive,
    early,
    partial,
    core_in,
    side_out,
    side_in,
    line_out,
    line_in,
    back_out,
    back_in,
    field_out,
    field_in,
    basis_out,
    basis_in,
    spread_ref,
    load_sem,
    send_sem,
    recv_sem,
):
    arnoldi = basis_ref.shape[0]
    width2 = basis_ref.shape[2]
    width = width2 // 2
    lane_tiles = width2 // 128
    offsets = 2 * reach + 1
    per = cycles // n
    half = n // 2
    chunks = cycles // CHUNK
    elements = float(n * cycles * width)
    me = lax.axis_index("azim")
    core = me & 1
    side = (me >> 1) & 1
    line = me >> 2
    lines = n // 4
    core_peer = me ^ 1
    side_peer = me ^ 2
    own_half = me >> 3

    def peer(step):
        return me ^ (n - step)

    barrier = pltpu.get_barrier_semaphore()
    for step in range(1, n):
        pl.semaphore_signal(
            barrier, inc=1, device_id={"azim": peer(step)}, device_id_type=pl.DeviceIdType.MESH
        )

    load_mask = pltpu.make_async_copy(mask_any, mask_ref, load_sem.at[0])
    load_last = pltpu.make_async_copy(
        basis_any.at[pl.ds(arnoldi - 1, 1)], raw_basis.at[pl.ds(arnoldi - 1, 1)], load_sem.at[1]
    )
    load_basis = pltpu.make_async_copy(
        basis_any.at[pl.ds(0, arnoldi - 1)], raw_basis.at[pl.ds(0, arnoldi - 1)], load_sem.at[2]
    )
    load_coupling = pltpu.make_async_copy(coupling_ref, raw_coupling, load_sem.at[3])
    load_table = pltpu.make_async_copy(table_any, table_ref, load_sem.at[4])
    start = (own_half * half + me) & (n - 1)
    load_wave = pltpu.make_async_copy(wave_any.at[start], wave_ref, load_sem.at[5])
    load_idle = pltpu.make_async_copy(idle_any.at[me], idle_ref, load_sem.at[6])
    load_precond = pltpu.make_async_copy(precond_ref, raw_precond, load_sem.at[7])
    for load in (
        load_mask,
        load_last,
        load_coupling,
        load_basis,
        load_table,
        load_wave,
        load_idle,
        load_precond,
    ):
        load.start()

    def message(source, target, send, recv, other):
        return pltpu.make_async_remote_copy(
            src_ref=source,
            dst_ref=target,
            send_sem=send_sem.at[send],
            recv_sem=recv_sem.at[recv],
            device_id={"azim": other},
            device_id_type=pl.DeviceIdType.MESH,
        )

    def send_all(phase, sources, targets):
        for step in range(1, n):
            other = peer(step)
            message(sources(other), targets.at[me], phase, phase, other).start()

    def all_of(phase, buffers):
        return message(
            buffers.at[pl.ds(0, n - 1)], buffers.at[pl.ds(0, n - 1)], phase, phase, core_peer
        )

    def wait_arrivals(phase, targets):
        all_of(phase, targets).wait_recv()

    def wait_sends(phase, sources):
        all_of(phase, sources).wait_send()

    def to_lanes(value):
        return jnp.concatenate([value[i * n : (i + 1) * n] for i in range(per)], axis=1)

    def to_rows(value):
        return jnp.concatenate(
            [value[:, i * width2 : (i + 1) * width2] for i in range(per)], axis=0
        )

    def order_basis(j):
        for part in range(2):
            basis_ref[j, :, part * width : (part + 1) * width] = raw_basis[j, :, part, :]

    load_mask.wait()
    masks[me] = jnp.zeros((1, 128), jnp.float32)
    masks[me, :, :cycles] = mask_ref[...].astype(jnp.float32)
    load_last.wait()
    order_basis(arnoldi - 1)
    current = basis_ref[arnoldi - 1].astype(jnp.bfloat16)
    for tile in range(lane_tiles):
        columns[me, tile * cycles : (tile + 1) * cycles, :] = current[
            :, tile * 128 : (tile + 1) * 128
        ]

    pl.semaphore_wait(barrier, n - 1)

    def pass_on(slot, other):
        message(columns.at[slot], columns.at[slot], GATHER, GATHER + slot, other).start()

    def arrived(slot):
        message(
            columns.at[slot], columns.at[slot], GATHER, GATHER + slot, core_peer
        ).wait_recv()

    def slot_of(far, plane):
        return (line ^ far) * 4 + plane

    plane = me & 3
    for far in (1, 3, 2):
        pass_on(me, slot_of(far, plane))
    pass_on(me, side_peer)
    pass_on(me, core_peer)
    send_all(MASKS, lambda other: masks.at[me], masks)

    rows = half * cycles
    padded = (cycles + 2 * reach) * half
    pick_row = lax.broadcasted_iota(jnp.int32, (padded, rows), 0)
    pick_lane = lax.broadcasted_iota(jnp.int32, (padded, rows), 1)
    pick_match = ((pick_row & (half - 1)) * cycles + (pick_row // half) - reach == pick_lane) & (
        (pick_row // half >= reach) & (pick_row // half < cycles + reach)
    )
    pick = jnp.where(pick_match, 1.0, 0.0).astype(jnp.bfloat16)

    load_basis.wait()
    for j in range(arnoldi - 1):
        order_basis(j)
    used = per * width2 // 128
    stored = basis_out.shape[1] // arnoldi
    for j in range(arnoldi):
        basis_out[:, j * stored : j * stored + used, :] = (
            to_lanes(basis_ref[j]).reshape(n, used, 128).astype(jnp.bfloat16)
        )

    distance = jnp.minimum(me, n - me)

    def build(offset):
        inside = jnp.where(distance <= band_ref[offset], 1.0, 0.0).astype(jnp.float32)
        keep = jnp.full((width, width), inside, jnp.float32).astype(jnp.bfloat16)
        real_part = raw_coupling[offset, 0] * keep
        imag_part = raw_coupling[offset, 1] * keep
        blocks[offset, :width, :width] = real_part
        blocks[offset, :width, width:] = imag_part
        blocks[offset, width:, :width] = -imag_part
        blocks[offset, width:, width:] = real_part

    load_coupling.wait()
    build(0)
    arrived(side_peer)
    pass_on(side_peer, core_peer)
    build(1)
    arrived(slot_of(1, plane))
    pass_on(slot_of(1, plane), side_peer)
    pass_on(slot_of(1, plane), core_peer)
    build(2)
    for far in (3, 2):
        arrived(slot_of(far, plane))
        pass_on(slot_of(far, plane), side_peer)
        pass_on(slot_of(far, plane), core_peer)
        build(6 - far)
    arrived(slot_of(1, plane ^ 2))
    pass_on(slot_of(1, plane ^ 2), core_peer)
    def send_basis(steps):
        for step in steps:
            other = me ^ step
            message(basis_out.at[other], basis_in.at[me], BASIS, BASIS, other).start()

    send_basis((12, 13, 8, 9, 4, 5, 1))

    wait_arrivals(MASKS, masks)
    every_mask = masks[...].reshape(n, 128)
    turn_row = lax.broadcasted_iota(jnp.int32, (n, n), 0)
    turn_lane = lax.broadcasted_iota(jnp.int32, (n, n), 1)
    turn = jnp.where(((start + turn_row) & (n - 1)) == turn_lane, 1.0, 0.0).astype(jnp.bfloat16)
    turned_mask = jnp.dot(
        turn, every_mask.astype(jnp.bfloat16), preferred_element_type=jnp.float32
    )
    mask_lane = lax.broadcasted_iota(jnp.int32, (rows, 128), 1)
    mask_row = lax.broadcasted_iota(jnp.int32, (rows, 128), 0)
    load_wave.wait()
    load_idle.wait()

    def group_start(group):
        base = pl.multiple_of((own_half ^ group) * half, half)
        tiles = [
            columns[pl.ds(base, half), tile * cycles : (tile + 1) * cycles, :].reshape(rows, 128)
            for tile in range(lane_tiles)
        ]
        gathered = jnp.concatenate(tiles, axis=1)
        group_mask = masks[pl.ds(base, half)]
        spread = jnp.broadcast_to(group_mask, (half, cycles, 128)).reshape(rows, 128)
        active = jnp.sum(
            jnp.where(mask_lane == (mask_row & (cycles - 1)), spread, 0.0), axis=1, keepdims=True
        )
        driving = (gathered.astype(jnp.float32) * active).astype(jnp.bfloat16)
        picked = jnp.dot(pick, driving, preferred_element_type=jnp.float32)
        even_drive[group] = picked.astype(jnp.bfloat16)
        odd_drive[group] = picked[half : padded - half].astype(jnp.bfloat16)
        return (gathered - driving).astype(jnp.bfloat16)

    def group_source(group, offset):
        first = (2 * reach - offset) * half
        if offset % 2 == 0:
            return even_drive[group, first : first + rows]
        return odd_drive[group, first - half : first - half + rows]

    def group_product(group):
        source = jnp.concatenate(
            [group_source(group, offset) for offset in range(offsets)], axis=1
        )
        return jnp.concatenate(
            [
                jnp.dot(
                    source[at : at + 128],
                    blocks[...].reshape(offsets * width2, width2),
                    preferred_element_type=jnp.float32,
                )
                for at in range(0, rows, 128)
            ],
            axis=0,
        )

    def group_finish(group, applied):
        spread = jnp.broadcast_to(
            turned_mask[group * half : (group + 1) * half].reshape(1, half, 128),
            (cycles, half, 128),
        ).reshape(rows, 128)
        active = jnp.sum(
            jnp.where(mask_lane == (mask_row // half), spread, 0.0), axis=1, keepdims=True
        )
        return (applied * active).astype(jnp.bfloat16)

    def wave(masked, chunk):
        block = masked[chunk * CHUNK * half : (chunk + 1) * CHUNK * half]
        swapped = jnp.concatenate([block[:, width:], -block[:, :width]], axis=1)
        return jnp.dot(
            wave_ref[...],
            jnp.concatenate([block, swapped], axis=0),
            preferred_element_type=jnp.float32,
        )

    for far in (0, 1):
        arrived(slot_of(far, plane ^ 1))
        arrived(slot_of(far, plane ^ 3))
    idle_rows = group_start(0)
    applied = group_product(0)
    for far in (3, 2):
        arrived(slot_of(far, plane ^ 2))
        pass_on(slot_of(far, plane ^ 2), core_peer)
    masked = group_finish(0, applied)
    for chunk in range(chunks):
        early[chunk] = wave(masked, chunk)
    idle_modes = jnp.dot(
        idle_ref[:, :rows], idle_rows, preferred_element_type=jnp.float32
    )

    for far in (3, 2):
        arrived(slot_of(far, plane ^ 1))
        arrived(slot_of(far, plane ^ 3))
    send_basis((14, 15, 10, 11, 6, 7, 2, 3))
    basis_in[me] = basis_out[me]
    idle_rows = group_start(1)
    applied = group_product(1)
    masked = group_finish(1, applied)

    core_recv = GATHER + n
    side_recv = core_recv + chunks
    line_recv = side_recv + chunks * lines

    def to_core(chunk):
        return message(
            partial.at[1 - core, chunk], core_in.at[chunk], CORE, core_recv + chunk, core_peer
        )

    def to_side(chunk, target):
        return message(
            side_out.at[chunk, target],
            side_in.at[chunk, target],
            SIDE,
            side_recv + chunk * lines + target,
            side_peer,
        )

    def to_line(chunk, target):
        return message(
            line_out.at[chunk, target],
            line_in.at[chunk, line],
            LINE,
            line_recv + chunk,
            target * 4 + plane,
        )

    def from_lines(chunk):
        inner = line_in.at[chunk, pl.ds(0, lines - 1)]
        return message(inner, inner, LINE, line_recv + chunk, core_peer)

    mode_of_row = lax.broadcasted_iota(jnp.int32, (n * CHUNK, 1), 0) // CHUNK
    sign = jnp.where((mode_of_row & 1) == 0, 1.0, -1.0)
    for chunk in range(chunks):
        modes = (early[chunk] + sign * wave(masked, chunk)).astype(jnp.bfloat16)
        for mode in range(n):
            partial[mode & 1, chunk, mode >> 2, (mode >> 1) & 1] = modes[
                mode * CHUNK : (mode + 1) * CHUNK
            ]
        to_core(chunk).start()

    def core_sum(chunk, target, half_side):
        return partial[core, chunk, target, half_side].astype(jnp.float32) + core_in[
            chunk, target, half_side
        ].astype(jnp.float32)

    def fold_core(chunk, target):
        side_out[chunk, target] = core_sum(chunk, target, 1 - side).astype(jnp.bfloat16)
        to_side(chunk, target).start()

    def side_sum(chunk, target):
        return core_sum(chunk, target, side) + side_in[chunk, target].astype(jnp.float32)

    for chunk in range(chunks):
        to_core(chunk).wait_recv()
        for far in (3, 2):
            fold_core(chunk, line ^ far)
    for far in (1, 0):
        for chunk in range(chunks):
            fold_core(chunk, line ^ far)

    idle_modes = idle_modes + jnp.dot(
        idle_ref[:, rows:], idle_rows, preferred_element_type=jnp.float32
    )
    idle_cos = idle_modes[:cycles]
    idle_sin = idle_modes[cycles:]
    idle_field = jnp.concatenate(
        [
            idle_cos[:, :width] + idle_sin[:, width:],
            idle_cos[:, width:] - idle_sin[:, :width],
        ],
        axis=1,
    )
    load_precond.wait()
    load_table.wait()
    real_part = raw_precond[0].astype(jnp.bfloat16)
    imag_part = raw_precond[1].astype(jnp.bfloat16)
    solver[:width, :width] = real_part
    solver[:width, width:] = imag_part
    solver[width:, :width] = -imag_part
    solver[width:, width:] = real_part

    for chunk, far in [(c, f) for fars in ((3, 2), (1,)) for c in range(chunks) for f in fars]:
        target = line ^ far
        to_side(chunk, target).wait_recv()
        line_out[chunk, target] = side_sum(chunk, target).astype(jnp.bfloat16)
        to_line(chunk, target).start()

    small_lane = lax.broadcasted_iota(jnp.int32, (1, 128), 1)

    def place(total, index, value):
        return total + jnp.where(small_lane == index, value, 0.0)

    def full_sum(value):
        return jnp.sum(jnp.sum(value, axis=0, keepdims=True), axis=1, keepdims=True)

    packed = jnp.zeros((1, 128), jnp.float32)
    gram_slots = []
    slot = 2 * arnoldi + 1
    for i in range(arnoldi):
        for j in range(i, arnoldi):
            left_real = basis_ref[i, :, :width]
            left_imag = basis_ref[i, :, width:]
            right_real = basis_ref[j, :, :width]
            right_imag = basis_ref[j, :, width:]
            packed = place(packed, slot, full_sum(left_real * right_real + left_imag * right_imag))
            if i == j:
                gram_slots.append((i, j, slot, None))
                slot += 1
            else:
                packed = place(
                    packed, slot + 1, full_sum(left_real * right_imag - left_imag * right_real)
                )
                gram_slots.append((i, j, slot, slot + 1))
                slot += 2

    spectrum_chunks = []
    for chunk in range(chunks):
        to_side(chunk, line).wait_recv()
        spectrum = side_sum(chunk, line)
        from_lines(chunk).wait_recv()
        for far in (1, 3, 2):
            spectrum = spectrum + line_in[chunk, line ^ far].astype(jnp.float32)
        spectrum_chunks.append(spectrum)
    spectrum = jnp.concatenate(spectrum_chunks, axis=0) + idle_field

    def azimuth_transform(value):
        both = jnp.dot(
            table_ref[...],
            value,
            preferred_element_type=jnp.float32,
            precision=lax.Precision.HIGHEST,
        )
        cosine = both[:n]
        sine = both[n:]
        outs = []
        for i in range(per):
            real = slice(i * width2, i * width2 + width)
            imag = slice(i * width2 + width, (i + 1) * width2)
            outs.append((cosine[:, real] - sine[:, imag]) * (1.0 / n))
            outs.append((cosine[:, imag] + sine[:, real]) * (1.0 / n))
        return jnp.concatenate(outs, axis=1)

    def exchange(phase, value, out_buffer, in_buffer, meanwhile):
        out_buffer[:, :used, :] = value.reshape(n, used, 128).astype(jnp.bfloat16)
        send_all(phase, lambda other: out_buffer.at[other], in_buffer)
        in_buffer[me] = out_buffer[me]
        meanwhile()
        wait_arrivals(phase, in_buffer)
        return in_buffer[:, :used, :].astype(jnp.float32).reshape(n, used * 128)

    solved = jnp.dot(
        spectrum.astype(jnp.bfloat16), solver[...], preferred_element_type=jnp.float32
    )
    def spread_basis():
        wait_arrivals(BASIS, basis_in)
        for j in range(arnoldi):
            spread_ref[j] = (
                basis_in[:, j * stored : j * stored + used, :]
                .astype(jnp.float32)
                .reshape(n, used * 128)
            )

    pieces = exchange(BACK, to_lanes(solved), back_out, back_in, spread_basis)
    field = azimuth_transform(pieces)
    packed = place(packed, 2 * arnoldi, full_sum(field * field))
    turned = jnp.concatenate(
        [
            part
            for i in range(per)
            for part in (
                field[:, i * width2 + width : (i + 1) * width2],
                -field[:, i * width2 : i * width2 + width],
            )
        ],
        axis=1,
    )
    for j in range(arnoldi):
        vector = spread_ref[j]
        packed = place(packed, j, full_sum(vector * field))
        packed = place(packed, arnoldi + j, full_sum(vector * turned))
    head = packed.astype(jnp.bfloat16)
    rest = packed - head.astype(jnp.float32)
    middle = rest.astype(jnp.bfloat16)
    last = (rest - middle.astype(jnp.float32)).astype(jnp.bfloat16)
    field_out[:, :used, :] = field.reshape(n, used, 128).astype(jnp.bfloat16)
    for part, value in enumerate((head, middle, last)):
        field_out[:, used + part : used + part + 1, :] = jnp.broadcast_to(
            value.reshape(1, 1, 128), (n, 1, 128)
        )
    send_all(FIELD, lambda other: field_out.at[other], field_in)
    field_in[me] = field_out[me]
    wait_arrivals(FIELD, field_in)
    result = to_rows(field_in[:, :used, :].astype(jnp.float32).reshape(n, used * 128))
    result_real = result[:, :width]
    result_imag = result[:, width:]
    parts = jnp.sum(field_in[:, used : used + 3, :].astype(jnp.float32), axis=0)
    total = parts[0:1] + parts[1:2] + parts[2:3]
    total = total * (1.0 / elements)

    def entry(index):
        return total[:, index : index + 1]

    project_real = [entry(j) for j in range(arnoldi)]
    project_imag = [entry(arnoldi + j) for j in range(arnoldi)]
    norm_square = entry(2 * arnoldi)
    for j in range(arnoldi):
        norm_square = norm_square - 2.0 * (
            project_real[j] * project_real[j] + project_imag[j] * project_imag[j]
        )
    for i, j, real_slot, imag_slot in gram_slots:
        cross_real = project_real[i] * project_real[j] + project_imag[i] * project_imag[j]
        if i == j:
            norm_square = norm_square + cross_real * entry(real_slot)
        else:
            cross_imag = project_real[i] * project_imag[j] - project_imag[i] * project_real[j]
            norm_square = norm_square + 2.0 * (
                cross_real * entry(real_slot) - cross_imag * entry(imag_slot)
            )
    scale_norm = jnp.sqrt(jnp.maximum(norm_square, 0.0) + 1e-06)
    remainder_real = result_real
    remainder_imag = result_imag
    for j in range(arnoldi):
        basis_real = basis_ref[j, :, :width]
        basis_imag = basis_ref[j, :, width:]
        remainder_real = remainder_real - (
            project_real[j] * basis_real - project_imag[j] * basis_imag
        )
        remainder_imag = remainder_imag - (
            project_real[j] * basis_imag + project_imag[j] * basis_real
        )
    out_ref[:, 0, :] = remainder_real / scale_norm
    out_ref[:, 1, :] = remainder_imag / scale_norm
    first = jnp.zeros((1, 128), jnp.float32)
    second = jnp.zeros((1, 128), jnp.float32)
    for j in range(arnoldi):
        first = place(first, j, project_real[j])
        second = place(second, j, project_imag[j])
    first = place(first, arnoldi, scale_norm)
    hess_ref[0:1] = first[:, : arnoldi + 1]
    hess_ref[1:2] = second[:, : arnoldi + 1]

    wait_sends(GATHER, columns)
    message(partial.at[0], partial.at[0], CORE, core_recv, core_peer).wait_send()
    message(side_out, side_out, SIDE, side_recv, side_peer).wait_send()
    sent = line_out.at[:, pl.ds(0, lines - 1)]
    message(sent, sent, LINE, line_recv, core_peer).wait_send()
    wait_sends(MASKS, masks)
    wait_sends(BACK, back_out)
    wait_sends(FIELD, field_out)
    wait_sends(BASIS, basis_out)


def hand_over(vector_ref, column_ref, out_ref, hess_ref):
    out_ref[0] = vector_ref[...]
    hess_ref[...] = column_ref[...]


def fused_body(coupling, band, precond, basis, mask):
    n = lax.axis_size("azim")
    arnoldi, _, cycles, _, width = basis.shape
    offsets = coupling.shape[1]
    reach = offsets // 2
    per = cycles // n
    half = n // 2
    chunks = cycles // CHUNK
    width2 = 2 * width
    vmem = pl.BlockSpec(memory_space=pltpu.VMEM)
    anywhere = pl.BlockSpec(memory_space=pl.ANY)
    lines = n // 4
    message_rows = -(-(per * width2 // 128 + 3) // 16) * 16
    message = pltpu.VMEM((n, message_rows, 128), jnp.bfloat16)
    waves = jnp.asarray(wave_constants(n, CHUNK))
    idles = jnp.asarray(idle_constants(n, cycles))
    vector, column = pl.pallas_call(
        functools.partial(step_kernel, n, cycles, reach),
        out_shape=(
            jax.ShapeDtypeStruct((cycles, 2, width), jnp.float32),
            jax.ShapeDtypeStruct((2, arnoldi + 1), jnp.float32),
        ),
        in_specs=[pl.BlockSpec(memory_space=pltpu.SMEM)] + [anywhere] * 7,
        out_specs=(vmem, vmem),
        scratch_shapes=[
            pltpu.VMEM(mask.shape, mask.dtype),
            pltpu.VMEM((arnoldi, cycles, 2, width), basis.dtype),
            pltpu.VMEM((arnoldi, cycles, width2), basis.dtype),
            pltpu.VMEM((2 * n, n), jnp.float32),
            pltpu.VMEM(waves.shape[1:], waves.dtype),
            pltpu.VMEM(idles.shape[1:], idles.dtype),
            pltpu.VMEM(coupling.shape[1:], coupling.dtype),
            pltpu.VMEM(precond.shape[1:], precond.dtype),
            pltpu.VMEM((offsets, width2, width2), jnp.bfloat16),
            pltpu.VMEM((width2, width2), jnp.bfloat16),
            pltpu.VMEM((n, width2 // 128 * cycles, 128), jnp.bfloat16),
            pltpu.VMEM((n, 1, 128), jnp.float32),
            pltpu.VMEM((2, (cycles + 2 * reach) * half, width2), jnp.bfloat16),
            pltpu.VMEM((2, (cycles + 2 * reach - 2) * half, width2), jnp.bfloat16),
            pltpu.VMEM((chunks, n * CHUNK, width2), jnp.float32),
            pltpu.VMEM((2, chunks, lines, 2, CHUNK, width2), jnp.bfloat16),
            pltpu.VMEM((chunks, lines, 2, CHUNK, width2), jnp.bfloat16),
            pltpu.VMEM((chunks, lines, CHUNK, width2), jnp.bfloat16),
            pltpu.VMEM((chunks, lines, CHUNK, width2), jnp.bfloat16),
            pltpu.VMEM((chunks, lines, CHUNK, width2), jnp.bfloat16),
            pltpu.VMEM((chunks, lines, CHUNK, width2), jnp.bfloat16),
            message,
            message,
            message,
            message,
            pltpu.VMEM((n, arnoldi * message_rows, 128), jnp.bfloat16),
            pltpu.VMEM((n, arnoldi * message_rows, 128), jnp.bfloat16),
            pltpu.VMEM((arnoldi, n, per * width2), jnp.float32),
            pltpu.SemaphoreType.DMA((8,)),
            pltpu.SemaphoreType.DMA((8,)),
            pltpu.SemaphoreType.DMA((GATHER + n + chunks * (lines + 2),)),
        ],
        compiler_params=pltpu.CompilerParams(
            collective_id=0, has_side_effects=True, vmem_limit_bytes=60 * 1024 * 1024
        ),
    )(
        band,
        mask,
        basis[:, 0],
        jnp.asarray(fourier_constants(n)),
        waves,
        idles,
        coupling[0],
        precond[0],
    )
    return pl.pallas_call(
        hand_over,
        out_shape=(
            jax.ShapeDtypeStruct((1,) + vector.shape, vector.dtype),
            jax.ShapeDtypeStruct(column.shape, column.dtype),
        ),
        in_specs=[vmem, vmem],
        out_specs=(vmem, vmem),
    )(vector, column)


def body(coupling, band, precond, basis, mask):
    n = lax.axis_size("azim")
    cycles = basis.shape[2]
    width = basis.shape[4]
    if n == 16 and cycles == 32 and width % 128 == 0:
        return fused_body(coupling, band, precond, basis, mask)
    return plain_body(coupling, band, precond, basis, mask)


def solution(mesh):
    return jax.shard_map(
        body,
        mesh=mesh,
        in_specs=(
            P("azim", "freq", None, None, None),
            P("freq"),
            P("azim", "freq", None, None),
            P("freq", "azim", None, None, None),
            P("azim", None),
        ),
        out_specs=(P("azim", "freq", None, None), P("freq", None)),
        check_vma=False,
    )
```
